128 devices in a mesh: sec: 4 (over y_lo, core), xy: 32 (over y_hi, z, x).
Axes of the slice: x: 4, y: 4 (y_hi: 2, y_lo: 2; y = y_hi * 2 + y_lo), z: 4, core: 2. Of those that a mesh axis runs over, the one named last changes fastest.
Arguments:
- raw_pieces: bfloat16 [16, 3072, 4096], P('sec', 'xy'), may hold values from -6 to 6
- piece_owner: int32 [16, 3072, 1], P('sec', 'xy'), may hold values from 0 to 31; in each aligned block of 96 rows (0 to 95, 96 to 191, ..., all dimensions but the last counted through in order) at most 6 rows name the same one
- piece_slot: int32 [16, 3072], P('sec', 'xy'), may hold values from 0 to 63
- blend: float32 [16, 3072], P('sec', 'xy'), may hold values from 0.5 to 2
Outputs:
- relaxed_mesh: float32 [15, 2, 64, 32], P(None, None, 'xy', 'sec')
The draws below stay inside these ranges and needn't reach their ends.
Inputs may be any that keep to these rules, and one draw needn't show every extreme that they name: `piece_owner`: among the pieces of one section held by one index of xy (an aligned block of 96), no block is named more than 6 times.
All inputs are finite; a program needn't handle non-finite values.
Results may differ from the reference program's by a relative error of at most 0.0023.
Values may be sent and summed in bfloat16 or wider, within the bound.
No kernel may reach another device: no remote copies, remote signals or barrier semaphores. Data moves between devices by JAX's collectives and lax.ppermute only.
A program may use at most 128 MiB of HBM per device.

```python
import math
import jax
import jax.numpy as jnp
import numpy as np
from jax import lax

PS = 64
PIECES_DEV = 96
ITERS = 8
SECTIONS = 16
PAIRS = 15
PIECES_SEC = 3072
BLOCK = 64
GX = 64
GY = 32
CAP = 6
N_XY = 32


def set_ends(result, key, smallest, high):
    place = [jax.random.randint(jax.random.fold_in(key, axis), (), 0, length) for axis, length in enumerate(result.shape)]
    longest = result.shape.index(max(result.shape))
    beside = place[:longest] + [(place[longest] + 1) % result.shape[longest]] + place[longest + 1:]
    return result.at[tuple(place)].set(smallest).at[tuple(beside)].set(high)


def levels(rng, extent, split, least, top_value):
    level, own = 1.0, jax.random.fold_in(rng, 6)
    for position, parts in split:
        draws = jnp.exp(jax.random.uniform(jax.random.fold_in(own, position), (parts,), jnp.float32, least / len(split), top_value / len(split)))
        level = level * jnp.repeat(draws, extent[position] // parts).reshape([-1 if axis == position else 1 for axis in range(len(extent))])
    return level


def shared_out(key, own, number, rows, amount, top, limit, slope):
    ranking = jax.random.permutation(key, amount)
    packed, ordinary = load_shares(amount, rows * top, limit, slope, True), load_shares(amount, rows * top, limit, slope, False)
    places = jnp.arange(amount)

    def named(sizes, offset_by):
        used = int((sizes > 0).sum())
        fixed = max(1, used // 4)
        shifted = fixed + (places - fixed + offset_by * (used - fixed)) % max(1, amount - fixed)
        return jnp.zeros((amount,), jnp.int32).at[ranking[jnp.where(places < fixed, places, shifted)]].set(jnp.asarray(sizes, jnp.int32))

    sizes = jnp.where(number % 4 == 0, named(packed, number // 4), named(ordinary, number - number // 4 - 1))
    mixed = jax.random.permutation(jax.random.fold_in(own, 3), amount)
    source_of, receiver = mixed[0:amount // 2 * 2:2], mixed[1:amount // 2 * 2:2]
    slack = jnp.minimum(sizes[source_of] - 1, limit - sizes[receiver]) // 2
    slack = jnp.where((source_of == ranking[0]) | (receiver == ranking[0]) | (sizes[receiver] == 0), 0, jnp.maximum(slack, 0))
    shifted = jax.random.randint(jax.random.fold_in(own, 4), (amount // 2,), 0, 1 << 20) % (slack + 1)
    sizes = sizes.at[source_of].add(-shifted).at[receiver].add(shifted)
    items = jnp.searchsorted(jnp.cumsum(sizes), jnp.arange(rows * top), side="right").astype(jnp.int32)
    table = items.reshape(top, rows).T
    table = table[jax.random.permutation(jax.random.fold_in(own, 1), rows)]
    offset_by = jax.random.randint(jax.random.fold_in(own, 2), (rows, 1), 0, top)
    return jnp.take_along_axis(table, (jnp.arange(top)[None, :] + offset_by) % top, axis=1)


def load_shares(amount, total, most, slope, full):
    weights = [(1 << 20) // math.isqrt(rank ** slope) + 1 for rank in range(1, amount + 1)]
    largest = most if full else min(most, max(-(-total // amount), total * weights[0] // sum(weights)))
    least = 1 if total - largest >= amount - 1 else 0
    given, rest = [largest] + [least] * (amount - 1), total - largest - least * (amount - 1)
    while rest > 0:
        movable = [i for i in range(1, amount) if given[i] < largest] or [i for i in range(1, amount) if given[i] < most]
        pool, left = sum([weights[i] for i in movable]), rest
        for i in movable:
            extra = min(most - given[i], max(1, left * weights[i] // pool), rest)
            given[i] = given[i] + extra
            rest = rest - extra
    return np.array(given)


def bell_draw(own_key, dims, width, most, cuts=(), kind=jnp.bfloat16):
    entries = width * jax.random.normal(own_key, dims, jnp.float32)
    if cuts:
        entries = entries * levels(own_key, dims, cuts, -0.22, 0.18)
    return jnp.clip(entries, -most, most).astype(kind)


def setup_inputs(seed: int = 0) -> dict:
    streams_of = jax.random.split(jax.random.key(seed), 5)
    raw_pieces = bell_draw(streams_of[0], (SECTIONS, PIECES_SEC, PS * PS), 1.0, 6.0, ((0, 4), (1, 32)))
    piece_owner_keys = jax.random.split(jax.random.fold_in(streams_of[1], 1), SECTIONS * PIECES_SEC // PIECES_DEV)
    piece_owner_turns = jax.random.permutation(jax.random.fold_in(streams_of[1], 3), SECTIONS * PIECES_SEC // PIECES_DEV)
    piece_owner = jax.vmap(lambda own, number: shared_out(jax.random.fold_in(streams_of[1], 2), own, number, PIECES_DEV, N_XY, 1, CAP, 2))(piece_owner_keys, piece_owner_turns).reshape((SECTIONS, PIECES_SEC, 1))
    piece_slot = set_ends(jax.random.randint(streams_of[2], (SECTIONS, PIECES_SEC), 0, BLOCK), jax.random.fold_in(streams_of[2], 1), 0, BLOCK - 1).astype(jnp.int32)
    blend = jnp.clip(jnp.exp(math.log(2.0) - 1.3862944 * jax.random.uniform(streams_of[3], (SECTIONS, PIECES_SEC), jnp.float32) ** levels(streams_of[3], (SECTIONS, PIECES_SEC), ((0, 4), (1, 32)), -0.2, 0.2)), 0.5, 2.0)
    return dict(raw_pieces=raw_pieces, piece_owner=piece_owner, piece_slot=piece_slot, blend=blend)


def normalize(patch):
    mean = lax.optimization_barrier(jnp.mean(patch, axis=(-2, -1), keepdims=True))
    centred = patch - mean
    var = lax.optimization_barrier(jnp.mean(centred * centred, axis=(-2, -1), keepdims=True))
    return centred / jnp.sqrt(var + 1e-05)

def relax_step(mesh, target):
    padded = jnp.pad(mesh, ((0, 0), (0, 0), (1, 1), (1, 1)))
    lap = padded[:, :, 2:, 1:-1] + padded[:, :, :-2, 1:-1] + padded[:, :, 1:-1, 2:] + padded[:, :, 1:-1, :-2] - 4.0 * mesh
    return mesh + 0.2 * (target - mesh + lap)

def reference(raw_pieces, piece_owner, piece_slot, blend):
    segments = N_XY * BLOCK

    def stitch_one(args):
        pieces, owner, slot, weight = args
        warped = (pieces.astype(jnp.float32) * weight[:, None]).astype(jnp.bfloat16)
        ids = owner[:, 0] * BLOCK + slot
        summed = jax.ops.segment_sum(warped.astype(jnp.float32), ids, num_segments=segments)
        return summed.astype(jnp.bfloat16)
    stitched = lax.map(stitch_one, (raw_pieces, piece_owner, piece_slot, blend))
    grid = stitched.reshape(SECTIONS, GX, GY, PS, PS)
    shifts = ((jnp.arange(PS) + PS // 2) % PS - PS // 2).astype(jnp.float32)

    def flow_one(index):
        first = normalize(lax.dynamic_index_in_dim(grid, index, 0, keepdims=False).astype(jnp.float32))
        second = normalize(lax.dynamic_index_in_dim(grid, index + 1, 0, keepdims=False).astype(jnp.float32))
        spec_a = jnp.fft.fft2(first)
        spec_b = jnp.fft.fft2(second)
        corr = jnp.real(jnp.fft.ifft2(jnp.conj(spec_a) * spec_b)) / float(PS * PS)
        power = corr * corr
        total = jnp.maximum(lax.optimization_barrier(jnp.sum(power, axis=(-2, -1))), 0.5)
        along_x = lax.optimization_barrier(jnp.sum(power * shifts[:, None], axis=(-2, -1))) / total
        along_y = lax.optimization_barrier(jnp.sum(power * shifts[None, :], axis=(-2, -1))) / total
        return jnp.stack([along_x, along_y], axis=0).astype(jnp.float32)
    flow = lax.map(flow_one, jnp.arange(PAIRS, dtype=jnp.int32))
    mesh = flow
    for step in range(ITERS):
        mesh = relax_step(mesh, flow)
    return mesh
```

```python
import functools
import math

import jax
import jax.numpy as jnp
import numpy as np
from jax import lax
from jax.experimental import pallas as pl
from jax.experimental.pallas import tpu as pltpu
from jax.sharding import PartitionSpec as P

PS = 64
FLAT = PS * PS
CAP = 6
N_SEC = 4
N_XY = 32
SEC_DEV = 4
PIECES = 96
BLOCK = 64
ITERS = 8
ROWS_IN = SEC_DEV * PIECES
CHUNK = SEC_DEV * CAP
ROWS_OUT = N_XY * CHUNK
SLOT_LANES = 128
WIDTH = FLAT + SLOT_LANES
PATCHES = SEC_DEV * BLOCK
TILE = 256
TILES = FLAT // TILE
GYW = 24
F32 = jnp.float32
BF16 = jnp.bfloat16
VMEM_LIMIT = 56 * 1024 * 1024

NT = (((1,), (1,)), ((), ()))
NN = (((1,), (0,)), ((), ()))


def real_basis(kind):
    pos = np.arange(PS)
    rows = {}
    for k in range(32):
        angle = 2.0 * math.pi * ((k * pos) % PS) / PS
        rows[k, 0] = np.cos(angle)
        rows[k, 1] = np.sin(angle) if k else np.cos(math.pi * pos)
    if kind == "forward":
        for (k, part), row in rows.items():
            rows[k, part] = row * (math.sqrt(2.0) if k else 1.0) / 8.0
    x_order = np.stack([rows[k, part] for part in range(2) for k in range(32)])
    y_order = np.stack([rows[k, part] for k in range(32) for part in range(2)])
    return x_order, y_order


def split_table(table):
    high = table.astype(jnp.bfloat16)
    low = (table - high.astype(np.float64)).astype(jnp.bfloat16)
    return np.concatenate([high, low], axis=0)


def tables():
    fwd_x, fwd_y = real_basis("forward")
    inv_x, inv_y = real_basis("inverse")
    eye = np.eye(4)
    first = np.einsum("ab,ky->kaby", eye, fwd_y).reshape(256, 256)
    second = np.einsum("ab,ktx->aktbx", eye, fwd_x.reshape(64, 16, 4)).reshape(256, 256)
    third = np.einsum("ab,kd->dabk", eye, inv_x).reshape(256, 256)
    fourth = np.einsum("ab,qkd->adqbk", eye, inv_y.reshape(16, 4, 64)).reshape(256, 256)
    return [split_table(t) for t in (first, second, third, fourth)]


def mm(a, b, dims=NN):
    return lax.dot_general(a, b, dims, preferred_element_type=F32)


def split(value):
    high = value.astype(BF16)
    return high, (value - high.astype(F32)).astype(BF16)


def mm3(table, high, low):
    both = mm(table, high)
    return both[:256] + both[256:] + mm(table[:256], low)


def send_kernel(meta_ref, raw_ref, out_ref, select, blend, warped):
    step = pl.program_id(0)

    @pl.when(step == 0)
    def _():
        key = meta_ref[0:1, :]
        column = jnp.broadcast_to(key, (128, ROWS_IN)).T
        column = jnp.concatenate([column] * 3, axis=1)
        before = lax.broadcasted_iota(jnp.int32, (ROWS_IN, ROWS_IN), 0) < lax.broadcasted_iota(
            jnp.int32, (ROWS_IN, ROWS_IN), 1
        )
        same = jnp.where((column == key) & before, 1.0, 0.0)
        rank = jnp.sum(same, axis=0, keepdims=True)
        target = (meta_ref[1:2, :] + rank).astype(jnp.int32)
        rows = lax.broadcasted_iota(jnp.int32, (ROWS_OUT, ROWS_IN), 0)
        select[...] = jnp.where(rows == target, 1.0, 0.0).astype(BF16)
        blend[...] = jnp.broadcast_to(meta_ref[2:3, :], (128, ROWS_IN)).T

    part = out_ref.shape[1]
    scale = blend[...]
    for lane in range(0, part, 128):
        warped[:, lane : lane + 128] = (
            raw_ref[:, lane : lane + 128].astype(F32) * scale
        ).astype(BF16)

    @pl.when(step == pl.num_programs(0) - 1)
    def _():
        slot = jnp.broadcast_to(meta_ref[3:4, :], (128, ROWS_IN)).T
        warped[:, part - 128 :] = slot.astype(BF16)

    out_ref[...] = mm(select[...], warped[...]).astype(BF16)


def send_rows(meta, raw):
    part = WIDTH // 3
    return pl.pallas_call(
        send_kernel,
        grid=(3,),
        out_shape=jax.ShapeDtypeStruct((ROWS_OUT, WIDTH), BF16),
        in_specs=[
            pl.BlockSpec((8, ROWS_IN), lambda i: (0, 0)),
            pl.BlockSpec((ROWS_IN, part), lambda i: (0, i)),
        ],
        out_specs=pl.BlockSpec((ROWS_OUT, part), lambda i: (0, i)),
        scratch_shapes=[
            pltpu.VMEM((ROWS_OUT, ROWS_IN), BF16),
            pltpu.VMEM((ROWS_IN, 128), F32),
            pltpu.VMEM((ROWS_IN, part), BF16),
        ],
        compiler_params=pltpu.CompilerParams(vmem_limit_bytes=VMEM_LIMIT),
    )(meta, raw)


def stitch_kernel(slot_ref, rows_ref, table_ref, first_ref, high_ref, low_ref, place):
    @pl.when(pl.program_id(0) == 0)
    def _():
        ids = slot_ref[...].astype(F32).T
        wanted = lax.broadcasted_iota(jnp.int32, (PATCHES, ROWS_OUT), 0).astype(F32) + 1.0
        place[...] = jnp.where(jnp.concatenate([ids, ids], axis=0) == wanted, 1.0, 0.0).astype(BF16)

    patches = mm(place[...], rows_ref[...]).astype(BF16)
    first_ref[...] = patches[:BLOCK]
    both = mm(table_ref[...], patches, NT)
    high, low = split(both[:256] + both[256:])
    high_ref[0] = high
    low_ref[0] = low


def stitch(rows, table):
    half = jax.ShapeDtypeStruct((TILES, 256, PATCHES), BF16)
    return pl.pallas_call(
        stitch_kernel,
        grid=(TILES,),
        out_shape=[jax.ShapeDtypeStruct((BLOCK, FLAT), BF16), half, half],
        in_specs=[
            pl.BlockSpec((ROWS_OUT, SLOT_LANES), lambda t: (0, FLAT // SLOT_LANES)),
            pl.BlockSpec((ROWS_OUT, TILE), lambda t: (0, t)),
            pl.BlockSpec((512, 256), lambda t: (0, 0)),
        ],
        out_specs=[
            pl.BlockSpec((BLOCK, TILE), lambda t: (0, t)),
            pl.BlockSpec((1, 256, PATCHES), lambda t: (t, 0, 0)),
            pl.BlockSpec((1, 256, PATCHES), lambda t: (t, 0, 0)),
        ],
        scratch_shapes=[pltpu.VMEM((PATCHES, ROWS_OUT), BF16)],
        compiler_params=pltpu.CompilerParams(vmem_limit_bytes=VMEM_LIMIT),
        cost_estimate=pl.CostEstimate(
            flops=2 * TILES * 256 * 256 * 5 * 256, bytes_accessed=12 << 20, transcendentals=0
        ),
    )(rows, rows, table)


def second_kernel(high_ref, low_ref, table_ref, out_ref):
    high = high_ref[...].reshape(256, PATCHES)
    low = low_ref[...].reshape(256, PATCHES)
    out_ref[0] = mm3(table_ref[...], high, low)


def second(high, low, table):
    return pl.pallas_call(
        second_kernel,
        grid=(TILES,),
        out_shape=jax.ShapeDtypeStruct((TILES, 256, PATCHES), F32),
        in_specs=[
            pl.BlockSpec((TILES, 16, PATCHES), lambda q: (0, q, 0)),
            pl.BlockSpec((TILES, 16, PATCHES), lambda q: (0, q, 0)),
            pl.BlockSpec((512, 256), lambda q: (0, 0)),
        ],
        out_specs=pl.BlockSpec((1, 256, PATCHES), lambda q: (q, 0, 0)),
        compiler_params=pltpu.CompilerParams(vmem_limit_bytes=VMEM_LIMIT),
        cost_estimate=pl.CostEstimate(
            flops=2 * TILES * 256 * 256 * 3 * 256, bytes_accessed=8 << 20, transcendentals=0
        ),
    )(high, low, table)


def sublane_sum(value):
    total = value[0:8]
    for row in range(8, value.shape[0], 8):
        total = total + value[row : row + 8]
    return total


def signed(index):
    return float((index + 32) % 64 - 32)


def cross(a, b, whole):
    def along_y(p, r):
        if whole:
            return a[p, 0] * b[r, 0], a[p, 1] * b[r, 1]
        return a[p, 0] * b[r, 0] + a[p, 1] * b[r, 1], a[p, 0] * b[r, 1] - a[p, 1] * b[r, 0]

    cc, cs, sc, ss = along_y(0, 0), along_y(0, 1), along_y(1, 0), along_y(1, 1)
    head = lax.broadcasted_iota(jnp.int32, cc[0].shape, 0) == 0
    out = {}
    for part in range(2):
        out[0, part] = cc[part] + jnp.where(head, 0.0, ss[part])
        out[1, part] = jnp.where(head, ss[part], cs[part] - sc[part])
    return out


def flow_kernel(
    spec_ref, next_ref, first_ref, second_ref, third_ref, fourth_ref, out_ref,
    next_high, next_low, back_high, back_low, square, next_square, sum_y, sum_x,
):
    lanes = PATCHES
    def next_first(t, carry):
        tile = next_ref[t]
        both = mm(first_ref[...], tile, NT)
        high, low = split(both[:256] + both[256:])
        next_high[t] = high
        next_low[t] = low
        return carry

    lax.fori_loop(0, TILES, next_first, 0)
    square[...] = jnp.zeros_like(square)
    next_square[...] = jnp.zeros_like(next_square)
    left = lax.broadcasted_iota(jnp.int32, (256, 128), 1) < BLOCK

    def per_q(q, carry):
        rows = pl.ds(pl.multiple_of(q * 16, 16), 16)
        follow = mm3(
            second_ref[...],
            next_high[:, rows, :].reshape(256, 128),
            next_low[:, rows, :].reshape(256, 128),
        )
        own = spec_ref[q]
        dc = (lax.broadcasted_iota(jnp.int32, (256, 1), 0) + q * 256) == 0
        own = jnp.where(dc, 0.0, own)
        follow = jnp.where(dc, 0.0, follow)
        low_half, high_half = own[:, :128], own[:, 128:]
        low_roll, high_roll = pltpu.roll(low_half, 64, 1), pltpu.roll(high_half, 64, 1)
        other = jnp.concatenate(
            [
                jnp.where(left, low_roll, high_roll),
                jnp.where(left, high_roll, pltpu.roll(follow, 64, 1)),
            ],
            axis=1,
        )
        square[...] += sublane_sum(own * own)
        next_square[...] += sublane_sum(other * other)
        def parts(value, base):
            return {
                (x, y): value[base + y * 64 + x * 32 : base + y * 64 + x * 32 + 32]
                for x in range(2)
                for y in range(2)
            }

        def emit(whole_first):
            pieces = []
            for yk in range(2):
                out = cross(
                    parts(own, yk * 128), parts(other, yk * 128), whole_first and yk == 0
                )
                pieces += [out[0, 0], out[1, 0], out[0, 1], out[1, 1]]
            high, low = split(jnp.concatenate(pieces, axis=0))
            high, low = split(mm3(third_ref[...], high, low))
            back_high[q] = high
            back_low[q] = low

        @pl.when(q == 0)
        def _():
            emit(True)

        @pl.when(q != 0)
        def _():
            emit(False)

        return carry

    lax.fori_loop(0, TILES, per_q, 0)
    sum_y[...] = jnp.zeros_like(sum_y)
    sum_x[...] = jnp.zeros_like(sum_x)

    def per_g(g, carry):
        rows = pl.ds(pl.multiple_of(g * 16, 16), 16)
        corr = mm3(
            fourth_ref[...],
            back_high[:, rows, :].reshape(256, lanes),
            back_low[:, rows, :].reshape(256, lanes),
        )
        power = corr * corr
        all_d0 = power[0:64]
        weighted = jnp.zeros((8, lanes), F32)
        for d in range(4):
            block = power[d * 64 : d * 64 + 64]
            if d:
                all_d0 = all_d0 + block
            index = g * 4 + d
            shift = jnp.where(index < 32, index, index - 64).astype(F32)
            weighted = weighted + sublane_sum(block) * shift
        sum_y[...] += all_d0
        sum_x[...] += weighted
        return carry

    lax.fori_loop(0, TILES, per_g, 0)

    def down(value):
        return jnp.sum(value, axis=0, keepdims=True)

    index = lax.broadcasted_iota(jnp.int32, (64, lanes), 0)
    shift = jnp.where(index < 32, index, index - 64).astype(F32)
    total = down(sum_y[...])
    along_x = down(sum_x[...])
    along_y = down(sum_y[...] * shift)
    norm = (down(square[...]) * (1.0 / FLAT) + 1e-05) * (
        down(next_square[...]) * (1.0 / FLAT) + 1e-05
    )
    factor = (1.0 / (float(FLAT) * float(FLAT))) / norm
    total = jnp.maximum(total * factor, 0.5)
    flow = jnp.concatenate([along_x * factor / total, along_y * factor / total], axis=0)
    tile_rows = []
    for half in range(2):
        value = flow[:, half * 128 : half * 128 + 128]
        tile_rows += [value, pltpu.roll(value, 64, 1)]
    grid = jnp.concatenate(tile_rows, axis=0)
    lane = lax.broadcasted_iota(jnp.int32, (8, 128), 1)
    for j in range(N_SEC):
        upper = pltpu.roll(grid, (8 - 8 * j) % 128, 1)
        lower = pltpu.roll(grid, (128 - 8 * j) % 128, 1)
        gy = jnp.where(lane < GYW, lane, lane - GYW) + (8 * j - 8)
        window = jnp.where(lane < GYW, upper, lower)
        window = jnp.where((lane < 2 * GYW) & (gy >= 0) & (gy < 32), window, 0.0)
        out_ref[j] = jnp.broadcast_to(window[None, :, : 2 * GYW], (N_XY, 8, 2 * GYW))


def flow_windows(spec, following, tabs):
    return pl.pallas_call(
        flow_kernel,
        out_shape=jax.ShapeDtypeStruct((N_SEC, N_XY, 8, 2 * GYW), F32),
        scratch_shapes=[
            pltpu.VMEM((TILES, 256, 128), BF16),
            pltpu.VMEM((TILES, 256, 128), BF16),
            pltpu.VMEM((TILES, 256, PATCHES), BF16),
            pltpu.VMEM((TILES, 256, PATCHES), BF16),
            pltpu.VMEM((8, PATCHES), F32),
            pltpu.VMEM((8, PATCHES), F32),
            pltpu.VMEM((64, PATCHES), F32),
            pltpu.VMEM((8, PATCHES), F32),
        ],
        compiler_params=pltpu.CompilerParams(vmem_limit_bytes=VMEM_LIMIT),
        cost_estimate=pl.CostEstimate(
            flops=2 * TILES * 256 * 256 * 8 * 256, bytes_accessed=8 << 20, transcendentals=0
        ),
    )(spec, following, *tabs)


def relax_kernel(place_ref, arrived_ref, out_ref):
    column, block = place_ref[0], place_ref[1]
    lane = lax.broadcasted_iota(jnp.int32, (8, 128), 1)
    top = lane < GYW
    gy = jnp.where(top, lane, lane - GYW) + (8 * column - 8)
    inside = (lane < 2 * GYW) & (gy >= 0) & (gy < 32)
    mask = {}
    for o in range(-4, 5):
        valid = (block + o >= 0) & (block + o < N_XY)
        mask[o] = jnp.where(inside & valid, 0.2, 0.0)
    for s in range(N_SEC):
        flow, mesh = {}, {}
        for o in range(-4, 5):
            at = jnp.clip(block + o, 0, N_XY - 1)
            value = arrived_ref[s, at]
            value = jnp.concatenate([value, jnp.zeros((8, 128 - 2 * GYW), F32)], axis=1)
            flow[o] = value * mask[o]
            mesh[o] = jnp.where(mask[o] > 0.0, value, 0.0)
        for step in range(ITERS):
            reach = (ITERS - step) // 2
            up = {o: pltpu.roll(mesh[o], 128 - GYW, 1) for o in mesh}
            down = {o: pltpu.roll(mesh[o], GYW, 1) for o in mesh}
            new = {}
            zero = jnp.zeros((8, 128), F32)
            for o in range(-reach, reach + 1):
                near = jnp.where(
                    top, up[o] + up.get(o - 1, zero), down[o] + down.get(o + 1, zero)
                )
                near = near + pltpu.roll(mesh[o], 1, 1) + pltpu.roll(mesh[o], 127, 1)
                new[o] = flow[o] + mask[o] * near
            mesh = new
        out_ref[s] = mesh[0]


def relax(place, arrived):
    return pl.pallas_call(
        relax_kernel,
        out_shape=jax.ShapeDtypeStruct((N_SEC, 8, 128), F32),
        in_specs=[
            pl.BlockSpec(memory_space=pltpu.SMEM),
            pl.BlockSpec(memory_space=pltpu.VMEM),
        ],
        out_specs=pl.BlockSpec(memory_space=pltpu.VMEM),
        compiler_params=pltpu.CompilerParams(vmem_limit_bytes=VMEM_LIMIT),
    )(place, arrived)


def local(raw_pieces, piece_owner, piece_slot, blend):
    tabs = [jnp.asarray(t) for t in tables()]
    owner = piece_owner[:, :, 0].astype(F32)
    section = jnp.arange(SEC_DEV, dtype=F32)[:, None]
    zero = jnp.zeros((SEC_DEV, PIECES), F32)
    meta = jnp.stack(
        [
            owner + N_XY * section,
            owner * CHUNK + section * CAP,
            blend,
            piece_slot.astype(F32) + (section * BLOCK + 1.0),
            zero, zero, zero, zero,
        ]
    ).reshape(8, ROWS_IN)
    outgoing = send_rows(meta, raw_pieces.reshape(ROWS_IN, FLAT))
    arrived = lax.all_to_all(outgoing, "xy", split_axis=0, concat_axis=0, tiled=True)
    first, high, low = stitch(arrived, tabs[0])
    back = [(i + 1, i) for i in range(N_SEC - 1)]
    following = lax.ppermute(first, "sec", back)
    spec = second(high, low, tabs[1])
    following = following.reshape(BLOCK, TILES, TILE).transpose(1, 0, 2)
    following = jnp.pad(following, ((0, 0), (0, 128 - BLOCK), (0, 0)))
    windows = flow_windows(spec, following, tabs)
    got = lax.all_to_all(
        windows.reshape(N_SEC * N_XY, 8, 2 * GYW), ("sec", "xy"), split_axis=0, concat_axis=0,
        tiled=True,
    )
    place = jnp.stack([lax.axis_index("sec"), lax.axis_index("xy")]).astype(jnp.int32)
    mesh = relax(place, got.reshape(N_SEC, N_XY, 8, 2 * GYW))
    mesh = mesh.reshape(N_SEC * 4, 2, 128)[:15, :, : 2 * GYW].reshape(15, 2, 2, GYW)
    return mesh[:, :, :, 8:16]


def solution(mesh):
    in_specs = (P("sec", "xy", None), P("sec", "xy", None), P("sec", "xy"), P("sec", "xy"))
    out_specs = P(None, None, "xy", "sec")
    return jax.shard_map(local, mesh=mesh, in_specs=in_specs, out_specs=out_specs, check_vma=False)
```

```python
import math

import jax
import jax.numpy as jnp
import numpy as np
from jax import lax
from jax.experimental import pallas as pl
from jax.experimental.pallas import tpu as pltpu
from jax.sharding import PartitionSpec as P

PS = 64
FLAT = PS * PS
CAP = 6
N_SEC = 4
N_XY = 32
SEC_DEV = 4
PIECES = 96
BLOCK = 64
ITERS = 8
KEYS = SEC_DEV * 128
CHUNK = SEC_DEV * CAP
ROWS_OUT = N_XY * CHUNK
SLOT_LANES = 128
WIDTH = FLAT + SLOT_LANES
PATCHES = SEC_DEV * BLOCK
TILE = 256
TILES = FLAT // TILE
GYW = 24
F32 = jnp.float32
BF16 = jnp.bfloat16
VMEM_LIMIT = 56 * 1024 * 1024

NT = (((1,), (1,)), ((), ()))
NN = (((1,), (0,)), ((), ()))


def real_basis(kind):
    pos = np.arange(PS)
    rows = {}
    for k in range(32):
        angle = 2.0 * math.pi * ((k * pos) % PS) / PS
        rows[k, 0] = np.cos(angle)
        rows[k, 1] = np.sin(angle) if k else np.cos(math.pi * pos)
    if kind == "forward":
        for (k, part), row in rows.items():
            rows[k, part] = row * (math.sqrt(2.0) if k else 1.0) / 8.0
    x_order = np.stack([rows[k, part] for part in range(2) for k in range(32)])
    y_order = np.stack([rows[k, part] for k in range(32) for part in range(2)])
    return x_order, y_order


def split_table(table):
    high = table.astype(jnp.bfloat16)
    low = (table - high.astype(np.float64)).astype(jnp.bfloat16)
    return np.concatenate([high, low], axis=0)


def tables():
    fwd_x, fwd_y = real_basis("forward")
    inv_x, inv_y = real_basis("inverse")
    eye = np.eye(4)
    first = np.einsum("ab,ky->kaby", eye, fwd_y).reshape(256, 256)
    second = np.einsum("ab,ktx->aktbx", eye, fwd_x.reshape(64, 16, 4)).reshape(256, 256)
    third = np.einsum("ab,kd->dabk", eye, inv_x).reshape(256, 256)
    fourth = np.einsum("ab,qkd->adqbk", eye, inv_y.reshape(16, 4, 64)).reshape(256, 256)
    return [split_table(t) for t in (first, second, third, fourth)]


def mm(a, b, dims=NN):
    return lax.dot_general(a, b, dims, preferred_element_type=F32)


def split(value):
    high = value.astype(BF16)
    return high, (value - high.astype(F32)).astype(BF16)


def mm3(table, high, low):
    both = mm(table, high)
    return both[:256] + both[256:] + mm(table[:256], low)


def lane_rows(scratch, ref):
    scratch[...] = jnp.zeros_like(scratch)
    scratch[0:SEC_DEV, 0:PIECES] = ref[...].astype(F32)
    return scratch[0:SEC_DEV, :]


def column(row):
    return jnp.broadcast_to(row, (128, 128)).T


def send_kernel(owner_ref, slot_ref, blend_ref, raw_ref, out_ref, lanes, select, blend, slots, warped):
    step = pl.program_id(0)

    @pl.when(step == 0)
    def _():
        warped[...] = jnp.zeros_like(warped)
        owners = lane_rows(lanes, owner_ref)
        slot_rows = lane_rows(lanes, slot_ref)
        blend_rows = lane_rows(lanes, blend_ref)
        line = lax.broadcasted_iota(jnp.int32, (128, 128), 0)
        lane = lax.broadcasted_iota(jnp.int32, (128, 128), 1)
        rows = lax.broadcasted_iota(jnp.int32, (ROWS_OUT, 128), 0)
        for s in range(SEC_DEV):
            owner = owners[s : s + 1]
            same = jnp.where((column(owner) == owner) & (line < lane), 1.0, 0.0)
            rank = jnp.sum(same, axis=0, keepdims=True)
            target = (owner * CHUNK + rank + float(s * CAP)).astype(jnp.int32)
            target = jnp.where(lane[0:1] < PIECES, target, -1)
            at = slice(128 * s, 128 * s + 128)
            select[:, at] = jnp.where(rows == target, 1.0, 0.0).astype(BF16)
            blend[at, :] = column(blend_rows[s : s + 1])
            slots[at, :] = (column(slot_rows[s : s + 1]) + float(s * BLOCK + 1)).astype(BF16)

    part = out_ref.shape[1]
    for s in range(SEC_DEV):
        at = slice(128 * s, 128 * s + PIECES)
        scale = blend[at, :]
        for lane in range(0, part, 128):
            warped[at, lane : lane + 128] = (
                raw_ref[s, :, lane : lane + 128].astype(F32) * scale
            ).astype(BF16)

    @pl.when(step == pl.num_programs(0) - 1)
    def _():
        for s in range(SEC_DEV):
            at = slice(128 * s, 128 * s + PIECES)
            warped[at, part - 128 :] = slots[at, :]

    out_ref[...] = mm(select[...], warped[...]).astype(BF16)


def send_rows(owner, slot, blend, raw):
    part = WIDTH // 3
    small = pl.BlockSpec((SEC_DEV, PIECES), lambda i: (0, 0))
    return pl.pallas_call(
        send_kernel,
        grid=(3,),
        out_shape=jax.ShapeDtypeStruct((ROWS_OUT, WIDTH), BF16),
        in_specs=[small, small, small, pl.BlockSpec((SEC_DEV, PIECES, part), lambda i: (0, 0, i))],
        out_specs=pl.BlockSpec((ROWS_OUT, part), lambda i: (0, i)),
        scratch_shapes=[
            pltpu.VMEM((8, 128), F32),
            pltpu.VMEM((ROWS_OUT, KEYS), BF16),
            pltpu.VMEM((KEYS, 128), F32),
            pltpu.VMEM((KEYS, 128), BF16),
            pltpu.VMEM((KEYS, part), BF16),
        ],
        compiler_params=pltpu.CompilerParams(vmem_limit_bytes=VMEM_LIMIT),
    )(owner, slot, blend, raw)


LANES_B = 1024


def stitch_kernel(slot_ref, rows_ref, first_ref, out_ref, place):
    @pl.when(pl.program_id(0) == 0)
    def _():
        ids = slot_ref[...].astype(F32).T
        wanted = lax.broadcasted_iota(jnp.int32, (PATCHES, ROWS_OUT), 0).astype(F32) + 1.0
        place[...] = jnp.where(jnp.concatenate([ids, ids], axis=0) == wanted, 1.0, 0.0).astype(BF16)

    patches = mm(place[...], rows_ref[...]).astype(BF16)
    first_ref[...] = patches[:BLOCK]
    out_ref[...] = patches


def stitch(rows):
    return pl.pallas_call(
        stitch_kernel,
        grid=(FLAT // LANES_B,),
        out_shape=[
            jax.ShapeDtypeStruct((BLOCK, FLAT), BF16),
            jax.ShapeDtypeStruct((PATCHES, FLAT), BF16),
        ],
        in_specs=[
            pl.BlockSpec((ROWS_OUT, SLOT_LANES), lambda t: (0, FLAT // SLOT_LANES)),
            pl.BlockSpec((ROWS_OUT, LANES_B), lambda t: (0, t)),
        ],
        out_specs=[
            pl.BlockSpec((BLOCK, LANES_B), lambda t: (0, t)),
            pl.BlockSpec((PATCHES, LANES_B), lambda t: (0, t)),
        ],
        scratch_shapes=[pltpu.VMEM((PATCHES, ROWS_OUT), BF16)],
        compiler_params=pltpu.CompilerParams(vmem_limit_bytes=VMEM_LIMIT),
    )(rows, rows)


GROUP = 4
GROUPS = TILES // GROUP


def spectrum_kernel(patch_ref, first_ref, second_ref, out_ref, high, low):
    @pl.when(pl.program_id(0) == 0)
    def _():
        for t in range(TILES):
            both = mm(first_ref[...], patch_ref[:, t * TILE : t * TILE + TILE], NT)
            high[t], low[t] = split(both[:256] + both[256:])

    for i in range(GROUP):
        at = pl.ds(pl.multiple_of(pl.program_id(0) * (16 * GROUP) + 16 * i, 16), 16)
        out_ref[i] = mm3(
            second_ref[...],
            high[:, at, :].reshape(256, PATCHES),
            low[:, at, :].reshape(256, PATCHES),
        )


def spectrum(patches, first, second):
    return pl.pallas_call(
        spectrum_kernel,
        grid=(GROUPS,),
        out_shape=jax.ShapeDtypeStruct((TILES, 256, PATCHES), F32),
        in_specs=[
            pl.BlockSpec((PATCHES, FLAT), lambda q: (0, 0)),
            pl.BlockSpec((512, 256), lambda q: (0, 0)),
            pl.BlockSpec((512, 256), lambda q: (0, 0)),
        ],
        out_specs=pl.BlockSpec((GROUP, 256, PATCHES), lambda q: (q, 0, 0)),
        scratch_shapes=[
            pltpu.VMEM((TILES, 256, PATCHES), BF16),
            pltpu.VMEM((TILES, 256, PATCHES), BF16),
        ],
        compiler_params=pltpu.CompilerParams(vmem_limit_bytes=VMEM_LIMIT),
        cost_estimate=pl.CostEstimate(
            flops=2 * TILES * 256 * 256 * 5 * 256, bytes_accessed=8 << 20, transcendentals=0
        ),
    )(patches, first, second)


def sublane_sum(value):
    total = value[0:8]
    for row in range(8, value.shape[0], 8):
        total = total + value[row : row + 8]
    return total


def next_spectrum(next_ref, first_ref, second_ref, high, low, follow):
    left = lax.broadcasted_iota(jnp.int32, (16, 128), 1) < BLOCK
    for tg in range(GROUPS):
        rows = jnp.concatenate(
            [
                next_ref[:, (GROUP * tg + i) * TILE : (GROUP * tg + i + 1) * TILE]
                for i in range(GROUP)
            ],
            axis=0,
        )
        both = mm(first_ref[...], rows, NT)
        value = both[:256] + both[256:]
        for half in range(2):
            lanes = value[:, half * 128 : half * 128 + 128]
            rolled = pltpu.roll(lanes, BLOCK, 1)
            for pair in range(TILES // 2):
                g, to = pair // 2, (pair % 2) * 128
                even = slice(32 * pair, 32 * pair + 16)
                odd = slice(32 * pair + 16, 32 * pair + 32)
                for i in range(2):
                    t = GROUP * tg + 2 * half + i
                    if i == 0:
                        packed = jnp.where(left, lanes[even], rolled[odd])
                    else:
                        packed = jnp.where(left, rolled[even], lanes[odd])
                    at = slice(16 * t, 16 * t + 16)
                    up, down = split(packed)
                    high[g, at, to : to + 128] = up
                    low[g, at, to : to + 128] = down
    for g in range(GROUPS):
        follow[g] = mm3(second_ref[...], high[g], low[g])


def cross(a, b, first_step):
    def along_y(p, r):
        b_sine, b_cosine = b[r, 1], b[r, 0]
        if first_step is not None:
            b_sine, b_cosine = (
                jnp.where(first_step, 0.0, b_sine),
                jnp.where(first_step, -b_sine, b_cosine),
            )
        return a[p, 0] * b[r, 0] + a[p, 1] * b_sine, a[p, 0] * b_sine - a[p, 1] * b_cosine

    cc, cs, sc, ss = along_y(0, 0), along_y(0, 1), along_y(1, 0), along_y(1, 1)
    head = lax.broadcasted_iota(jnp.int32, cc[0].shape, 0) == 0
    out = {}
    for part in range(2):
        out[0, part] = cc[part] + jnp.where(head, 0.0, ss[part])
        out[1, part] = jnp.where(head, ss[part], cs[part] - sc[part])
    return out


def flow_kernel(
    spec_ref, next_ref, first_ref, second_ref, third_ref, fourth_ref, out_ref,
    next_high, next_low, follow, back_high, back_low, square, next_square, sum_y, sum_x,
):
    lanes = PATCHES
    step = pl.program_id(0)

    @pl.when(step == 0)
    def _():
        next_spectrum(next_ref, first_ref, second_ref, next_high, next_low, follow)
        square[...] = jnp.zeros_like(square)
        next_square[...] = jnp.zeros_like(next_square)

    left = lax.broadcasted_iota(jnp.int32, (256, 128), 1) < BLOCK
    top = lax.broadcasted_iota(jnp.int32, (256, 1), 0) == 0
    own_total = jnp.zeros((8, lanes), F32)
    other_total = jnp.zeros((8, lanes), F32)
    for i in range(GROUP):
        own = spec_ref[i]
        after = follow[step, :, (i // 2) * 128 : (i // 2) * 128 + 128]
        if i == 0:
            zero = top & (step == 0)
            own = jnp.where(zero, 0.0, own)
            after = jnp.where(zero, 0.0, after)
        if i % 2 == 0:
            after = pltpu.roll(after, BLOCK, 1)
        low_roll = pltpu.roll(own[:, :128], BLOCK, 1)
        high_roll = pltpu.roll(own[:, 128:], BLOCK, 1)
        other = jnp.concatenate(
            [jnp.where(left, low_roll, high_roll), jnp.where(left, high_roll, after)], axis=1
        )
        own_total = own_total + sublane_sum(own * own)
        other_total = other_total + sublane_sum(other * other)
        pieces = []
        for yk in range(2):
            a, b = (
                {
                    (x, y): value[yk * 128 + y * 64 + x * 32 : yk * 128 + y * 64 + x * 32 + 32]
                    for x in range(2)
                    for y in range(2)
                }
                for value in (own, other)
            )
            out = cross(a, b, step == 0 if i == 0 and yk == 0 else None)
            pieces += [out[0, 0], out[1, 0], out[0, 1], out[1, 1]]
        high, low = split(jnp.concatenate(pieces, axis=0))
        high, low = split(mm3(third_ref[...], high, low))
        back_high[step * GROUP + i] = high
        back_low[step * GROUP + i] = low
    square[...] += own_total
    next_square[...] += other_total

    @pl.when(step == GROUPS - 1)
    def _():
        finish(fourth_ref, out_ref, back_high, back_low, square, next_square, sum_y, sum_x)


def finish(fourth_ref, out_ref, back_high, back_low, square, next_square, sum_y, sum_x):
    lanes = PATCHES
    sum_y[...] = jnp.zeros_like(sum_y)
    sum_x[...] = jnp.zeros_like(sum_x)

    def per_group(group, carry):
        all_d0 = jnp.zeros((64, lanes), F32)
        weighted = jnp.zeros((8, lanes), F32)
        for i in range(GROUP):
            g = group * GROUP + i
            rows = pl.ds(pl.multiple_of(g * 16, 16), 16)
            corr = mm3(
                fourth_ref[...],
                back_high[:, rows, :].reshape(256, lanes),
                back_low[:, rows, :].reshape(256, lanes),
            )
            power = corr * corr
            for d in range(4):
                block = power[d * 64 : d * 64 + 64]
                all_d0 = all_d0 + block
                index = g * 4 + d
                shift = jnp.where(index < 32, index, index - 64).astype(F32)
                weighted = weighted + sublane_sum(block) * shift
        sum_y[...] += all_d0
        sum_x[...] += weighted
        return carry

    lax.fori_loop(0, GROUPS, per_group, 0)

    def down(value):
        return jnp.sum(value, axis=0, keepdims=True)

    index = lax.broadcasted_iota(jnp.int32, (64, lanes), 0)
    shift = jnp.where(index < 32, index, index - 64).astype(F32)
    total = down(sum_y[...])
    along_x = down(sum_x[...])
    along_y = down(sum_y[...] * shift)
    norm = (down(square[...]) * (1.0 / FLAT) + 1e-05) * (
        down(next_square[...]) * (1.0 / FLAT) + 1e-05
    )
    factor = (1.0 / (float(FLAT) * float(FLAT))) / norm
    total = jnp.maximum(total * factor, 0.5)
    tile_rows = []
    for value in (along_x * factor / total, along_y * factor / total):
        for half in range(2):
            lane_tile = value[:, half * 128 : half * 128 + 128]
            tile_rows += [lane_tile, pltpu.roll(lane_tile, 64, 1)]
    grid = jnp.concatenate(tile_rows, axis=0)
    lane = lax.broadcasted_iota(jnp.int32, (8, 128), 1)
    for j in range(N_SEC):
        upper = pltpu.roll(grid, (8 - 8 * j) % 128, 1)
        lower = pltpu.roll(grid, (128 - 8 * j) % 128, 1)
        gy = jnp.where(lane < GYW, lane, lane - GYW) + (8 * j - 8)
        window = jnp.where(lane < GYW, upper, lower)
        window = jnp.where((lane < 2 * GYW) & (gy >= 0) & (gy < 32), window, 0.0)
        for b in range(N_XY):
            out_ref[(j * N_XY + b) * 8 : (j * N_XY + b) * 8 + 8, :] = window


def flow_windows(spec, following, tabs):
    table = pl.BlockSpec((512, 256), lambda q: (0, 0))
    return pl.pallas_call(
        flow_kernel,
        grid=(GROUPS,),
        out_shape=jax.ShapeDtypeStruct((N_SEC * N_XY * 8, 128), F32),
        in_specs=[
            pl.BlockSpec((GROUP, 256, PATCHES), lambda q: (q, 0, 0)),
            pl.BlockSpec((BLOCK, FLAT), lambda q: (0, 0)),
            table, table, table, table,
        ],
        out_specs=pl.BlockSpec((N_SEC * N_XY * 8, 128), lambda q: (0, 0)),
        scratch_shapes=[
            pltpu.VMEM((GROUPS, 256, 256), BF16),
            pltpu.VMEM((GROUPS, 256, 256), BF16),
            pltpu.VMEM((GROUPS, 256, 256), F32),
            pltpu.VMEM((TILES, 256, PATCHES), BF16),
            pltpu.VMEM((TILES, 256, PATCHES), BF16),
            pltpu.VMEM((8, PATCHES), F32),
            pltpu.VMEM((8, PATCHES), F32),
            pltpu.VMEM((64, PATCHES), F32),
            pltpu.VMEM((8, PATCHES), F32),
        ],
        compiler_params=pltpu.CompilerParams(vmem_limit_bytes=VMEM_LIMIT),
        cost_estimate=pl.CostEstimate(
            flops=2 * TILES * 256 * 256 * 8 * 256, bytes_accessed=8 << 20, transcendentals=0
        ),
    )(spec, following, *tabs)


def relax_kernel(place_ref, arrived_ref, out_ref):
    column, block = place_ref[0], place_ref[1]
    lane = lax.broadcasted_iota(jnp.int32, (8, 128), 1)
    top = lane < GYW
    gy = jnp.where(top, lane, lane - GYW) + (8 * column - 8)
    inside = (lane < 2 * GYW) & (gy >= 0) & (gy < 32)
    mask = {}
    for o in range(-4, 5):
        valid = (block + o >= 0) & (block + o < N_XY)
        mask[o] = jnp.where(inside & valid, 0.2, 0.0)
    zero = jnp.zeros((8, 128), F32)
    result = []
    for s in range(N_SEC):
        flow, mesh = {}, {}
        for o in range(-4, 5):
            at = s * N_XY + jnp.clip(block + o, 0, N_XY - 1)
            value = arrived_ref[pl.ds(pl.multiple_of(at * 8, 8), 8), :]
            flow[o] = value * mask[o]
            mesh[o] = jnp.where(mask[o] > 0.0, value, 0.0)
        for step in range(ITERS):
            reach = (ITERS - step) // 2
            up = {o: pltpu.roll(mesh[o], 128 - GYW, 1) for o in mesh}
            down = {o: pltpu.roll(mesh[o], GYW, 1) for o in mesh}
            new = {}
            for o in range(-reach, reach + 1):
                near = jnp.where(
                    top, up[o] + up.get(o - 1, zero), down[o] + down.get(o + 1, zero)
                )
                near = near + pltpu.roll(mesh[o], 1, 1) + pltpu.roll(mesh[o], 127, 1)
                new[o] = flow[o] + mask[o] * near
            mesh = new
        result.append(mesh[0])
    for c in range(2):
        rows = [value[4 * c : 4 * c + 4] for value in result]
        turned = jnp.concatenate(rows + [jnp.zeros((112, 128), F32)], axis=0).T
        for i in range(2):
            out_ref[c, i] = turned[GYW * i + 8 : GYW * i + 16, :15]


def relax(place, arrived):
    return pl.pallas_call(
        relax_kernel,
        out_shape=jax.ShapeDtypeStruct((2, 2, 8, 15), F32),
        in_specs=[
            pl.BlockSpec(memory_space=pltpu.SMEM),
            pl.BlockSpec(memory_space=pltpu.VMEM),
        ],
        out_specs=pl.BlockSpec(memory_space=pltpu.VMEM),
        compiler_params=pltpu.CompilerParams(vmem_limit_bytes=VMEM_LIMIT),
    )(place, arrived)


def local(raw_pieces, piece_owner, piece_slot, blend):
    tabs = [jnp.asarray(t) for t in tables()]
    outgoing = send_rows(piece_owner[:, :, 0], piece_slot, blend, raw_pieces)
    arrived = lax.all_to_all(outgoing, "xy", split_axis=0, concat_axis=0, tiled=True)
    first, patches = stitch(arrived)
    back = [(i + 1, i) for i in range(N_SEC - 1)]
    following = lax.ppermute(first, "sec", back)
    spec = spectrum(patches, tabs[0], tabs[1])
    windows = flow_windows(spec, following, tabs)
    got = lax.all_to_all(windows, ("sec", "xy"), split_axis=0, concat_axis=0, tiled=True)
    place = jnp.stack([lax.axis_index("sec"), lax.axis_index("xy")]).astype(jnp.int32)
    return relax(place, got).transpose(3, 0, 1, 2)


def solution(mesh):
    in_specs = (P("sec", "xy", None), P("sec", "xy", None), P("sec", "xy"), P("sec", "xy"))
    out_specs = P(None, None, "xy", "sec")
    return jax.shard_map(local, mesh=mesh, in_specs=in_specs, out_specs=out_specs, check_vma=False)
```

```python
import math

import jax
import jax.numpy as jnp
import numpy as np
from jax import lax
from jax.experimental import pallas as pl
from jax.experimental.pallas import tpu as pltpu
from jax.sharding import PartitionSpec as P

PS = 64
FLAT = PS * PS
CAP = 6
N_SEC = 4
N_XY = 32
SEC_DEV = 4
PIECES = 96
BLOCK = 64
ITERS = 8
KEYS = SEC_DEV * 128
CHUNK = SEC_DEV * CAP
LANE_TILES = FLAT // 128
PARTS = CHUNK // 8
TILES_OUT = PARTS * LANE_TILES + 1
PATCHES = SEC_DEV * BLOCK
TILE = 256
TILES = FLAT // TILE
GYW = 24
F32 = jnp.float32
BF16 = jnp.bfloat16
MIB = 1024 * 1024

VMEM_SPEC = pl.BlockSpec(memory_space=pltpu.VMEM)
NT = (((1,), (1,)), ((), ()))
NN = (((1,), (0,)), ((), ()))


def real_basis(kind):
    pos = np.arange(PS)
    rows = {}
    for k in range(32):
        angle = 2.0 * math.pi * ((k * pos) % PS) / PS
        rows[k, 0] = np.cos(angle)
        rows[k, 1] = np.sin(angle) if k else np.cos(math.pi * pos)
    if kind == "forward":
        for (k, part), row in rows.items():
            rows[k, part] = row * (math.sqrt(2.0) if k else 1.0) / 8.0
    x_order = np.stack([rows[k, part] for part in range(2) for k in range(32)])
    y_order = np.stack([rows[k, part] for k in range(32) for part in range(2)])
    return x_order, y_order


def split_table(table):
    high = table.astype(jnp.bfloat16)
    low = (table - high.astype(np.float64)).astype(jnp.bfloat16)
    return np.concatenate([high, low], axis=0)


def tables():
    fwd_x, fwd_y = real_basis("forward")
    inv_x, inv_y = real_basis("inverse")
    eye = np.eye(4)
    first = np.einsum("ab,ky->kaby", eye, fwd_y).reshape(256, 256)
    second = np.einsum("ab,ktx->aktbx", eye, fwd_x.reshape(64, 16, 4)).reshape(256, 256)
    third = np.einsum("ab,kd->dabk", eye, inv_x).reshape(256, 256)
    fourth = np.einsum("ab,qkd->adqbk", eye, inv_y.reshape(16, 4, 64)).reshape(256, 256)
    return [split_table(t) for t in (first, second, third, fourth)]


def mm(a, b, dims=NN):
    return lax.dot_general(a, b, dims, preferred_element_type=F32)


def split(value):
    high = value.astype(BF16)
    return high, (value - high.astype(F32)).astype(BF16)


def mm3(table, high, low):
    both = mm(table, high)
    return both[:256] + both[256:] + mm(table[:256], low)


def lane_rows(scratch, ref):
    scratch[...] = jnp.zeros_like(scratch)
    scratch[0:SEC_DEV, 0:PIECES] = ref[...].astype(F32)
    return scratch[0:SEC_DEV, :]


def column(row):
    return jnp.broadcast_to(row, (128, 128)).T


SEND_LANES = 1024
SENDS = FLAT // SEND_LANES


def send_kernel(
    owner_hbm, slot_hbm, blend_hbm, raw_hbm, out_hbm,
    owner_ref, slot_ref, blend_ref, raw_ref, lanes, select, blend, slots, warped, out_ref,
    sems, raw_sems, out_sems,
):
    small = [
        pltpu.make_async_copy(source, target, sems.at[i])
        for i, (source, target) in enumerate(
            [(owner_hbm, owner_ref), (slot_hbm, slot_ref), (blend_hbm, blend_ref)]
        )
    ]
    for copy in small:
        copy.start()
    large = [
        pltpu.make_async_copy(
            raw_hbm.at[:, :, pl.ds(i * SEND_LANES, SEND_LANES)], raw_ref.at[i], raw_sems.at[i]
        )
        for i in range(SENDS)
    ]
    for copy in large:
        copy.start()
    for s in range(SEC_DEV):
        for i in range(SENDS):
            warped[i, 128 * s + PIECES : 128 * s + 128, :] = jnp.zeros((32, SEND_LANES), BF16)
    line = lax.broadcasted_iota(jnp.int32, (128, 128), 0)
    lane = lax.broadcasted_iota(jnp.int32, (128, 128), 1)
    rows = lax.broadcasted_iota(jnp.int32, (8 * N_XY, 128), 0)
    rows = (rows // 8) * CHUNK + rows % 8
    for copy in small:
        copy.wait()
    owners = lane_rows(lanes, owner_ref)
    slot_rows = lane_rows(lanes, slot_ref)
    blend_rows = lane_rows(lanes, blend_ref)
    for s in range(SEC_DEV):
        owner = owners[s : s + 1]
        same = jnp.where((column(owner) == owner) & (line < lane), 1.0, 0.0)
        rank = jnp.sum(same, axis=0, keepdims=True)
        target = (owner * CHUNK + rank + float(s * CAP)).astype(jnp.int32)
        target = jnp.where(lane[0:1] < PIECES, target, -1)
        for j in range(PARTS):
            if s - j in (0, 1):
                at = slice(128 * (s - j), 128 * (s - j) + 128)
                select[j, :, at] = jnp.where(rows + 8 * j == target, 1.0, 0.0).astype(BF16)
        at = slice(128 * s, 128 * s + 128)
        blend[at, :] = column(blend_rows[s : s + 1])
        slots[at, :] = (column(slot_rows[s : s + 1]) + float(s * BLOCK + 1)).astype(BF16)

    copies = []

    def send_tiles(first, count):
        at = pl.ds(first, count)
        copies.append(
            pltpu.make_async_copy(out_ref.at[:, at], out_hbm.at[:, at], out_sems.at[len(copies)])
        )
        copies[-1].start()

    for i in range(SENDS):
        large[i].wait()
        for s in range(SEC_DEV):
            at = slice(128 * s, 128 * s + PIECES)
            scale = blend[at, :]
            for lane_at in range(0, SEND_LANES, 128):
                to = slice(lane_at, lane_at + 128)
                warped[i, at, to] = (raw_ref[i, s, :, to].astype(F32) * scale).astype(BF16)
        for j in range(PARTS):
            value = mm(select[j], warped[i, 128 * j : 128 * j + 256, :])
            first = LANE_TILES * j + i * (SEND_LANES // 128)
            for tile in range(SEND_LANES // 128):
                piece = value[:, tile * 128 : tile * 128 + 128].reshape(N_XY, 8, 128)
                out_ref[:, first + tile] = piece.astype(BF16)
            send_tiles(first, SEND_LANES // 128)
    ids = [mm(select[j], slots[128 * j : 128 * j + 256, :]) for j in range(PARTS)]
    lane = lax.broadcasted_iota(jnp.int32, (8 * N_XY, 128), 1)
    ids = jnp.where(lane == 0, ids[0], jnp.where(lane == 1, ids[1], ids[2]))
    out_ref[:, TILES_OUT - 1] = ids.reshape(N_XY, 8, 128).astype(BF16)
    send_tiles(TILES_OUT - 1, 1)
    for copy in copies:
        copy.wait()


def send_rows(owner, slot, blend, raw):
    hbm = pl.BlockSpec(memory_space=pltpu.HBM)
    return pl.pallas_call(
        send_kernel,
        out_shape=jax.ShapeDtypeStruct((N_XY, TILES_OUT, 8, 128), BF16),
        in_specs=[hbm, hbm, hbm, hbm],
        out_specs=hbm,
        scratch_shapes=[
            pltpu.VMEM((SEC_DEV, PIECES), jnp.int32),
            pltpu.VMEM((SEC_DEV, PIECES), jnp.int32),
            pltpu.VMEM((SEC_DEV, PIECES), F32),
            pltpu.VMEM((SENDS, SEC_DEV, PIECES, SEND_LANES), BF16),
            pltpu.VMEM((8, 128), F32),
            pltpu.VMEM((PARTS, 8 * N_XY, 256), BF16),
            pltpu.VMEM((KEYS, 128), F32),
            pltpu.VMEM((KEYS, 128), BF16),
            pltpu.VMEM((SENDS, KEYS, SEND_LANES), BF16),
            pltpu.VMEM((N_XY, TILES_OUT, 8, 128), BF16),
            pltpu.SemaphoreType.DMA((3,)),
            pltpu.SemaphoreType.DMA((SENDS,)),
            pltpu.SemaphoreType.DMA((SENDS * PARTS + 1,)),
        ],
        compiler_params=pltpu.CompilerParams(vmem_limit_bytes=60 * MIB),
    )(owner, slot, blend, raw)


def places(ids, part, count):
    wanted = lax.broadcasted_iota(jnp.int32, (count, 8 * N_XY), 0).astype(F32)
    match = ids[part : part + 1] == wanted + float(part * BLOCK + 1)
    return jnp.where(match, 1.0, 0.0).astype(BF16)


def row_ids(rows_ref):
    return rows_ref[:, TILES_OUT - 1].astype(F32).reshape(8 * N_XY, 128).T


def row_tiles(rows_ref, part, lane, size):
    first = LANE_TILES * part + lane // 128
    return jnp.concatenate(
        [rows_ref[:, first + tile].reshape(8 * N_XY, 128) for tile in range(size // 128)], axis=1
    )


def first_kernel(rows_ref, out_ref, place):
    place[...] = places(row_ids(rows_ref), 0, BLOCK)
    for at in range(0, FLAT, 1024):
        out_ref[:, at : at + 1024] = mm(place[...], row_tiles(rows_ref, 0, at, 1024)).astype(BF16)


def first_section(rows):
    return pl.pallas_call(
        first_kernel,
        out_shape=jax.ShapeDtypeStruct((BLOCK, FLAT), BF16),
        in_specs=[VMEM_SPEC],
        out_specs=VMEM_SPEC,
        scratch_shapes=[pltpu.VMEM((BLOCK, 8 * N_XY), BF16)],
        compiler_params=pltpu.CompilerParams(vmem_limit_bytes=8 * MIB),
        cost_estimate=pl.CostEstimate(flops=1 << 28, bytes_accessed=3 << 20, transcendentals=0),
    )(rows)


GROUP = 4
GROUPS = TILES // GROUP


def spectrum_kernel(rows_ref, first_ref, second_ref, out_ref, place, high, low):
    ids = row_ids(rows_ref)
    for j in range(PARTS):
        place[j] = places(ids, j, 2 * BLOCK)
    wide = 2 * TILE
    for at in range(0, FLAT, wide):
        pieces, before = [], None
        for j in range(PARTS):
            value = mm(place[j], row_tiles(rows_ref, j, at, wide))
            pieces.append(value[:BLOCK] if before is None else before + value[:BLOCK])
            before = value[BLOCK:]
        patches = jnp.concatenate(pieces + [before], axis=0).astype(BF16)
        for i in range(2):
            both = mm(first_ref[...], patches[:, i * TILE : (i + 1) * TILE], NT)
            t = at // TILE + i
            high[t], low[t] = split(both[:256] + both[256:])

    def per_group(group, carry):
        for i in range(GROUP):
            q = group * GROUP + i
            at = pl.ds(pl.multiple_of(16 * q, 16), 16)
            out_ref[q] = mm3(
                second_ref[...],
                high[:, at, :].reshape(256, PATCHES),
                low[:, at, :].reshape(256, PATCHES),
            )
        return carry

    lax.fori_loop(0, GROUPS, per_group, 0)
    out_ref[0, 0:1, :] = jnp.zeros((1, PATCHES), F32)


def spectrum(rows, first, second):
    return pl.pallas_call(
        spectrum_kernel,
        out_shape=jax.ShapeDtypeStruct((TILES, 256, PATCHES), F32),
        in_specs=[VMEM_SPEC] * 3,
        out_specs=VMEM_SPEC,
        scratch_shapes=[
            pltpu.VMEM((PARTS, 2 * BLOCK, 8 * N_XY), BF16),
            pltpu.VMEM((TILES, 256, PATCHES), BF16),
            pltpu.VMEM((TILES, 256, PATCHES), BF16),
        ],
        compiler_params=pltpu.CompilerParams(vmem_limit_bytes=16 * MIB),
        cost_estimate=pl.CostEstimate(
            flops=2 * TILES * 256 * 256 * 8 * 256, bytes_accessed=12 << 20, transcendentals=0
        ),
    )(rows, first, second)


def sublane_sum(value):
    total = value[0:8]
    for row in range(8, value.shape[0], 8):
        total = total + value[row : row + 8]
    return total


def next_spectrum(next_ref, first_ref, second_ref, high, low, follow):
    left = lax.broadcasted_iota(jnp.int32, (16, 128), 1) < BLOCK
    for tg in range(GROUPS):
        rows = jnp.concatenate(
            [
                next_ref[:, (GROUP * tg + i) * TILE : (GROUP * tg + i + 1) * TILE]
                for i in range(GROUP)
            ],
            axis=0,
        )
        both = mm(first_ref[...], rows, NT)
        value = both[:256] + both[256:]
        for half in range(2):
            lanes = value[:, half * 128 : half * 128 + 128]
            rolled = pltpu.roll(lanes, BLOCK, 1)
            for pair in range(TILES // 2):
                g, to = pair // 2, (pair % 2) * 128
                even = slice(32 * pair, 32 * pair + 16)
                odd = slice(32 * pair + 16, 32 * pair + 32)
                for i in range(2):
                    t = GROUP * tg + 2 * half + i
                    if i == 0:
                        packed = jnp.where(left, lanes[even], rolled[odd])
                    else:
                        packed = jnp.where(left, rolled[even], lanes[odd])
                    at = slice(16 * t, 16 * t + 16)
                    up, down = split(packed)
                    high[g, at, to : to + 128] = up
                    low[g, at, to : to + 128] = down
    for g in range(GROUPS):
        follow[g] = mm3(second_ref[...], high[g], low[g])
    follow[0, 0:1, 0:BLOCK] = jnp.zeros((1, BLOCK), F32)


def cross(a, b, first_step):
    def along_y(p, r):
        b_sine, b_cosine = b[r, 1], b[r, 0]
        if first_step is not None:
            b_sine, b_cosine = (
                jnp.where(first_step, 0.0, b_sine),
                jnp.where(first_step, -b_sine, b_cosine),
            )
        return a[p, 0] * b[r, 0] + a[p, 1] * b_sine, a[p, 0] * b_sine - a[p, 1] * b_cosine

    cc, cs, sc, ss = along_y(0, 0), along_y(0, 1), along_y(1, 0), along_y(1, 1)
    head = lax.broadcasted_iota(jnp.int32, cc[0].shape, 0) == 0
    out = {}
    for part in range(2):
        out[0, part] = cc[part] + jnp.where(head, 0.0, ss[part])
        out[1, part] = jnp.where(head, ss[part], cs[part] - sc[part])
    return out


def flow_kernel(
    spec_ref, next_ref, first_ref, second_ref, third_ref, fourth_ref, out_ref,
    next_high, next_low, follow, back_high, back_low, square, next_square, sum_y, sum_x,
):
    lanes = PATCHES
    next_spectrum(next_ref, first_ref, second_ref, next_high, next_low, follow)
    square[...] = jnp.zeros_like(square)
    left = lax.broadcasted_iota(jnp.int32, (256, 128), 1) < BLOCK

    def per_group(step, carry):
        own_total = jnp.zeros((8, lanes), F32)
        for i in range(GROUP):
            own = spec_ref[step * GROUP + i]
            after = follow[step, :, (i // 2) * 128 : (i // 2) * 128 + 128]
            if i % 2 == 0:
                after = pltpu.roll(after, BLOCK, 1)
            low_roll = pltpu.roll(own[:, :128], BLOCK, 1)
            high_roll = pltpu.roll(own[:, 128:], BLOCK, 1)
            other = jnp.concatenate(
                [jnp.where(left, low_roll, high_roll), jnp.where(left, high_roll, after)], axis=1
            )
            own_total = own_total + sublane_sum(own * own)
            pieces = []
            for yk in range(2):
                a, b = (
                    {
                        (x, y): value[yk * 128 + y * 64 + x * 32 : yk * 128 + y * 64 + x * 32 + 32]
                        for x in range(2)
                        for y in range(2)
                    }
                    for value in (own, other)
                )
                out = cross(a, b, step == 0 if i == 0 and yk == 0 else None)
                pieces += [out[0, 0], out[1, 0], out[0, 1], out[1, 1]]
            high, low = split(jnp.concatenate(pieces, axis=0))
            high, low = split(mm3(third_ref[...], high, low))
            back_high[step * GROUP + i] = high
            back_low[step * GROUP + i] = low
        square[...] += own_total
        return carry

    lax.fori_loop(0, GROUPS, per_group, 0)
    after = jnp.zeros((8, lanes), F32)
    for g in range(GROUPS):
        after = after + sublane_sum(follow[g] * follow[g])
    after = after[:, :128] + after[:, 128:]
    after = after + pltpu.roll(after, BLOCK, 1)
    own = square[...]
    low_roll, high_roll = (pltpu.roll(own[:, i : i + 128], BLOCK, 1) for i in (0, 128))
    left = lax.broadcasted_iota(jnp.int32, (8, 128), 1) < BLOCK
    next_square[...] = jnp.concatenate(
        [jnp.where(left, low_roll, high_roll), jnp.where(left, high_roll, after)], axis=1
    )
    finish(fourth_ref, out_ref, back_high, back_low, square, next_square, sum_y, sum_x)


def finish(fourth_ref, out_ref, back_high, back_low, square, next_square, sum_y, sum_x):
    lanes = PATCHES
    sum_y[...] = jnp.zeros_like(sum_y)
    sum_x[...] = jnp.zeros_like(sum_x)

    def per_group(group, carry):
        all_d0 = jnp.zeros((64, lanes), F32)
        weighted = jnp.zeros((8, lanes), F32)
        for i in range(GROUP):
            g = group * GROUP + i
            rows = pl.ds(pl.multiple_of(g * 16, 16), 16)
            corr = mm3(
                fourth_ref[...],
                back_high[:, rows, :].reshape(256, lanes),
                back_low[:, rows, :].reshape(256, lanes),
            )
            power = corr * corr
            for d in range(4):
                block = power[d * 64 : d * 64 + 64]
                all_d0 = all_d0 + block
                index = g * 4 + d
                shift = jnp.where(index < 32, index, index - 64).astype(F32)
                weighted = weighted + sublane_sum(block) * shift
        sum_y[...] += all_d0
        sum_x[...] += weighted
        return carry

    lax.fori_loop(0, GROUPS, per_group, 0)

    def down(value):
        return jnp.sum(value, axis=0, keepdims=True)

    index = lax.broadcasted_iota(jnp.int32, (64, lanes), 0)
    shift = jnp.where(index < 32, index, index - 64).astype(F32)
    total = down(sum_y[...])
    along_x = down(sum_x[...])
    along_y = down(sum_y[...] * shift)
    norm = (down(square[...]) * (1.0 / FLAT) + 1e-05) * (
        down(next_square[...]) * (1.0 / FLAT) + 1e-05
    )
    factor = (1.0 / (float(FLAT) * float(FLAT))) / norm
    total = jnp.maximum(total * factor, 0.5)
    tile_rows = []
    for value in (along_x * factor / total, along_y * factor / total):
        for half in range(2):
            lane_tile = value[:, half * 128 : half * 128 + 128]
            tile_rows += [lane_tile, pltpu.roll(lane_tile, 64, 1)]
    grid = jnp.concatenate(tile_rows, axis=0)
    lane = lax.broadcasted_iota(jnp.int32, (8, 128), 1)
    for j in range(N_SEC):
        upper = pltpu.roll(grid, (8 - 8 * j) % 128, 1)
        lower = pltpu.roll(grid, (128 - 8 * j) % 128, 1)
        gy = jnp.where(lane < GYW, lane, lane - GYW) + (8 * j - 8)
        window = jnp.where(lane < GYW, upper, lower)
        window = jnp.where((lane < 2 * GYW) & (gy >= 0) & (gy < 32), window, 0.0)
        packed = window[0:4] + pltpu.roll(window, 64, 1)[4:8]
        for b in range(N_XY):
            out_ref[j * N_XY + b] = packed


def flow_windows(spec, following, tabs):
    return pl.pallas_call(
        flow_kernel,
        out_shape=jax.ShapeDtypeStruct((N_SEC * N_XY, 4, 128), F32),
        in_specs=[VMEM_SPEC] * 6,
        out_specs=VMEM_SPEC,
        scratch_shapes=[
            pltpu.VMEM((GROUPS, 256, 256), BF16),
            pltpu.VMEM((GROUPS, 256, 256), BF16),
            pltpu.VMEM((GROUPS, 256, 256), F32),
            pltpu.VMEM((TILES, 256, PATCHES), BF16),
            pltpu.VMEM((TILES, 256, PATCHES), BF16),
            pltpu.VMEM((8, PATCHES), F32),
            pltpu.VMEM((8, PATCHES), F32),
            pltpu.VMEM((64, PATCHES), F32),
            pltpu.VMEM((8, PATCHES), F32),
        ],
        compiler_params=pltpu.CompilerParams(vmem_limit_bytes=24 * MIB),
        cost_estimate=pl.CostEstimate(
            flops=2 * TILES * 256 * 256 * 8 * 256, bytes_accessed=8 << 20, transcendentals=0
        ),
    )(spec, following, *tabs)


def relax_kernel(place_ref, arrived_ref, out_ref):
    column, block = place_ref[0], place_ref[1]
    lane = lax.broadcasted_iota(jnp.int32, (8, 128), 1)
    lane = jnp.where(lane < 64, lane, lane - 64)
    top = lane < GYW
    gy = jnp.where(top, lane, lane - GYW) + (8 * column - 8)
    inside = (lane < 2 * GYW) & (gy >= 0) & (gy < 32)
    mask = {}
    for o in range(-4, 5):
        valid = (block + o >= 0) & (block + o < N_XY)
        mask[o] = jnp.where(inside & valid, 0.2, 0.0)
    zero = jnp.zeros((8, 128), F32)
    result = []
    for s in range(0, N_SEC, 2):
        flow, mesh = {}, {}
        for o in range(-4, 5):
            at = jnp.clip(block + o, 0, N_XY - 1)
            value = jnp.concatenate(
                [arrived_ref[s * N_XY + at], arrived_ref[(s + 1) * N_XY + at]], axis=0
            )
            flow[o] = value * mask[o]
            mesh[o] = jnp.where(mask[o] > 0.0, value, 0.0)
        for step in range(ITERS):
            reach = (ITERS - step) // 2
            up = {o: pltpu.roll(mesh[o], 128 - GYW, 1) for o in mesh}
            down = {o: pltpu.roll(mesh[o], GYW, 1) for o in mesh}
            new = {}
            for o in range(-reach, reach + 1):
                near = jnp.where(
                    top, up[o] + up.get(o - 1, zero), down[o] + down.get(o + 1, zero)
                )
                near = near + pltpu.roll(mesh[o], 1, 1) + pltpu.roll(mesh[o], 127, 1)
                new[o] = flow[o] + mask[o] * near
            mesh = new
        result.append(mesh[0])
    turned = jnp.concatenate(result + [jnp.zeros((112, 128), F32)], axis=0).T
    for c in range(2):
        for i in range(2):
            at = 64 * c + GYW * i + 8
            out_ref[c, i] = turned[at : at + 8, :15]


def relax(place, arrived):
    return pl.pallas_call(
        relax_kernel,
        out_shape=jax.ShapeDtypeStruct((2, 2, 8, 15), F32),
        in_specs=[
            pl.BlockSpec(memory_space=pltpu.SMEM),
            pl.BlockSpec(memory_space=pltpu.VMEM),
        ],
        out_specs=pl.BlockSpec(memory_space=pltpu.VMEM),
        compiler_params=pltpu.CompilerParams(vmem_limit_bytes=8 * MIB),
    )(place, arrived)


def local(raw_pieces, piece_owner, piece_slot, blend):
    tabs = [jnp.asarray(t) for t in tables()]
    outgoing = send_rows(piece_owner[:, :, 0], piece_slot, blend, raw_pieces)
    arrived = lax.all_to_all(outgoing, "xy", split_axis=0, concat_axis=0, tiled=True)
    first = first_section(arrived)
    back = [(i + 1, i) for i in range(N_SEC - 1)]
    following = lax.ppermute(first, "sec", back)
    spec = spectrum(arrived, tabs[0], tabs[1])
    windows = flow_windows(spec, following, tabs)
    got = lax.all_to_all(windows, ("sec", "xy"), split_axis=0, concat_axis=0, tiled=True)
    place = jnp.stack([lax.axis_index("sec"), lax.axis_index("xy")]).astype(jnp.int32)
    return relax(place, got).transpose(3, 0, 1, 2)


def solution(mesh):
    in_specs = (P("sec", "xy", None), P("sec", "xy", None), P("sec", "xy"), P("sec", "xy"))
    out_specs = P(None, None, "xy", "sec")
    return jax.shard_map(local, mesh=mesh, in_specs=in_specs, out_specs=out_specs, check_vma=False)
```

```python
import math

import jax
import jax.numpy as jnp
import numpy as np
from jax import lax
from jax.experimental import pallas as pl
from jax.experimental.pallas import tpu as pltpu
from jax.sharding import PartitionSpec as P

PS = 64
FLAT = PS * PS
CAP = 6
N_SEC = 4
N_XY = 32
SEC_DEV = 4
PIECES = 96
BLOCK = 64
ITERS = 8
KEYS = SEC_DEV * 128
CHUNK = SEC_DEV * CAP
LANE_TILES = FLAT // 128
PARTS = CHUNK // 8
TILES_OUT = PARTS * LANE_TILES + 1
PATCHES = SEC_DEV * BLOCK
TILE = 256
TILES = FLAT // TILE
GYW = 24
F32 = jnp.float32
BF16 = jnp.bfloat16
MIB = 1024 * 1024

VMEM_SPEC = pl.BlockSpec(memory_space=pltpu.VMEM)
NT = (((1,), (1,)), ((), ()))
NN = (((1,), (0,)), ((), ()))


def real_basis(kind):
    pos = np.arange(PS)
    rows = {}
    for k in range(32):
        angle = 2.0 * math.pi * ((k * pos) % PS) / PS
        rows[k, 0] = np.cos(angle)
        rows[k, 1] = np.sin(angle) if k else np.cos(math.pi * pos)
    if kind == "forward":
        for (k, part), row in rows.items():
            rows[k, part] = row * (math.sqrt(2.0) if k else 1.0) / 8.0
    x_order = np.stack([rows[k, part] for part in range(2) for k in range(32)])
    y_order = np.stack([rows[k, part] for k in range(32) for part in range(2)])
    return x_order, y_order


def split_table(table):
    high = table.astype(jnp.bfloat16)
    low = (table - high.astype(np.float64)).astype(jnp.bfloat16)
    return np.concatenate([high, low], axis=0)


def tables():
    fwd_x, fwd_y = real_basis("forward")
    inv_x, inv_y = real_basis("inverse")
    eye = np.eye(4)
    first = np.einsum("ab,ky->kaby", eye, fwd_y).reshape(256, 256)
    second = np.einsum("ab,ktx->aktbx", eye, fwd_x.reshape(64, 16, 4)).reshape(256, 256)
    third = np.einsum("ab,kd->dabk", eye, inv_x).reshape(256, 256)
    fourth = np.einsum("ab,qkd->adqbk", eye, inv_y.reshape(16, 4, 64)).reshape(256, 256)
    return [split_table(t) for t in (first, second, third, fourth)]


def mm(a, b, dims=NN):
    return lax.dot_general(a, b, dims, preferred_element_type=F32)


def split(value):
    high = value.astype(BF16)
    return high, (value - high.astype(F32)).astype(BF16)


def mm3(table, high, low):
    both = mm(table, high)
    return both[:256] + both[256:] + mm(table[:256], low)


def lane_rows(scratch, ref):
    scratch[...] = jnp.zeros_like(scratch)
    scratch[0:SEC_DEV, 0:PIECES] = ref[...].astype(F32)
    return scratch[0:SEC_DEV, :]


def column(row):
    return jnp.broadcast_to(row, (128, 128)).T


SEND_LANES = 1024
SENDS = FLAT // SEND_LANES


def send_kernel(
    owner_hbm, slot_hbm, blend_hbm, raw_hbm, out_hbm,
    owner_ref, slot_ref, blend_ref, raw_ref, lanes, select, blend, slots, warped, out_ref,
    sems, raw_sems, out_sems,
):
    small = [
        pltpu.make_async_copy(source, target, sems.at[i])
        for i, (source, target) in enumerate(
            [(owner_hbm, owner_ref), (slot_hbm, slot_ref), (blend_hbm, blend_ref)]
        )
    ]
    for copy in small:
        copy.start()
    large = [
        pltpu.make_async_copy(
            raw_hbm.at[:, :, pl.ds(i * SEND_LANES, SEND_LANES)], raw_ref.at[i], raw_sems.at[i]
        )
        for i in range(SENDS)
    ]
    for copy in large:
        copy.start()
    for s in range(SEC_DEV):
        for i in range(SENDS):
            warped[i, 128 * s + PIECES : 128 * s + 128, :] = jnp.zeros((32, SEND_LANES), BF16)
    line = lax.broadcasted_iota(jnp.int32, (128, 128), 0)
    lane = lax.broadcasted_iota(jnp.int32, (128, 128), 1)
    rows = lax.broadcasted_iota(jnp.int32, (8 * N_XY, 128), 0)
    rows = (rows // 8) * CHUNK + rows % 8
    for copy in small:
        copy.wait()
    owners = lane_rows(lanes, owner_ref)
    slot_rows = lane_rows(lanes, slot_ref)
    blend_rows = lane_rows(lanes, blend_ref)
    for s in range(SEC_DEV):
        owner = owners[s : s + 1]
        same = jnp.where((column(owner) == owner) & (line < lane), 1.0, 0.0)
        rank = jnp.sum(same, axis=0, keepdims=True)
        target = (owner * CHUNK + rank + float(s * CAP)).astype(jnp.int32)
        target = jnp.where(lane[0:1] < PIECES, target, -1)
        for j in range(PARTS):
            if s - j in (0, 1):
                at = slice(128 * (s - j), 128 * (s - j) + 128)
                select[j, :, at] = jnp.where(rows + 8 * j == target, 1.0, 0.0).astype(BF16)
        at = slice(128 * s, 128 * s + 128)
        blend[at, :] = column(blend_rows[s : s + 1])
        slots[at, :] = (column(slot_rows[s : s + 1]) + float(s * BLOCK + 1)).astype(BF16)

    copies = []

    def send_tiles(first, count):
        at = pl.ds(first, count)
        copies.append(
            pltpu.make_async_copy(out_ref.at[:, at], out_hbm.at[:, at], out_sems.at[len(copies)])
        )
        copies[-1].start()

    for i in range(SENDS):
        large[i].wait()
        for s in range(SEC_DEV):
            at = slice(128 * s, 128 * s + PIECES)
            scale = blend[at, :]
            for lane_at in range(0, SEND_LANES, 128):
                to = slice(lane_at, lane_at + 128)
                warped[i, at, to] = (raw_ref[i, s, :, to].astype(F32) * scale).astype(BF16)
        for j in range(PARTS):
            value = mm(select[j], warped[i, 128 * j : 128 * j + 256, :])
            first = LANE_TILES * j + i * (SEND_LANES // 128)
            for tile in range(SEND_LANES // 128):
                piece = value[:, tile * 128 : tile * 128 + 128].reshape(N_XY, 8, 128)
                out_ref[:, first + tile] = piece.astype(BF16)
            send_tiles(first, SEND_LANES // 128)
    ids = [mm(select[j], slots[128 * j : 128 * j + 256, :]) for j in range(PARTS)]
    lane = lax.broadcasted_iota(jnp.int32, (8 * N_XY, 128), 1)
    ids = jnp.where(lane == 0, ids[0], jnp.where(lane == 1, ids[1], ids[2]))
    out_ref[:, TILES_OUT - 1] = ids.reshape(N_XY, 8, 128).astype(BF16)
    send_tiles(TILES_OUT - 1, 1)
    for copy in copies:
        copy.wait()


def send_rows(owner, slot, blend, raw):
    hbm = pl.BlockSpec(memory_space=pltpu.HBM)
    return pl.pallas_call(
        send_kernel,
        out_shape=jax.ShapeDtypeStruct((N_XY, TILES_OUT, 8, 128), BF16),
        in_specs=[hbm, hbm, hbm, hbm],
        out_specs=hbm,
        scratch_shapes=[
            pltpu.VMEM((SEC_DEV, PIECES), jnp.int32),
            pltpu.VMEM((SEC_DEV, PIECES), jnp.int32),
            pltpu.VMEM((SEC_DEV, PIECES), F32),
            pltpu.VMEM((SENDS, SEC_DEV, PIECES, SEND_LANES), BF16),
            pltpu.VMEM((8, 128), F32),
            pltpu.VMEM((PARTS, 8 * N_XY, 256), BF16),
            pltpu.VMEM((KEYS, 128), F32),
            pltpu.VMEM((KEYS, 128), BF16),
            pltpu.VMEM((SENDS, KEYS, SEND_LANES), BF16),
            pltpu.VMEM((N_XY, TILES_OUT, 8, 128), BF16),
            pltpu.SemaphoreType.DMA((3,)),
            pltpu.SemaphoreType.DMA((SENDS,)),
            pltpu.SemaphoreType.DMA((SENDS * PARTS + 1,)),
        ],
        compiler_params=pltpu.CompilerParams(vmem_limit_bytes=60 * MIB),
    )(owner, slot, blend, raw)


def places(ids, part, count):
    wanted = lax.broadcasted_iota(jnp.int32, (count, 8 * N_XY), 0).astype(F32)
    match = ids[part : part + 1] == wanted + float(part * BLOCK + 1)
    return jnp.where(match, 1.0, 0.0).astype(BF16)


def row_ids(rows_ref):
    return rows_ref[:, TILES_OUT - 1].astype(F32).reshape(8 * N_XY, 128).T


def row_tiles(rows_ref, part, lane, size):
    first = LANE_TILES * part + lane // 128
    return jnp.concatenate(
        [rows_ref[:, first + tile].reshape(8 * N_XY, 128) for tile in range(size // 128)], axis=1
    )


def first_kernel(rows_ref, out_ref, place):
    place[...] = places(row_ids(rows_ref), 0, BLOCK)
    for at in range(0, FLAT, 1024):
        out_ref[:, at : at + 1024] = mm(place[...], row_tiles(rows_ref, 0, at, 1024)).astype(BF16)


def first_section(rows):
    return pl.pallas_call(
        first_kernel,
        out_shape=jax.ShapeDtypeStruct((BLOCK, FLAT), BF16),
        in_specs=[VMEM_SPEC],
        out_specs=VMEM_SPEC,
        scratch_shapes=[pltpu.VMEM((BLOCK, 8 * N_XY), BF16)],
        compiler_params=pltpu.CompilerParams(vmem_limit_bytes=8 * MIB),
        cost_estimate=pl.CostEstimate(flops=1 << 28, bytes_accessed=3 << 20, transcendentals=0),
    )(rows)


GROUP = 4
GROUPS = TILES // GROUP


def sublane_sum(value):
    total = value[0:8]
    for row in range(8, value.shape[0], 8):
        total = total + value[row : row + 8]
    return total


def cross(a, b, first_step):
    def along_y(p, r):
        b_sine, b_cosine = b[r, 1], b[r, 0]
        if first_step is not None:
            b_sine, b_cosine = (
                jnp.zeros_like(b_sine) if first_step else b_sine,
                -b_sine if first_step else b_cosine,
            )
        return a[p, 0] * b[r, 0] + a[p, 1] * b_sine, a[p, 0] * b_sine - a[p, 1] * b_cosine

    cc, cs, sc, ss = along_y(0, 0), along_y(0, 1), along_y(1, 0), along_y(1, 1)
    head = lax.broadcasted_iota(jnp.int32, cc[0].shape, 0) == 0
    out = {}
    for part in range(2):
        out[0, part] = cc[part] + jnp.where(head, 0.0, ss[part])
        out[1, part] = jnp.where(head, ss[part], cs[part] - sc[part])
    return out


def cross_rows(own, other, first_step):
    pieces = []
    for yk in range(2):
        a, b = (
            {
                (x, y): value[yk * 128 + y * 64 + x * 32 : yk * 128 + y * 64 + x * 32 + 32]
                for x in range(2)
                for y in range(2)
            }
            for value in (own, other)
        )
        out = cross(a, b, first_step if yk == 0 else None)
        pieces += [out[0, 0], out[1, 0], out[0, 1], out[1, 1]]
    return split(jnp.concatenate(pieces, axis=0))


def signed(index):
    return float((index + 32) % 64 - 32)


def down(value):
    return jnp.sum(value, axis=0, keepdims=True)


def flow_sums(operands, third_ref, fourth_ref, back_high, back_low, sums_ref):
    lanes = 128
    for q in range(0, TILES, 2):
        rows = [cross_rows(*operands(q + i), q + i == 0) for i in range(2)]
        high, low = (jnp.concatenate([rows[0][i], rows[1][i]], axis=1) for i in range(2))
        high, low = split(mm3(third_ref[...], high, low))
        for i in range(2):
            back_high[q + i] = high[:, i * lanes : (i + 1) * lanes]
            back_low[q + i] = low[:, i * lanes : (i + 1) * lanes]
    all_d0 = jnp.zeros((64, lanes), F32)
    weighted = jnp.zeros((8, lanes), F32)
    for g in range(0, TILES, 2):
        high, low = (
            jnp.concatenate(
                [ref[:, 16 * (g + i) : 16 * (g + i) + 16, :].reshape(256, lanes) for i in range(2)],
                axis=1,
            )
            for ref in (back_high, back_low)
        )
        corr = mm3(fourth_ref[...], high, low)
        power = corr * corr
        for i in range(2):
            for d in range(4):
                block = power[d * 64 : d * 64 + 64, i * lanes : (i + 1) * lanes]
                all_d0 = all_d0 + block
                weighted = weighted + sublane_sum(block) * signed((g + i) * 4 + d)
    index = lax.broadcasted_iota(jnp.int32, (64, lanes), 0)
    shift = jnp.where(index < 32, index, index - 64).astype(F32)
    sums_ref[0:1, :] = down(all_d0)
    sums_ref[1:2, :] = down(weighted)
    sums_ref[2:3, :] = down(all_d0 * shift)


def spectrum_kernel(
    rows_ref, first_ref, second_ref, third_ref, fourth_ref, own_ref, square_ref, sums_ref,
    place, high, low, own_first, back_high, back_low,
):
    ids = row_ids(rows_ref)
    for j in range(PARTS):
        place[j] = places(ids, j, 2 * BLOCK)
    wide = 2 * TILE
    for at in range(0, FLAT, wide):
        pieces, before = [], None
        for j in range(PARTS):
            value = mm(place[j], row_tiles(rows_ref, j, at, wide))
            pieces.append(value[:BLOCK] if before is None else before + value[:BLOCK])
            before = value[BLOCK:]
        patches = jnp.concatenate(pieces + [before], axis=0).astype(BF16)
        for i in range(2):
            both = mm(first_ref[...], patches[:, i * TILE : (i + 1) * TILE], NT)
            t = at // TILE + i
            high[t], low[t] = split(both[:256] + both[256:])

    square = jnp.zeros((8, PATCHES), F32)
    for q in range(TILES):
        at = slice(16 * q, 16 * q + 16)
        own = mm3(
            second_ref[...],
            high[:, at, :].reshape(256, PATCHES),
            low[:, at, :].reshape(256, PATCHES),
        )
        if q == 0:
            own = jnp.where(lax.broadcasted_iota(jnp.int32, (256, 1), 0) == 0, 0.0, own)
        square = square + sublane_sum(own * own)
        own_first[q] = own[:, :128]
        own_ref[q] = own[:, 128:]
    square_ref[...] = square
    left = lax.broadcasted_iota(jnp.int32, (256, 128), 1) < BLOCK

    def operands(q):
        own, after = own_first[q], own_ref[q]
        return own, jnp.where(left, pltpu.roll(own, BLOCK, 1), pltpu.roll(after, BLOCK, 1))

    flow_sums(operands, third_ref, fourth_ref, back_high, back_low, sums_ref)


def spectrum(rows, tabs):
    return pl.pallas_call(
        spectrum_kernel,
        out_shape=[
            jax.ShapeDtypeStruct((TILES, 256, 128), F32),
            jax.ShapeDtypeStruct((8, PATCHES), F32),
            jax.ShapeDtypeStruct((8, 128), F32),
        ],
        in_specs=[VMEM_SPEC] * 5,
        out_specs=[VMEM_SPEC] * 3,
        scratch_shapes=[
            pltpu.VMEM((PARTS, 2 * BLOCK, 8 * N_XY), BF16),
            pltpu.VMEM((TILES, 256, PATCHES), BF16),
            pltpu.VMEM((TILES, 256, PATCHES), BF16),
            pltpu.VMEM((TILES, 256, 128), F32),
            pltpu.VMEM((TILES, 256, 128), BF16),
            pltpu.VMEM((TILES, 256, 128), BF16),
        ],
        compiler_params=pltpu.CompilerParams(vmem_limit_bytes=20 * MIB),
        cost_estimate=pl.CostEstimate(
            flops=2 * TILES * 256 * 256 * 11 * 256, bytes_accessed=12 << 20, transcendentals=0
        ),
    )(rows, *tabs)


def next_spectrum(next_ref, first_ref, second_ref, high, low, follow):
    left = lax.broadcasted_iota(jnp.int32, (16, 128), 1) < BLOCK
    for tg in range(GROUPS):
        rows = jnp.concatenate(
            [
                next_ref[:, (GROUP * tg + i) * TILE : (GROUP * tg + i + 1) * TILE]
                for i in range(GROUP)
            ],
            axis=0,
        )
        both = mm(first_ref[...], rows, NT)
        value = both[:256] + both[256:]
        for half in range(2):
            lanes = value[:, half * 128 : half * 128 + 128]
            rolled = pltpu.roll(lanes, BLOCK, 1)
            for pair in range(TILES // 2):
                g, to = pair // 2, (pair % 2) * 128
                even = slice(32 * pair, 32 * pair + 16)
                odd = slice(32 * pair + 16, 32 * pair + 32)
                for i in range(2):
                    t = GROUP * tg + 2 * half + i
                    if i == 0:
                        packed = jnp.where(left, lanes[even], rolled[odd])
                    else:
                        packed = jnp.where(left, rolled[even], lanes[odd])
                    at = slice(16 * t, 16 * t + 16)
                    up, down = split(packed)
                    high[g, at, to : to + 128] = up
                    low[g, at, to : to + 128] = down
    for g in range(GROUPS):
        follow[g] = mm3(second_ref[...], high[g], low[g])
    follow[0, 0:1, 0:BLOCK] = jnp.zeros((1, BLOCK), F32)


def flow_kernel(
    own_ref, square_ref, early_ref, next_ref, first_ref, second_ref, third_ref, fourth_ref, out_ref,
    next_high, next_low, follow, back_high, back_low, late,
):
    next_spectrum(next_ref, first_ref, second_ref, next_high, next_low, follow)
    left = lax.broadcasted_iota(jnp.int32, (256, 128), 1) < BLOCK

    def operands(q):
        i = q % GROUP
        own = own_ref[q]
        after = follow[q // GROUP, :, (i // 2) * 128 : (i // 2) * 128 + 128]
        if i % 2 == 0:
            after = pltpu.roll(after, BLOCK, 1)
        return own, jnp.where(left, pltpu.roll(own, BLOCK, 1), after)

    flow_sums(operands, third_ref, fourth_ref, back_high, back_low, late)
    after = jnp.zeros((8, 256), F32)
    for g in range(GROUPS):
        after = after + sublane_sum(follow[g] * follow[g])
    after = after[:, :128] + after[:, 128:]
    after = after + pltpu.roll(after, BLOCK, 1)
    own = square_ref[...]
    low_roll, high_roll = (pltpu.roll(own[:, i : i + 128], BLOCK, 1) for i in (0, 128))
    left = lax.broadcasted_iota(jnp.int32, (8, 128), 1) < BLOCK
    other = jnp.concatenate(
        [jnp.where(left, low_roll, high_roll), jnp.where(left, high_roll, after)], axis=1
    )
    total, along_x, along_y = (
        jnp.concatenate([early_ref[i : i + 1, :], late[i : i + 1, :]], axis=1) for i in range(3)
    )
    norm = (down(own) * (1.0 / FLAT) + 1e-05) * (down(other) * (1.0 / FLAT) + 1e-05)
    factor = (1.0 / (float(FLAT) * float(FLAT))) / norm
    total = jnp.maximum(total * factor, 0.5)
    tile_rows = []
    for value in (along_x * factor / total, along_y * factor / total):
        for half in range(2):
            lane_tile = value[:, half * 128 : half * 128 + 128]
            tile_rows += [lane_tile, pltpu.roll(lane_tile, 64, 1)]
    grid = jnp.concatenate(tile_rows, axis=0)
    lane = lax.broadcasted_iota(jnp.int32, (8, 128), 1)
    for j in range(N_SEC):
        upper = pltpu.roll(grid, (8 - 8 * j) % 128, 1)
        lower = pltpu.roll(grid, (128 - 8 * j) % 128, 1)
        gy = jnp.where(lane < GYW, lane, lane - GYW) + (8 * j - 8)
        window = jnp.where(lane < GYW, upper, lower)
        window = jnp.where((lane < 2 * GYW) & (gy >= 0) & (gy < 32), window, 0.0)
        packed = window[0:4] + pltpu.roll(window, 64, 1)[4:8]
        for b in range(N_XY):
            out_ref[j * N_XY + b] = packed


def flow_windows(own, square, early, following, tabs):
    return pl.pallas_call(
        flow_kernel,
        out_shape=jax.ShapeDtypeStruct((N_SEC * N_XY, 4, 128), F32),
        in_specs=[VMEM_SPEC] * 8,
        out_specs=VMEM_SPEC,
        scratch_shapes=[
            pltpu.VMEM((GROUPS, 256, 256), BF16),
            pltpu.VMEM((GROUPS, 256, 256), BF16),
            pltpu.VMEM((GROUPS, 256, 256), F32),
            pltpu.VMEM((TILES, 256, 128), BF16),
            pltpu.VMEM((TILES, 256, 128), BF16),
            pltpu.VMEM((8, 128), F32),
        ],
        compiler_params=pltpu.CompilerParams(vmem_limit_bytes=24 * MIB),
        cost_estimate=pl.CostEstimate(
            flops=2 * TILES * 256 * 256 * 8 * 256, bytes_accessed=8 << 20, transcendentals=0
        ),
    )(own, square, early, following, *tabs)


def relax_kernel(place_ref, arrived_ref, out_ref):
    column, block = place_ref[0], place_ref[1]
    lane = lax.broadcasted_iota(jnp.int32, (8, 128), 1)
    lane = jnp.where(lane < 64, lane, lane - 64)
    top = lane < GYW
    gy = jnp.where(top, lane, lane - GYW) + (8 * column - 8)
    inside = (lane < 2 * GYW) & (gy >= 0) & (gy < 32)
    mask = {}
    for o in range(-4, 5):
        valid = (block + o >= 0) & (block + o < N_XY)
        mask[o] = jnp.where(inside & valid, 0.2, 0.0)
    zero = jnp.zeros((8, 128), F32)
    result = []
    for s in range(0, N_SEC, 2):
        flow, mesh = {}, {}
        for o in range(-4, 5):
            at = jnp.clip(block + o, 0, N_XY - 1)
            value = jnp.concatenate(
                [arrived_ref[s * N_XY + at], arrived_ref[(s + 1) * N_XY + at]], axis=0
            )
            flow[o] = value * mask[o]
            mesh[o] = jnp.where(mask[o] > 0.0, value, 0.0)
        for step in range(ITERS):
            reach = (ITERS - step) // 2
            up = {o: pltpu.roll(mesh[o], 128 - GYW, 1) for o in mesh}
            down = {o: pltpu.roll(mesh[o], GYW, 1) for o in mesh}
            new = {}
            for o in range(-reach, reach + 1):
                near = jnp.where(
                    top, up[o] + up.get(o - 1, zero), down[o] + down.get(o + 1, zero)
                )
                near = near + pltpu.roll(mesh[o], 1, 1) + pltpu.roll(mesh[o], 127, 1)
                new[o] = flow[o] + mask[o] * near
            mesh = new
        result.append(mesh[0])
    turned = jnp.concatenate(result + [jnp.zeros((112, 128), F32)], axis=0).T
    for c in range(2):
        for i in range(2):
            at = 64 * c + GYW * i + 8
            out_ref[c, i] = turned[at : at + 8, :15]


def relax(place, arrived):
    return pl.pallas_call(
        relax_kernel,
        out_shape=jax.ShapeDtypeStruct((2, 2, 8, 15), F32),
        in_specs=[
            pl.BlockSpec(memory_space=pltpu.SMEM),
            pl.BlockSpec(memory_space=pltpu.VMEM),
        ],
        out_specs=pl.BlockSpec(memory_space=pltpu.VMEM),
        compiler_params=pltpu.CompilerParams(vmem_limit_bytes=8 * MIB),
    )(place, arrived)


def local(raw_pieces, piece_owner, piece_slot, blend):
    tabs = [jnp.asarray(t) for t in tables()]
    outgoing = send_rows(piece_owner[:, :, 0], piece_slot, blend, raw_pieces)
    arrived = lax.all_to_all(outgoing, "xy", split_axis=0, concat_axis=0, tiled=True)
    first = first_section(arrived)
    back = [(i + 1, i) for i in range(N_SEC - 1)]
    following = lax.ppermute(first, "sec", back)
    own, square, early = spectrum(arrived, tabs)
    windows = flow_windows(own, square, early, following, tabs)
    got = lax.all_to_all(windows, ("sec", "xy"), split_axis=0, concat_axis=0, tiled=True)
    place = jnp.stack([lax.axis_index("sec"), lax.axis_index("xy")]).astype(jnp.int32)
    return relax(place, got).transpose(3, 0, 1, 2)


def solution(mesh):
    in_specs = (P("sec", "xy", None), P("sec", "xy", None), P("sec", "xy"), P("sec", "xy"))
    out_specs = P(None, None, "xy", "sec")
    return jax.shard_map(local, mesh=mesh, in_specs=in_specs, out_specs=out_specs, check_vma=False)
```

```python
import math

import jax
import jax.numpy as jnp
import numpy as np
from jax import lax
from jax.experimental import pallas as pl
from jax.experimental.pallas import tpu as pltpu
from jax.sharding import PartitionSpec as P

PS = 64
FLAT = PS * PS
CAP = 6
N_SEC = 4
N_XY = 32
SEC_DEV = 4
PIECES = 96
BLOCK = 64
ITERS = 8
KEYS = SEC_DEV * 128
CHUNK = SEC_DEV * CAP
LANE_TILES = FLAT // 128
PARTS = CHUNK // 8
TILES_OUT = PARTS * LANE_TILES + 1
PATCHES = SEC_DEV * BLOCK
TILE = 256
TILES = FLAT // TILE
GYW = 24
F32 = jnp.float32
BF16 = jnp.bfloat16
MIB = 1024 * 1024

VMEM_SPEC = pl.BlockSpec(memory_space=pltpu.VMEM)
NT = (((1,), (1,)), ((), ()))
NN = (((1,), (0,)), ((), ()))


def real_basis():
    pos = np.arange(PS)
    rows = np.zeros((2, 32, PS))
    for k in range(32):
        angle = 2.0 * math.pi * ((k * pos) % PS) / PS
        rows[0, k] = np.cos(angle)
        rows[1, k] = np.sin(angle) if k else np.cos(math.pi * pos)
        rows[:, k] *= (math.sqrt(2.0) if k else 1.0) / 8.0
    return rows


def split_table(table):
    high = table.astype(jnp.bfloat16)
    low = (table - high.astype(np.float64)).astype(jnp.bfloat16)
    return np.concatenate([high, low], axis=0)


def tables():
    basis = real_basis()
    by_x = basis.reshape(2, 8, 4, PS)
    by_y = basis.reshape(2, 16, 2, PS)
    two, four = np.eye(2), np.eye(4)
    first = np.einsum("ab,pqky->qpkaby", four, by_y).reshape(256, 256)
    second = np.einsum("pu,kv,cgitb->cgpkituvb", two, two, by_x.reshape(2, 8, 4, 16, 4))
    second = second.reshape(256, 256)
    shift = (np.arange(PS) + 32) % PS - 32
    weigh = np.einsum("pkd,d,rld->pkrl", basis, shift, basis)
    third = np.einsum("pu,kv,cgidhj->cgpkidhuvj", two, two, weigh.reshape(2, 8, 4, 2, 8, 4))
    third = third.reshape(256, 256)
    fourth = np.einsum("ij,pqkurv->qpkiruvj", four, weigh.reshape(2, 16, 2, 2, 16, 2))
    fourth = fourth.reshape(256, 256)
    return [split_table(t) for t in (first, second, third, fourth)]


def mm(a, b, dims=NN):
    return lax.dot_general(a, b, dims, preferred_element_type=F32)


def split(value):
    high = value.astype(BF16)
    return high, (value - high.astype(F32)).astype(BF16)


def mm3(table, high, low):
    both = mm(table, high)
    return both[:256] + both[256:] + mm(table[:256], low)


def lane_rows(scratch, ref):
    scratch[...] = jnp.zeros_like(scratch)
    scratch[0:SEC_DEV, 0:PIECES] = ref[...].astype(F32)
    return scratch[0:SEC_DEV, :]


def column(row):
    return jnp.broadcast_to(row, (128, 128)).T


SEND_LANES = 1024
SENDS = FLAT // SEND_LANES


def send_kernel(
    owner_hbm, slot_hbm, blend_hbm, raw_hbm, out_hbm,
    owner_ref, slot_ref, blend_ref, raw_ref, lanes, select, blend, slots, warped, out_ref,
    sems, raw_sems, out_sems,
):
    small = [
        pltpu.make_async_copy(source, target, sems.at[i])
        for i, (source, target) in enumerate(
            [(owner_hbm, owner_ref), (slot_hbm, slot_ref), (blend_hbm, blend_ref)]
        )
    ]
    for copy in small:
        copy.start()
    large = [
        pltpu.make_async_copy(
            raw_hbm.at[:, :, pl.ds(i * SEND_LANES, SEND_LANES)], raw_ref.at[i], raw_sems.at[i]
        )
        for i in range(SENDS)
    ]
    for copy in large:
        copy.start()
    for s in range(SEC_DEV):
        for i in range(SENDS):
            warped[i, 128 * s + PIECES : 128 * s + 128, :] = jnp.zeros((32, SEND_LANES), BF16)
    line = lax.broadcasted_iota(jnp.int32, (128, 128), 0)
    lane = lax.broadcasted_iota(jnp.int32, (128, 128), 1)
    rows = lax.broadcasted_iota(jnp.int32, (8 * N_XY, 128), 0)
    rows = (rows // 8) * CHUNK + rows % 8
    for copy in small:
        copy.wait()
    owners = lane_rows(lanes, owner_ref)
    slot_rows = lane_rows(lanes, slot_ref)
    blend_rows = lane_rows(lanes, blend_ref)
    for s in range(SEC_DEV):
        owner = owners[s : s + 1]
        same = jnp.where((column(owner) == owner) & (line < lane), 1.0, 0.0)
        rank = jnp.sum(same, axis=0, keepdims=True)
        target = (owner * CHUNK + rank + float(s * CAP)).astype(jnp.int32)
        target = jnp.where(lane[0:1] < PIECES, target, -1)
        for j in range(PARTS):
            if s - j in (0, 1):
                at = slice(128 * (s - j), 128 * (s - j) + 128)
                select[j, :, at] = jnp.where(rows + 8 * j == target, 1.0, 0.0).astype(BF16)
        at = slice(128 * s, 128 * s + 128)
        blend[at, :] = column(blend_rows[s : s + 1])
        slots[at, :] = (column(slot_rows[s : s + 1]) + float(s * BLOCK + 1)).astype(BF16)

    copies = []

    def send_tiles(first, count):
        at = pl.ds(first, count)
        copies.append(
            pltpu.make_async_copy(out_ref.at[:, at], out_hbm.at[:, at], out_sems.at[len(copies)])
        )
        copies[-1].start()

    for i in range(SENDS):
        large[i].wait()
        for s in range(SEC_DEV):
            at = slice(128 * s, 128 * s + PIECES)
            scale = blend[at, :]
            for lane_at in range(0, SEND_LANES, 128):
                to = slice(lane_at, lane_at + 128)
                warped[i, at, to] = (raw_ref[i, s, :, to].astype(F32) * scale).astype(BF16)
        for j in range(PARTS):
            value = mm(select[j], warped[i, 128 * j : 128 * j + 256, :])
            first = LANE_TILES * j + i * (SEND_LANES // 128)
            for tile in range(SEND_LANES // 128):
                piece = value[:, tile * 128 : tile * 128 + 128].reshape(N_XY, 8, 128)
                out_ref[:, first + tile] = piece.astype(BF16)
            send_tiles(first, SEND_LANES // 128)
    ids = [mm(select[j], slots[128 * j : 128 * j + 256, :]) for j in range(PARTS)]
    lane = lax.broadcasted_iota(jnp.int32, (8 * N_XY, 128), 1)
    ids = jnp.where(lane == 0, ids[0], jnp.where(lane == 1, ids[1], ids[2]))
    out_ref[:, TILES_OUT - 1] = ids.reshape(N_XY, 8, 128).astype(BF16)
    send_tiles(TILES_OUT - 1, 1)
    for copy in copies:
        copy.wait()


def send_rows(owner, slot, blend, raw):
    hbm = pl.BlockSpec(memory_space=pltpu.HBM)
    return pl.pallas_call(
        send_kernel,
        out_shape=jax.ShapeDtypeStruct((N_XY, TILES_OUT, 8, 128), BF16),
        in_specs=[hbm, hbm, hbm, hbm],
        out_specs=hbm,
        scratch_shapes=[
            pltpu.VMEM((SEC_DEV, PIECES), jnp.int32),
            pltpu.VMEM((SEC_DEV, PIECES), jnp.int32),
            pltpu.VMEM((SEC_DEV, PIECES), F32),
            pltpu.VMEM((SENDS, SEC_DEV, PIECES, SEND_LANES), BF16),
            pltpu.VMEM((8, 128), F32),
            pltpu.VMEM((PARTS, 8 * N_XY, 256), BF16),
            pltpu.VMEM((KEYS, 128), F32),
            pltpu.VMEM((KEYS, 128), BF16),
            pltpu.VMEM((SENDS, KEYS, SEND_LANES), BF16),
            pltpu.VMEM((N_XY, TILES_OUT, 8, 128), BF16),
            pltpu.SemaphoreType.DMA((3,)),
            pltpu.SemaphoreType.DMA((SENDS,)),
            pltpu.SemaphoreType.DMA((SENDS * PARTS + 1,)),
        ],
        compiler_params=pltpu.CompilerParams(vmem_limit_bytes=60 * MIB),
    )(owner, slot, blend, raw)


def places(ids, part, count):
    wanted = lax.broadcasted_iota(jnp.int32, (count, 8 * N_XY), 0).astype(F32)
    match = ids[part : part + 1] == wanted + float(part * BLOCK + 1)
    return jnp.where(match, 1.0, 0.0).astype(BF16)


def row_ids(rows_ref):
    return rows_ref[:, TILES_OUT - 1].astype(F32).reshape(8 * N_XY, 128).T


def row_tiles(rows_ref, part, lane, size):
    first = LANE_TILES * part + lane // 128
    return jnp.concatenate(
        [rows_ref[:, first + tile].reshape(8 * N_XY, 128) for tile in range(size // 128)], axis=1
    )


def first_kernel(rows_ref, out_ref, place):
    place[...] = places(row_ids(rows_ref), 0, BLOCK)
    for at in range(0, FLAT, 1024):
        out_ref[:, at : at + 1024] = mm(place[...], row_tiles(rows_ref, 0, at, 1024)).astype(BF16)


def first_section(rows):
    return pl.pallas_call(
        first_kernel,
        out_shape=jax.ShapeDtypeStruct((BLOCK, FLAT), BF16),
        in_specs=[VMEM_SPEC],
        out_specs=VMEM_SPEC,
        scratch_shapes=[pltpu.VMEM((BLOCK, 8 * N_XY), BF16)],
        compiler_params=pltpu.CompilerParams(vmem_limit_bytes=8 * MIB),
        cost_estimate=pl.CostEstimate(flops=1 << 28, bytes_accessed=3 << 20, transcendentals=0),
    )(rows)


GROUP = 4
GROUPS = TILES // GROUP


def sublane_sum(value):
    total = value[0:8]
    for row in range(8, value.shape[0], 8):
        total = total + value[row : row + 8]
    return total


ROOT = math.sqrt(2.0)


def cross_rows(own, other, first_step):
    lanes = own.shape[1]
    a, b = (value.reshape(2, 8, 2, 8, lanes) for value in (own, other))
    shape = (8, 8, lanes)
    line = lax.broadcasted_iota(jnp.int32, shape, 1)
    head = (lax.broadcasted_iota(jnp.int32, shape, 0) == 0) & ((line == 0) | (line == 4))
    pair = line < 4
    if first_step < lanes:
        pair = pair & (lax.broadcasted_iota(jnp.int32, shape, 2) < first_step)

    def along_y(p, r):
        b_cosine, b_sine = b[r, :, 0], b[r, :, 1]
        if first_step:
            mixed, b_sine = b_sine, jnp.where(pair, 0.0, b_sine)
            turned = jnp.where(pair, -mixed, b_cosine)
        else:
            turned = b_cosine
        return (
            a[p, :, 0] * b_cosine + a[p, :, 1] * b_sine,
            a[p, :, 0] * b_sine - a[p, :, 1] * turned,
        )

    cc, cs, sc, ss = along_y(0, 0), along_y(0, 1), along_y(1, 0), along_y(1, 1)
    parts = {}
    for y in range(2):
        parts[0, y] = jnp.where(head, ROOT * cc[y], cc[y] + ss[y])
        parts[1, y] = jnp.where(head, ROOT * ss[y], cs[y] - sc[y])
        if first_step:
            for x in range(2):
                parts[x, y] = jnp.where(pair, ROOT * parts[x, y], parts[x, y])
    rows = jnp.stack([jnp.stack([parts[x, y] for y in range(2)], axis=1) for x in range(2)])
    return rows.reshape(256, lanes)


def down(value):
    return jnp.sum(value, axis=0, keepdims=True)


def weighed(table_ref, high):
    both = mm(table_ref[...], high)
    return both[:256] + both[256:]


def flow_sums(operands, third_ref, fourth_ref, high_ref, twice_ref, sums_ref):
    lanes = 128
    total = jnp.zeros((8, 2 * lanes), F32)
    along_x = jnp.zeros((8, 2 * lanes), F32)
    along_y = jnp.zeros((8, 2 * lanes), F32)
    for q in range(0, TILES, 2):
        rows = jnp.concatenate(
            [cross_rows(*operands(q + i), 0 if q + i else lanes) for i in range(2)], axis=1
        )
        high = rows.astype(BF16)
        twice = 2.0 * rows - high.astype(F32)
        total = total + sublane_sum(rows * rows)
        along_x = along_x + sublane_sum(twice * weighed(third_ref, high))
        for i in range(2):
            high_ref[q + i] = high[:, i * lanes : (i + 1) * lanes]
            twice_ref[q + i] = twice[:, i * lanes : (i + 1) * lanes]
    for g in range(0, TILES, 2):
        high, twice = (
            jnp.concatenate(
                [ref[:, 16 * (g + i) : 16 * (g + i) + 16, :].reshape(256, lanes) for i in range(2)],
                axis=1,
            )
            for ref in (high_ref, twice_ref)
        )
        along_y = along_y + sublane_sum(twice * weighed(fourth_ref, high))
    for i, value in enumerate((total, along_x, along_y)):
        sums_ref[i : i + 1, :] = down(value[:, :lanes] + value[:, lanes:])


def turn(value):
    return pltpu.roll(value, BLOCK, 1)


def flow_sums_packed(operands, third_ref, fourth_ref, turned_ref, sums_ref):
    total = jnp.zeros((8, 256), F32)
    along_x = jnp.zeros((8, 256), F32)
    along_y = jnp.zeros((8, 256), F32)
    left = lax.broadcasted_iota(jnp.int32, (8, 16, 128), 2) < BLOCK
    for p in range(0, TILES // 2, 2):
        pieces = [cross_rows(*operands(p + i), 0 if p + i else BLOCK) for i in range(2)]
        for i, piece in enumerate(pieces):
            straight = piece.reshape(8, 2, 16, 128)
            turned = turn(piece).reshape(8, 2, 16, 128)
            turned_ref[:, 2 * (p + i)] = jnp.where(left, straight[:, 0], turned[:, 1])
            turned_ref[:, 2 * (p + i) + 1] = jnp.where(left, turned[:, 0], straight[:, 1])
        rows = jnp.concatenate(pieces, axis=1)
        high = rows.astype(BF16)
        total = total + sublane_sum(rows * rows)
        twice = 2.0 * rows - high.astype(F32)
        along_x = along_x + sublane_sum(twice * weighed(third_ref, high))
    for g in range(0, TILES // 2, 2):
        rows = jnp.concatenate([turned_ref[g + i].reshape(256, 128) for i in range(2)], axis=1)
        high = rows.astype(BF16)
        twice = 2.0 * rows - high.astype(F32)
        along_y = along_y + sublane_sum(twice * weighed(fourth_ref, high))
    for i, value in enumerate((total, along_x, along_y)):
        value = down(value[:, :128] + value[:, 128:])
        sums_ref[i : i + 1, :] = value + turn(value)


def spectrum_kernel(
    rows_ref, first_ref, second_ref, third_ref, fourth_ref, last_ref, square_ref, sums_ref, third_sums_ref,
    place, high, low, own_first, own_second, high_part, twice_part, turned,
):
    ids = row_ids(rows_ref)
    for j in range(PARTS):
        place[j] = places(ids, j, 2 * BLOCK)
    wide = 2 * TILE
    for at in range(0, FLAT, wide):
        pieces, before = [], None
        for j in range(PARTS):
            value = mm(place[j], row_tiles(rows_ref, j, at, wide))
            pieces.append(value[:BLOCK] if before is None else before + value[:BLOCK])
            before = value[BLOCK:]
        patches = jnp.concatenate(pieces + [before], axis=0).astype(BF16)
        for i in range(2):
            both = mm(first_ref[...], patches[:, i * TILE : (i + 1) * TILE], NT)
            t = at // TILE + i
            high[t], low[t] = split(both[:256] + both[256:])

    square = jnp.zeros((8, PATCHES), F32)
    for q in range(TILES):
        at = slice(16 * q, 16 * q + 16)
        own = mm3(
            second_ref[...],
            high[:, at, :].reshape(256, PATCHES),
            low[:, at, :].reshape(256, PATCHES),
        )
        if q == 0:
            own = jnp.where(lax.broadcasted_iota(jnp.int32, (256, 1), 0) == 0, 0.0, own)
        square = square + sublane_sum(own * own)
        own_first[q] = own[:, :128]
        own_second[q] = own[:, 128:]
    square_ref[...] = square
    left = lax.broadcasted_iota(jnp.int32, (256, 128), 1) < BLOCK

    def operands(q):
        own = own_first[q]
        return own, jnp.where(left, turn(own), turn(own_second[q]))

    def packed_operands(p):
        even, odd = own_second[2 * p], own_second[2 * p + 1]
        last = jnp.where(left, turn(even), odd)
        last_ref[p] = last
        return jnp.where(left, even, turn(odd)), last

    flow_sums(operands, third_ref, fourth_ref, high_part, twice_part, sums_ref)
    flow_sums_packed(packed_operands, third_ref, fourth_ref, turned, third_sums_ref)


def spectrum(rows, tabs):
    return pl.pallas_call(
        spectrum_kernel,
        out_shape=[
            jax.ShapeDtypeStruct((TILES // 2, 256, 128), F32),
            jax.ShapeDtypeStruct((8, PATCHES), F32),
            jax.ShapeDtypeStruct((8, 128), F32),
            jax.ShapeDtypeStruct((8, 128), F32),
        ],
        in_specs=[VMEM_SPEC] * 5,
        out_specs=[VMEM_SPEC] * 4,
        scratch_shapes=[
            pltpu.VMEM((PARTS, 2 * BLOCK, 8 * N_XY), BF16),
            pltpu.VMEM((TILES, 256, PATCHES), BF16),
            pltpu.VMEM((TILES, 256, PATCHES), BF16),
            pltpu.VMEM((TILES, 256, 128), F32),
            pltpu.VMEM((TILES, 256, 128), F32),
            pltpu.VMEM((TILES, 256, 128), BF16),
            pltpu.VMEM((TILES, 256, 128), F32),
            pltpu.VMEM((TILES // 2, TILES, 16, 128), F32),
        ],
        compiler_params=pltpu.CompilerParams(vmem_limit_bytes=24 * MIB),
        cost_estimate=pl.CostEstimate(
            flops=2 * TILES * 256 * 256 * 11 * 256, bytes_accessed=12 << 20, transcendentals=0
        ),
    )(rows, *tabs)


def next_spectrum(next_ref, first_ref, second_ref, high, low, follow):
    left = lax.broadcasted_iota(jnp.int32, (16, 128), 1) < BLOCK
    for tg in range(GROUPS):
        rows = jnp.concatenate(
            [
                next_ref[:, (GROUP * tg + i) * TILE : (GROUP * tg + i + 1) * TILE]
                for i in range(GROUP)
            ],
            axis=0,
        )
        both = mm(first_ref[...], rows, NT)
        value = both[:256] + both[256:]
        for half in range(2):
            lanes = value[:, half * 128 : half * 128 + 128]
            rolled = pltpu.roll(lanes, BLOCK, 1)
            for pair in range(TILES // 2):
                g, to = pair // 2, (pair % 2) * 128
                even = slice(32 * pair, 32 * pair + 16)
                odd = slice(32 * pair + 16, 32 * pair + 32)
                for i in range(2):
                    t = GROUP * tg + 2 * half + i
                    if i == 0:
                        packed = jnp.where(left, lanes[even], rolled[odd])
                    else:
                        packed = jnp.where(left, rolled[even], lanes[odd])
                    at = slice(16 * t, 16 * t + 16)
                    up, down = split(packed)
                    high[g, at, to : to + 128] = up
                    low[g, at, to : to + 128] = down
    for g in range(GROUPS):
        follow[g] = mm3(second_ref[...], high[g], low[g])
    follow[0, 0:1, 0:BLOCK] = jnp.zeros((1, BLOCK), F32)


def flow_kernel(
    last_ref, square_ref, early_ref, third_sums_ref, next_ref,
    first_ref, second_ref, third_ref, fourth_ref, out_ref,
    next_high, next_low, follow, turned, late,
):
    next_spectrum(next_ref, first_ref, second_ref, next_high, next_low, follow)

    def operands(p):
        return last_ref[p], follow[p // 2, :, (p % 2) * 128 : (p % 2) * 128 + 128]

    flow_sums_packed(operands, third_ref, fourth_ref, turned, late)
    after = jnp.zeros((8, 256), F32)
    for g in range(GROUPS):
        after = after + sublane_sum(follow[g] * follow[g])
    after = after[:, :128] + after[:, 128:]
    after = after + pltpu.roll(after, BLOCK, 1)
    own = square_ref[...]
    low_roll, high_roll = (pltpu.roll(own[:, i : i + 128], BLOCK, 1) for i in (0, 128))
    left = lax.broadcasted_iota(jnp.int32, (8, 128), 1) < BLOCK
    other = jnp.concatenate(
        [jnp.where(left, low_roll, high_roll), jnp.where(left, high_roll, after)], axis=1
    )
    later = jnp.where(left, third_sums_ref[...], late[...])
    total, along_x, along_y = (
        jnp.concatenate([early_ref[i : i + 1, :], later[i : i + 1, :]], axis=1) for i in range(3)
    )
    norm = (down(own) * (1.0 / FLAT) + 1e-05) * (down(other) * (1.0 / FLAT) + 1e-05)
    factor = (1024.0 / (float(FLAT) * float(FLAT))) / norm
    total = jnp.maximum(total * factor, 0.5)
    tile_rows = []
    for value in (along_x * factor / total, along_y * factor / total):
        for half in range(2):
            lane_tile = value[:, half * 128 : half * 128 + 128]
            tile_rows += [lane_tile, pltpu.roll(lane_tile, 64, 1)]
    grid = jnp.concatenate(tile_rows, axis=0)
    lane = lax.broadcasted_iota(jnp.int32, (8, 128), 1)
    for j in range(N_SEC):
        upper = pltpu.roll(grid, (8 - 8 * j) % 128, 1)
        lower = pltpu.roll(grid, (128 - 8 * j) % 128, 1)
        gy = jnp.where(lane < GYW, lane, lane - GYW) + (8 * j - 8)
        window = jnp.where(lane < GYW, upper, lower)
        window = jnp.where((lane < 2 * GYW) & (gy >= 0) & (gy < 32), window, 0.0)
        packed = window[0:4] + pltpu.roll(window, 64, 1)[4:8]
        for b in range(N_XY):
            out_ref[j * N_XY + b] = packed


def flow_windows(own, following, tabs):
    return pl.pallas_call(
        flow_kernel,
        out_shape=jax.ShapeDtypeStruct((N_SEC * N_XY, 4, 128), F32),
        in_specs=[VMEM_SPEC] * 9,
        out_specs=VMEM_SPEC,
        scratch_shapes=[
            pltpu.VMEM((GROUPS, 256, 256), BF16),
            pltpu.VMEM((GROUPS, 256, 256), BF16),
            pltpu.VMEM((GROUPS, 256, 256), F32),
            pltpu.VMEM((TILES // 2, TILES, 16, 128), F32),
            pltpu.VMEM((8, 128), F32),
        ],
        compiler_params=pltpu.CompilerParams(vmem_limit_bytes=24 * MIB),
        cost_estimate=pl.CostEstimate(
            flops=2 * TILES * 256 * 256 * 8 * 256, bytes_accessed=8 << 20, transcendentals=0
        ),
    )(*own, following, *tabs)


def relax_kernel(place_ref, arrived_ref, out_ref):
    column, block = place_ref[0], place_ref[1]
    lane = lax.broadcasted_iota(jnp.int32, (8, 128), 1)
    lane = jnp.where(lane < 64, lane, lane - 64)
    top = lane < GYW
    gy = jnp.where(top, lane, lane - GYW) + (8 * column - 8)
    inside = (lane < 2 * GYW) & (gy >= 0) & (gy < 32)
    mask = {}
    for o in range(-4, 5):
        valid = (block + o >= 0) & (block + o < N_XY)
        mask[o] = jnp.where(inside & valid, 0.2, 0.0)
    zero = jnp.zeros((8, 128), F32)
    result = []
    for s in range(0, N_SEC, 2):
        flow, mesh = {}, {}
        for o in range(-4, 5):
            at = jnp.clip(block + o, 0, N_XY - 1)
            value = jnp.concatenate(
                [arrived_ref[s * N_XY + at], arrived_ref[(s + 1) * N_XY + at]], axis=0
            )
            flow[o] = value * mask[o]
            mesh[o] = jnp.where(mask[o] > 0.0, value, 0.0)
        for step in range(ITERS):
            reach = (ITERS - step) // 2
            up = {o: pltpu.roll(mesh[o], 128 - GYW, 1) for o in mesh}
            down = {o: pltpu.roll(mesh[o], GYW, 1) for o in mesh}
            new = {}
            for o in range(-reach, reach + 1):
                near = jnp.where(
                    top, up[o] + up.get(o - 1, zero), down[o] + down.get(o + 1, zero)
                )
                near = near + pltpu.roll(mesh[o], 1, 1) + pltpu.roll(mesh[o], 127, 1)
                new[o] = flow[o] + mask[o] * near
            mesh = new
        result.append(mesh[0])
    turned = jnp.concatenate(result + [jnp.zeros((112, 128), F32)], axis=0).T
    for c in range(2):
        for i in range(2):
            at = 64 * c + GYW * i + 8
            out_ref[c, i] = turned[at : at + 8, :15]


def relax(place, arrived):
    return pl.pallas_call(
        relax_kernel,
        out_shape=jax.ShapeDtypeStruct((2, 2, 8, 15), F32),
        in_specs=[
            pl.BlockSpec(memory_space=pltpu.SMEM),
            pl.BlockSpec(memory_space=pltpu.VMEM),
        ],
        out_specs=pl.BlockSpec(memory_space=pltpu.VMEM),
        compiler_params=pltpu.CompilerParams(vmem_limit_bytes=8 * MIB),
    )(place, arrived)


def local(raw_pieces, piece_owner, piece_slot, blend):
    tabs = [jnp.asarray(t) for t in tables()]
    outgoing = send_rows(piece_owner[:, :, 0], piece_slot, blend, raw_pieces)
    arrived = lax.all_to_all(outgoing, "xy", split_axis=0, concat_axis=0, tiled=True)
    first = first_section(arrived)
    back = [(i + 1, i) for i in range(N_SEC - 1)]
    following = lax.ppermute(first, "sec", back)
    own = spectrum(arrived, tabs)
    windows = flow_windows(own, following, tabs)
    got = lax.all_to_all(windows, ("sec", "xy"), split_axis=0, concat_axis=0, tiled=True)
    place = jnp.stack([lax.axis_index("sec"), lax.axis_index("xy")]).astype(jnp.int32)
    return relax(place, got).transpose(3, 0, 1, 2)


def solution(mesh):
    in_specs = (P("sec", "xy", None), P("sec", "xy", None), P("sec", "xy"), P("sec", "xy"))
    out_specs = P(None, None, "xy", "sec")
    return jax.shard_map(local, mesh=mesh, in_specs=in_specs, out_specs=out_specs, check_vma=False)
```

```python
import math

import jax
import jax.numpy as jnp
import numpy as np
from jax import lax
from jax.experimental import pallas as pl
from jax.experimental.pallas import tpu as pltpu
from jax.sharding import PartitionSpec as P

PS = 64
FLAT = PS * PS
CAP = 6
N_SEC = 4
N_XY = 32
SEC_DEV = 4
PIECES = 96
BLOCK = 64
ITERS = 8
KEYS = SEC_DEV * 128
CHUNK = SEC_DEV * CAP
LANE_TILES = FLAT // 128
PARTS = CHUNK // 8
TILES_OUT = PARTS * LANE_TILES + 1
PATCHES = SEC_DEV * BLOCK
TILE = 256
TILES = FLAT // TILE
GYW = 24
F32 = jnp.float32
BF16 = jnp.bfloat16
MIB = 1024 * 1024

VMEM_SPEC = pl.BlockSpec(memory_space=pltpu.VMEM)
NT = (((1,), (1,)), ((), ()))
NN = (((1,), (0,)), ((), ()))


def real_basis():
    pos = np.arange(PS)
    rows = np.zeros((2, 32, PS))
    for k in range(32):
        angle = 2.0 * math.pi * ((k * pos) % PS) / PS
        rows[0, k] = np.cos(angle)
        rows[1, k] = np.sin(angle) if k else np.cos(math.pi * pos)
        rows[:, k] *= (math.sqrt(2.0) if k else 1.0) / 8.0
    return rows


def split_table(table):
    high = table.astype(jnp.bfloat16)
    low = (table - high.astype(np.float64)).astype(jnp.bfloat16)
    return np.concatenate([high, low], axis=0)


def tables():
    basis = real_basis()
    by_x = basis.reshape(2, 8, 4, PS)
    by_y = basis.reshape(2, 16, 2, PS)
    two, four = np.eye(2), np.eye(4)
    first = np.einsum("ab,pqky->qpkaby", four, by_y).reshape(256, 256)
    second = np.einsum("pu,kv,cgitb->cgpkituvb", two, two, by_x.reshape(2, 8, 4, 16, 4))
    second = second.reshape(256, 256)
    shift = (np.arange(PS) + 32) % PS - 32
    weigh = np.einsum("pkd,d,rld->pkrl", basis, shift, basis)
    third = np.einsum("pu,kv,cgidhj->cgpkidhuvj", two, two, weigh.reshape(2, 8, 4, 2, 8, 4))
    third = third.reshape(256, 256)
    fourth = np.einsum("ij,pqkurv->qpkiruvj", four, weigh.reshape(2, 16, 2, 2, 16, 2))
    fourth = fourth.reshape(256, 256)
    return [split_table(t) for t in (first, second, third, fourth)]


def mm(a, b, dims=NN):
    return lax.dot_general(a, b, dims, preferred_element_type=F32)


def split(value):
    high = value.astype(BF16)
    return high, (value - high.astype(F32)).astype(BF16)


def mm3(table, high, low):
    both = mm(table, high)
    return both[:256] + both[256:] + mm(table[:256], low)


def lane_rows(scratch, ref):
    scratch[...] = jnp.zeros_like(scratch)
    scratch[0:SEC_DEV, 0:PIECES] = ref[...].astype(F32)
    return scratch[0:SEC_DEV, :]


def column(row):
    return jnp.broadcast_to(row, (128, 128)).T


SEND_LANES = 1024
SENDS = FLAT // SEND_LANES
SEND_TILES = SEND_LANES // 128


def tile_of(part, lane_tile):
    return (lane_tile // SEND_TILES * PARTS + part) * SEND_TILES + lane_tile % SEND_TILES


def send_kernel(
    owner_hbm, slot_hbm, blend_hbm, raw_hbm, out_hbm,
    owner_ref, slot_ref, blend_ref, raw_ref, lanes, select, blend, slots, warped, out_ref,
    sems, raw_sems, out_sems,
):
    small = [
        pltpu.make_async_copy(source, target, sems.at[i])
        for i, (source, target) in enumerate(
            [(owner_hbm, owner_ref), (slot_hbm, slot_ref), (blend_hbm, blend_ref)]
        )
    ]
    for copy in small:
        copy.start()
    large = [
        pltpu.make_async_copy(
            raw_hbm.at[:, :, pl.ds(i * SEND_LANES, SEND_LANES)], raw_ref.at[i], raw_sems.at[i]
        )
        for i in range(SENDS)
    ]
    large[0].start()
    for s in range(SEC_DEV):
        for i in range(SENDS):
            warped[i, 128 * s + PIECES : 128 * s + 128, :] = jnp.zeros((32, SEND_LANES), BF16)
    line = lax.broadcasted_iota(jnp.int32, (128, 128), 0)
    lane = lax.broadcasted_iota(jnp.int32, (128, 128), 1)
    lane_id = lax.broadcasted_iota(jnp.int32, (8 * N_XY, 128), 1)
    rows = lax.broadcasted_iota(jnp.int32, (8 * N_XY, 128), 0)
    rows = (rows // 8) * CHUNK + rows % 8
    for copy in small:
        copy.wait()
    large[1].start()
    owners = lane_rows(lanes, owner_ref)
    slot_rows = lane_rows(lanes, slot_ref)
    blend_rows = lane_rows(lanes, blend_ref)
    for s in range(SEC_DEV):
        owner = owners[s : s + 1]
        same = jnp.where((column(owner) == owner) & (line < lane), 1.0, 0.0)
        rank = jnp.sum(same, axis=0, keepdims=True)
        target = (owner * CHUNK + rank + float(s * CAP)).astype(jnp.int32)
        target = jnp.where(lane[0:1] < PIECES, target, -1)
        for j in range(PARTS):
            if s - j in (0, 1):
                at = slice(128 * (s - j), 128 * (s - j) + 128)
                select[j, :, at] = jnp.where(rows + 8 * j == target, 1.0, 0.0).astype(BF16)
        at = slice(128 * s, 128 * s + 128)
        blend[at, :] = column(blend_rows[s : s + 1])
        slots[at, :] = (column(slot_rows[s : s + 1]) + float(s * BLOCK + 1)).astype(BF16)

    ids = [mm(select[j], slots[128 * j : 128 * j + 256, :]) for j in range(PARTS)]
    ids = jnp.where(lane_id == 0, ids[0], jnp.where(lane_id == 1, ids[1], ids[2]))
    out_ref[:, TILES_OUT - 1] = ids.reshape(N_XY, 8, 128).astype(BF16)
    copies = []
    for i in range(SENDS):
        large[i].wait()
        if i == 0:
            large[2].start()
            large[3].start()
        for s in range(SEC_DEV):
            at = slice(128 * s, 128 * s + PIECES)
            scale = blend[at, :]
            for lane_at in range(0, SEND_LANES, 128):
                to = slice(lane_at, lane_at + 128)
                warped[i, at, to] = (raw_ref[i, s, :, to].astype(F32) * scale).astype(BF16)
        for j in range(PARTS):
            value = mm(select[j], warped[i, 128 * j : 128 * j + 256, :])
            for tile in range(SEND_TILES):
                piece = value[:, tile * 128 : tile * 128 + 128].reshape(N_XY, 8, 128)
                out_ref[:, tile_of(j, i * SEND_TILES + tile)] = piece.astype(BF16)
        at = pl.ds(i * PARTS * SEND_TILES, PARTS * SEND_TILES + (i == SENDS - 1))
        copies.append(pltpu.make_async_copy(out_ref.at[:, at], out_hbm.at[:, at], out_sems.at[i]))
        copies[i].start()
    for copy in copies:
        copy.wait()


def send_rows(owner, slot, blend, raw):
    hbm = pl.BlockSpec(memory_space=pltpu.HBM)
    return pl.pallas_call(
        send_kernel,
        out_shape=jax.ShapeDtypeStruct((N_XY, TILES_OUT, 8, 128), BF16),
        in_specs=[hbm, hbm, hbm, hbm],
        out_specs=hbm,
        scratch_shapes=[
            pltpu.VMEM((SEC_DEV, PIECES), jnp.int32),
            pltpu.VMEM((SEC_DEV, PIECES), jnp.int32),
            pltpu.VMEM((SEC_DEV, PIECES), F32),
            pltpu.VMEM((SENDS, SEC_DEV, PIECES, SEND_LANES), BF16),
            pltpu.VMEM((8, 128), F32),
            pltpu.VMEM((PARTS, 8 * N_XY, 256), BF16),
            pltpu.VMEM((KEYS, 128), F32),
            pltpu.VMEM((KEYS, 128), BF16),
            pltpu.VMEM((SENDS, KEYS, SEND_LANES), BF16),
            pltpu.VMEM((N_XY, TILES_OUT, 8, 128), BF16),
            pltpu.SemaphoreType.DMA((3,)),
            pltpu.SemaphoreType.DMA((SENDS,)),
            pltpu.SemaphoreType.DMA((SENDS,)),
        ],
        compiler_params=pltpu.CompilerParams(vmem_limit_bytes=60 * MIB),
    )(owner, slot, blend, raw)


def places(ids, part, count):
    wanted = lax.broadcasted_iota(jnp.int32, (count, 8 * N_XY), 0).astype(F32)
    match = ids[part : part + 1] == wanted + float(part * BLOCK + 1)
    return jnp.where(match, 1.0, 0.0).astype(BF16)


def row_ids(rows_ref):
    return rows_ref[:, TILES_OUT - 1].astype(F32).reshape(8 * N_XY, 128).T


def row_tiles(rows_ref, part, lane, size):
    first = lane // 128
    return jnp.concatenate(
        [
            rows_ref[:, tile_of(part, first + tile)].reshape(8 * N_XY, 128)
            for tile in range(size // 128)
        ],
        axis=1,
    )


def first_kernel(rows_ref, out_ref, place):
    place[...] = places(row_ids(rows_ref), 0, BLOCK)
    for at in range(0, FLAT, 1024):
        out_ref[:, at : at + 1024] = mm(place[...], row_tiles(rows_ref, 0, at, 1024)).astype(BF16)


def first_section(rows):
    return pl.pallas_call(
        first_kernel,
        out_shape=jax.ShapeDtypeStruct((BLOCK, FLAT), BF16),
        in_specs=[VMEM_SPEC],
        out_specs=VMEM_SPEC,
        scratch_shapes=[pltpu.VMEM((BLOCK, 8 * N_XY), BF16)],
        compiler_params=pltpu.CompilerParams(vmem_limit_bytes=8 * MIB),
        cost_estimate=pl.CostEstimate(flops=1 << 28, bytes_accessed=3 << 20, transcendentals=0),
    )(rows)


GROUP = 4
GROUPS = TILES // GROUP


def sublane_sum(value):
    total = value[0:8]
    for row in range(8, value.shape[0], 8):
        total = total + value[row : row + 8]
    return total


ROOT = math.sqrt(2.0)


def cross_rows(own, other, first_step):
    lanes = own.shape[1]
    a, b = (value.reshape(2, 8, 2, 8, lanes) for value in (own, other))
    shape = (8, 8, lanes)
    line = lax.broadcasted_iota(jnp.int32, shape, 1)
    head = (lax.broadcasted_iota(jnp.int32, shape, 0) == 0) & ((line == 0) | (line == 4))
    pair = line < 4
    if first_step < lanes:
        pair = pair & (lax.broadcasted_iota(jnp.int32, shape, 2) < first_step)

    def along_y(p, r):
        b_cosine, b_sine = b[r, :, 0], b[r, :, 1]
        if first_step:
            mixed, b_sine = b_sine, jnp.where(pair, 0.0, b_sine)
            turned = jnp.where(pair, -mixed, b_cosine)
        else:
            turned = b_cosine
        return (
            a[p, :, 0] * b_cosine + a[p, :, 1] * b_sine,
            a[p, :, 0] * b_sine - a[p, :, 1] * turned,
        )

    cc, cs, sc, ss = along_y(0, 0), along_y(0, 1), along_y(1, 0), along_y(1, 1)
    parts = {}
    for y in range(2):
        parts[0, y] = jnp.where(head, ROOT * cc[y], cc[y] + ss[y])
        parts[1, y] = jnp.where(head, ROOT * ss[y], cs[y] - sc[y])
        if first_step:
            for x in range(2):
                parts[x, y] = jnp.where(pair, ROOT * parts[x, y], parts[x, y])
    rows = jnp.stack([jnp.stack([parts[x, y] for y in range(2)], axis=1) for x in range(2)])
    return rows.reshape(256, lanes)


def down(value):
    return jnp.sum(value, axis=0, keepdims=True)


def weighed(table_ref, high):
    both = mm(table_ref[...], high)
    return both[:256] + both[256:]


def flow_sums(operands, third_ref, fourth_ref, high_ref, twice_ref, sums_ref):
    lanes = 128
    total = jnp.zeros((8, 2 * lanes), F32)
    along_x = jnp.zeros((8, 2 * lanes), F32)
    along_y = jnp.zeros((8, 2 * lanes), F32)
    for q in range(0, TILES, 2):
        rows = jnp.concatenate(
            [cross_rows(*operands(q + i), 0 if q + i else lanes) for i in range(2)], axis=1
        )
        high = rows.astype(BF16)
        twice = 2.0 * rows - high.astype(F32)
        total = total + sublane_sum(rows * rows)
        along_x = along_x + sublane_sum(twice * weighed(third_ref, high))
        for i in range(2):
            high_ref[q + i] = high[:, i * lanes : (i + 1) * lanes]
            twice_ref[q + i] = twice[:, i * lanes : (i + 1) * lanes]
    for g in range(0, TILES, 2):
        high, twice = (
            jnp.concatenate(
                [ref[:, 16 * (g + i) : 16 * (g + i) + 16, :].reshape(256, lanes) for i in range(2)],
                axis=1,
            )
            for ref in (high_ref, twice_ref)
        )
        along_y = along_y + sublane_sum(twice * weighed(fourth_ref, high))
    for i, value in enumerate((total, along_x, along_y)):
        sums_ref[i : i + 1, :] = down(value[:, :lanes] + value[:, lanes:])


def turn(value):
    return pltpu.roll(value, BLOCK, 1)


def flow_sums_packed(operands, third_ref, fourth_ref, turned_ref, sums_ref):
    total = jnp.zeros((8, 256), F32)
    along_x = jnp.zeros((8, 256), F32)
    along_y = jnp.zeros((8, 256), F32)
    left = lax.broadcasted_iota(jnp.int32, (8, 16, 128), 2) < BLOCK
    for p in range(0, TILES // 2, 2):
        pieces = [cross_rows(*operands(p + i), 0 if p + i else BLOCK) for i in range(2)]
        for i, piece in enumerate(pieces):
            straight = piece.reshape(8, 2, 16, 128)
            turned = turn(piece).reshape(8, 2, 16, 128)
            turned_ref[:, 2 * (p + i)] = jnp.where(left, straight[:, 0], turned[:, 1])
            turned_ref[:, 2 * (p + i) + 1] = jnp.where(left, turned[:, 0], straight[:, 1])
        rows = jnp.concatenate(pieces, axis=1)
        high = rows.astype(BF16)
        total = total + sublane_sum(rows * rows)
        twice = 2.0 * rows - high.astype(F32)
        along_x = along_x + sublane_sum(twice * weighed(third_ref, high))
    for g in range(0, TILES // 2, 2):
        rows = jnp.concatenate([turned_ref[g + i].reshape(256, 128) for i in range(2)], axis=1)
        high = rows.astype(BF16)
        twice = 2.0 * rows - high.astype(F32)
        along_y = along_y + sublane_sum(twice * weighed(fourth_ref, high))
    for i, value in enumerate((total, along_x, along_y)):
        value = down(value[:, :128] + value[:, 128:])
        sums_ref[i : i + 1, :] = value + turn(value)


def spectrum_kernel(
    rows_ref, first_ref, second_ref, third_ref, fourth_ref, last_ref, square_ref, sums_ref, third_sums_ref,
    place, high, low, own_first, own_second, high_part, twice_part, turned,
):
    ids = row_ids(rows_ref)
    for j in range(PARTS):
        place[j] = places(ids, j, 2 * BLOCK)
    wide = 2 * TILE
    for at in range(0, FLAT, wide):
        pieces, before = [], None
        for j in range(PARTS):
            value = mm(place[j], row_tiles(rows_ref, j, at, wide))
            pieces.append(value[:BLOCK] if before is None else before + value[:BLOCK])
            before = value[BLOCK:]
        patches = jnp.concatenate(pieces + [before], axis=0).astype(BF16)
        for i in range(2):
            both = mm(first_ref[...], patches[:, i * TILE : (i + 1) * TILE], NT)
            t = at // TILE + i
            high[t], low[t] = split(both[:256] + both[256:])

    square = jnp.zeros((8, PATCHES), F32)
    for q in range(TILES):
        at = slice(16 * q, 16 * q + 16)
        own = mm3(
            second_ref[...],
            high[:, at, :].reshape(256, PATCHES),
            low[:, at, :].reshape(256, PATCHES),
        )
        if q == 0:
            own = jnp.where(lax.broadcasted_iota(jnp.int32, (256, 1), 0) == 0, 0.0, own)
        square = square + sublane_sum(own * own)
        own_first[q] = own[:, :128]
        own_second[q] = own[:, 128:]
    square_ref[...] = square
    left = lax.broadcasted_iota(jnp.int32, (256, 128), 1) < BLOCK

    def operands(q):
        own = own_first[q]
        return own, jnp.where(left, turn(own), turn(own_second[q]))

    def packed_operands(p):
        even, odd = own_second[2 * p], own_second[2 * p + 1]
        last = jnp.where(left, turn(even), odd)
        last_ref[p] = last
        return jnp.where(left, even, turn(odd)), last

    flow_sums(operands, third_ref, fourth_ref, high_part, twice_part, sums_ref)
    flow_sums_packed(packed_operands, third_ref, fourth_ref, turned, third_sums_ref)


def spectrum(rows, tabs):
    return pl.pallas_call(
        spectrum_kernel,
        out_shape=[
            jax.ShapeDtypeStruct((TILES // 2, 256, 128), F32),
            jax.ShapeDtypeStruct((8, PATCHES), F32),
            jax.ShapeDtypeStruct((8, 128), F32),
            jax.ShapeDtypeStruct((8, 128), F32),
        ],
        in_specs=[VMEM_SPEC] * 5,
        out_specs=[VMEM_SPEC] * 4,
        scratch_shapes=[
            pltpu.VMEM((PARTS, 2 * BLOCK, 8 * N_XY), BF16),
            pltpu.VMEM((TILES, 256, PATCHES), BF16),
            pltpu.VMEM((TILES, 256, PATCHES), BF16),
            pltpu.VMEM((TILES, 256, 128), F32),
            pltpu.VMEM((TILES, 256, 128), F32),
            pltpu.VMEM((TILES, 256, 128), BF16),
            pltpu.VMEM((TILES, 256, 128), F32),
            pltpu.VMEM((TILES // 2, TILES, 16, 128), F32),
        ],
        compiler_params=pltpu.CompilerParams(vmem_limit_bytes=24 * MIB),
        cost_estimate=pl.CostEstimate(
            flops=2 * TILES * 256 * 256 * 11 * 256, bytes_accessed=12 << 20, transcendentals=0
        ),
    )(rows, *tabs)


def next_spectrum(next_ref, first_ref, second_ref, high, low, follow):
    left = lax.broadcasted_iota(jnp.int32, (16, 128), 1) < BLOCK
    for tg in range(GROUPS):
        rows = jnp.concatenate(
            [
                next_ref[:, (GROUP * tg + i) * TILE : (GROUP * tg + i + 1) * TILE]
                for i in range(GROUP)
            ],
            axis=0,
        )
        both = mm(first_ref[...], rows, NT)
        value = both[:256] + both[256:]
        for half in range(2):
            lanes = value[:, half * 128 : half * 128 + 128]
            rolled = pltpu.roll(lanes, BLOCK, 1)
            for pair in range(TILES // 2):
                g, to = pair // 2, (pair % 2) * 128
                even = slice(32 * pair, 32 * pair + 16)
                odd = slice(32 * pair + 16, 32 * pair + 32)
                for i in range(2):
                    t = GROUP * tg + 2 * half + i
                    if i == 0:
                        packed = jnp.where(left, lanes[even], rolled[odd])
                    else:
                        packed = jnp.where(left, rolled[even], lanes[odd])
                    at = slice(16 * t, 16 * t + 16)
                    up, down = split(packed)
                    high[g, at, to : to + 128] = up
                    low[g, at, to : to + 128] = down
    for g in range(GROUPS):
        follow[g] = mm3(second_ref[...], high[g], low[g])
    follow[0, 0:1, 0:BLOCK] = jnp.zeros((1, BLOCK), F32)


def flow_kernel(
    last_ref, square_ref, early_ref, third_sums_ref, next_ref,
    first_ref, second_ref, third_ref, fourth_ref, out_ref,
    next_high, next_low, follow, turned, late,
):
    next_spectrum(next_ref, first_ref, second_ref, next_high, next_low, follow)

    def operands(p):
        return last_ref[p], follow[p // 2, :, (p % 2) * 128 : (p % 2) * 128 + 128]

    flow_sums_packed(operands, third_ref, fourth_ref, turned, late)
    after = jnp.zeros((8, 256), F32)
    for g in range(GROUPS):
        after = after + sublane_sum(follow[g] * follow[g])
    after = after[:, :128] + after[:, 128:]
    after = after + pltpu.roll(after, BLOCK, 1)
    own = square_ref[...]
    low_roll, high_roll = (pltpu.roll(own[:, i : i + 128], BLOCK, 1) for i in (0, 128))
    left = lax.broadcasted_iota(jnp.int32, (8, 128), 1) < BLOCK
    other = jnp.concatenate(
        [jnp.where(left, low_roll, high_roll), jnp.where(left, high_roll, after)], axis=1
    )
    later = jnp.where(left, third_sums_ref[...], late[...])
    total, along_x, along_y = (
        jnp.concatenate([early_ref[i : i + 1, :], later[i : i + 1, :]], axis=1) for i in range(3)
    )
    norm = (down(own) * (1.0 / FLAT) + 1e-05) * (down(other) * (1.0 / FLAT) + 1e-05)
    factor = (1024.0 / (float(FLAT) * float(FLAT))) / norm
    total = jnp.maximum(total * factor, 0.5)
    tile_rows = []
    for value in (along_x * factor / total, along_y * factor / total):
        for half in range(2):
            lane_tile = value[:, half * 128 : half * 128 + 128]
            tile_rows += [lane_tile, pltpu.roll(lane_tile, 64, 1)]
    grid = jnp.concatenate(tile_rows, axis=0)
    lane = lax.broadcasted_iota(jnp.int32, (8, 128), 1)
    for j in range(N_SEC):
        upper = pltpu.roll(grid, (8 - 8 * j) % 128, 1)
        lower = pltpu.roll(grid, (128 - 8 * j) % 128, 1)
        gy = jnp.where(lane < GYW, lane, lane - GYW) + (8 * j - 8)
        window = jnp.where(lane < GYW, upper, lower)
        window = jnp.where((lane < 2 * GYW) & (gy >= 0) & (gy < 32), window, 0.0)
        packed = window[0:4] + pltpu.roll(window, 64, 1)[4:8]
        for b in range(N_XY):
            out_ref[j * N_XY + b] = packed


def flow_windows(own, following, tabs):
    return pl.pallas_call(
        flow_kernel,
        out_shape=jax.ShapeDtypeStruct((N_SEC * N_XY, 4, 128), F32),
        in_specs=[VMEM_SPEC] * 9,
        out_specs=VMEM_SPEC,
        scratch_shapes=[
            pltpu.VMEM((GROUPS, 256, 256), BF16),
            pltpu.VMEM((GROUPS, 256, 256), BF16),
            pltpu.VMEM((GROUPS, 256, 256), F32),
            pltpu.VMEM((TILES // 2, TILES, 16, 128), F32),
            pltpu.VMEM((8, 128), F32),
        ],
        compiler_params=pltpu.CompilerParams(vmem_limit_bytes=24 * MIB),
        cost_estimate=pl.CostEstimate(
            flops=2 * TILES * 256 * 256 * 8 * 256, bytes_accessed=8 << 20, transcendentals=0
        ),
    )(*own, following, *tabs)


def relax_kernel(arrived_ref, out_ref):
    column, block = lax.axis_index("sec"), lax.axis_index("xy")
    lane = lax.broadcasted_iota(jnp.int32, (8, 128), 1)
    lane = jnp.where(lane < 64, lane, lane - 64)
    top = lane < GYW
    gy = jnp.where(top, lane, lane - GYW) + (8 * column - 8)
    inside = (lane < 2 * GYW) & (gy >= 0) & (gy < 32)
    mask = {}
    for o in range(-4, 5):
        valid = (block + o >= 0) & (block + o < N_XY)
        mask[o] = jnp.where(inside & valid, 0.2, 0.0)
    zero = jnp.zeros((8, 128), F32)
    result = []
    for s in range(0, N_SEC, 2):
        flow, mesh = {}, {}
        for o in range(-4, 5):
            at = jnp.clip(block + o, 0, N_XY - 1)
            value = jnp.concatenate(
                [arrived_ref[s * N_XY + at], arrived_ref[(s + 1) * N_XY + at]], axis=0
            )
            flow[o] = value * mask[o]
            mesh[o] = jnp.where(mask[o] > 0.0, value, 0.0)
        for step in range(ITERS):
            reach = (ITERS - step) // 2
            up = {o: pltpu.roll(mesh[o], 128 - GYW, 1) for o in mesh}
            down = {o: pltpu.roll(mesh[o], GYW, 1) for o in mesh}
            new = {}
            for o in range(-reach, reach + 1):
                near = jnp.where(
                    top, up[o] + up.get(o - 1, zero), down[o] + down.get(o + 1, zero)
                )
                near = near + pltpu.roll(mesh[o], 1, 1) + pltpu.roll(mesh[o], 127, 1)
                new[o] = flow[o] + mask[o] * near
            mesh = new
        result.append(mesh[0])
    turned = jnp.concatenate(result + [jnp.zeros((112, 128), F32)], axis=0).T
    for c in range(2):
        for i in range(2):
            at = 64 * c + GYW * i + 8
            out_ref[c, i] = turned[at : at + 8, :15]


def relax(arrived):
    return pl.pallas_call(
        relax_kernel,
        out_shape=jax.ShapeDtypeStruct((2, 2, 8, 15), F32),
        in_specs=[VMEM_SPEC],
        out_specs=pl.BlockSpec(memory_space=pltpu.VMEM),
        compiler_params=pltpu.CompilerParams(vmem_limit_bytes=8 * MIB),
    )(arrived)


def local(raw_pieces, piece_owner, piece_slot, blend):
    tabs = [jnp.asarray(t) for t in tables()]
    outgoing = send_rows(piece_owner[:, :, 0], piece_slot, blend, raw_pieces)
    arrived = lax.all_to_all(outgoing, "xy", split_axis=0, concat_axis=0, tiled=True)
    first = first_section(arrived)
    back = [(i + 1, i) for i in range(N_SEC - 1)]
    following = lax.ppermute(first, "sec", back)
    own = spectrum(arrived, tabs)
    windows = flow_windows(own, following, tabs)
    got = lax.all_to_all(windows, ("sec", "xy"), split_axis=0, concat_axis=0, tiled=True)
    return relax(got).transpose(3, 0, 1, 2)


def solution(mesh):
    in_specs = (P("sec", "xy", None), P("sec", "xy", None), P("sec", "xy"), P("sec", "xy"))
    out_specs = P(None, None, "xy", "sec")
    return jax.shard_map(local, mesh=mesh, in_specs=in_specs, out_specs=out_specs, check_vma=False)
```

```python
import math

import jax
import jax.numpy as jnp
import numpy as np
from jax import lax
from jax.experimental import pallas as pl
from jax.experimental.pallas import tpu as pltpu
from jax.sharding import PartitionSpec as P

PS = 64
FLAT = PS * PS
CAP = 6
N_SEC = 4
N_XY = 32
SEC_DEV = 4
PIECES = 96
BLOCK = 64
ITERS = 8
KEYS = SEC_DEV * 128
CHUNK = SEC_DEV * CAP
LANE_TILES = FLAT // 128
PARTS = CHUNK // 8
TILES_OUT = PARTS * LANE_TILES + 1
PATCHES = SEC_DEV * BLOCK
TILE = 256
TILES = FLAT // TILE
GYW = 24
F32 = jnp.float32
BF16 = jnp.bfloat16
MIB = 1024 * 1024

VMEM_SPEC = pl.BlockSpec(memory_space=pltpu.VMEM)
NT = (((1,), (1,)), ((), ()))
NN = (((1,), (0,)), ((), ()))


def real_basis():
    pos = np.arange(PS)
    rows = np.zeros((2, 32, PS))
    for k in range(32):
        angle = 2.0 * math.pi * ((k * pos) % PS) / PS
        rows[0, k] = np.cos(angle)
        rows[1, k] = np.sin(angle) if k else np.cos(math.pi * pos)
        rows[:, k] *= (math.sqrt(2.0) if k else 1.0) / 8.0
    return rows


def split_table(table):
    high = table.astype(jnp.bfloat16)
    low = (table - high.astype(np.float64)).astype(jnp.bfloat16)
    return np.concatenate([high, low], axis=0)


def tables():
    basis = real_basis()
    by_x = basis.reshape(2, 8, 4, PS)
    by_y = basis.reshape(2, 16, 2, PS)
    two, four = np.eye(2), np.eye(4)
    first = np.einsum("ab,pqky->qpkaby", four, by_y).reshape(256, 256)
    second = np.einsum("pu,kv,cgitb->cgpkituvb", two, two, by_x.reshape(2, 8, 4, 16, 4))
    second = second.reshape(256, 256)
    shift = (np.arange(PS) + 32) % PS - 32
    weigh = np.einsum("pkd,d,rld->pkrl", basis, shift, basis)
    third = np.einsum("pu,kv,cgidhj->cgpkidhuvj", two, two, weigh.reshape(2, 8, 4, 2, 8, 4))
    third = third.reshape(256, 256)
    fourth = np.einsum("ij,pqkurv->qpkiruvj", four, weigh.reshape(2, 16, 2, 2, 16, 2))
    fourth = fourth.reshape(256, 256)
    return [split_table(t) for t in (first, second, third, fourth)]


def mm(a, b, dims=NN):
    return lax.dot_general(a, b, dims, preferred_element_type=F32)


def split(value):
    high = value.astype(BF16)
    return high, (value - high.astype(F32)).astype(BF16)


def mm3(table, high, low):
    both = mm(table, high)
    return both[:256] + both[256:] + mm(table[:256], low)


def lane_rows(scratch, ref):
    scratch[...] = jnp.zeros_like(scratch)
    scratch[0:SEC_DEV, 0:PIECES] = ref[...].astype(F32)
    return scratch[0:SEC_DEV, :]


def column(row):
    return jnp.broadcast_to(row, (128, 128)).T


SEND_LANES = 1024
SENDS = FLAT // SEND_LANES
SEND_TILES = SEND_LANES // 128


def tile_of(part, lane_tile):
    return (lane_tile // SEND_TILES * PARTS + part) * SEND_TILES + lane_tile % SEND_TILES


def send_kernel(
    owner_hbm, slot_hbm, blend_hbm, raw_hbm, out_hbm,
    owner_ref, slot_ref, blend_ref, raw_ref, lanes, select, blend, slots, warped, out_ref,
    sems, raw_sems, out_sems,
):
    small = [
        pltpu.make_async_copy(source, target, sems.at[i])
        for i, (source, target) in enumerate(
            [(owner_hbm, owner_ref), (slot_hbm, slot_ref), (blend_hbm, blend_ref)]
        )
    ]
    for copy in small:
        copy.start()
    large = [
        pltpu.make_async_copy(
            raw_hbm.at[:, :, pl.ds(i * SEND_LANES, SEND_LANES)], raw_ref.at[i], raw_sems.at[i]
        )
        for i in range(SENDS)
    ]
    large[0].start()
    for s in range(SEC_DEV):
        for i in range(SENDS):
            warped[i, 128 * s + PIECES : 128 * s + 128, :] = jnp.zeros((32, SEND_LANES), BF16)
    line = lax.broadcasted_iota(jnp.int32, (128, 128), 0)
    lane = lax.broadcasted_iota(jnp.int32, (128, 128), 1)
    lane_id = lax.broadcasted_iota(jnp.int32, (8 * N_XY, 128), 1)
    rows = lax.broadcasted_iota(jnp.int32, (8 * N_XY, 128), 0)
    rows = (rows // 8) * CHUNK + rows % 8
    for copy in small:
        copy.wait()
    large[1].start()
    owners = lane_rows(lanes, owner_ref)
    slot_rows = lane_rows(lanes, slot_ref)
    blend_rows = lane_rows(lanes, blend_ref)
    for s in range(SEC_DEV):
        owner = owners[s : s + 1]
        same = jnp.where((column(owner) == owner) & (line < lane), 1.0, 0.0)
        rank = jnp.sum(same, axis=0, keepdims=True)
        target = (owner * CHUNK + rank + float(s * CAP)).astype(jnp.int32)
        target = jnp.where(lane[0:1] < PIECES, target, -1)
        for j in range(PARTS):
            if s - j in (0, 1):
                at = slice(128 * (s - j), 128 * (s - j) + 128)
                select[j, :, at] = jnp.where(rows + 8 * j == target, 1.0, 0.0).astype(BF16)
        at = slice(128 * s, 128 * s + 128)
        blend[at, :] = column(blend_rows[s : s + 1])
        slots[at, :] = (column(slot_rows[s : s + 1]) + float(s * BLOCK + 1)).astype(BF16)

    ids = [mm(select[j], slots[128 * j : 128 * j + 256, :]) for j in range(PARTS)]
    ids = jnp.where(lane_id == 0, ids[0], jnp.where(lane_id == 1, ids[1], ids[2]))
    out_ref[:, TILES_OUT - 1] = ids.reshape(N_XY, 8, 128).astype(BF16)
    copies = []
    for i in range(SENDS):
        large[i].wait()
        if i == 0:
            large[2].start()
            large[3].start()
        for s in range(SEC_DEV):
            at = slice(128 * s, 128 * s + PIECES)
            scale = blend[at, :]
            for lane_at in range(0, SEND_LANES, 128):
                to = slice(lane_at, lane_at + 128)
                warped[i, at, to] = (raw_ref[i, s, :, to].astype(F32) * scale).astype(BF16)
        for j in range(PARTS):
            value = mm(select[j], warped[i, 128 * j : 128 * j + 256, :])
            for tile in range(SEND_TILES):
                piece = value[:, tile * 128 : tile * 128 + 128].reshape(N_XY, 8, 128)
                out_ref[:, tile_of(j, i * SEND_TILES + tile)] = piece.astype(BF16)
        at = pl.ds(i * PARTS * SEND_TILES, PARTS * SEND_TILES + (i == SENDS - 1))
        copies.append(pltpu.make_async_copy(out_ref.at[:, at], out_hbm.at[:, at], out_sems.at[i]))
        copies[i].start()
    for copy in copies:
        copy.wait()


def send_rows(owner, slot, blend, raw):
    hbm = pl.BlockSpec(memory_space=pltpu.HBM)
    return pl.pallas_call(
        send_kernel,
        out_shape=jax.ShapeDtypeStruct((N_XY, TILES_OUT, 8, 128), BF16),
        in_specs=[hbm, hbm, hbm, hbm],
        out_specs=hbm,
        scratch_shapes=[
            pltpu.VMEM((SEC_DEV, PIECES), jnp.int32),
            pltpu.VMEM((SEC_DEV, PIECES), jnp.int32),
            pltpu.VMEM((SEC_DEV, PIECES), F32),
            pltpu.VMEM((SENDS, SEC_DEV, PIECES, SEND_LANES), BF16),
            pltpu.VMEM((8, 128), F32),
            pltpu.VMEM((PARTS, 8 * N_XY, 256), BF16),
            pltpu.VMEM((KEYS, 128), F32),
            pltpu.VMEM((KEYS, 128), BF16),
            pltpu.VMEM((SENDS, KEYS, SEND_LANES), BF16),
            pltpu.VMEM((N_XY, TILES_OUT, 8, 128), BF16),
            pltpu.SemaphoreType.DMA((3,)),
            pltpu.SemaphoreType.DMA((SENDS,)),
            pltpu.SemaphoreType.DMA((SENDS,)),
        ],
        compiler_params=pltpu.CompilerParams(vmem_limit_bytes=60 * MIB),
    )(owner, slot, blend, raw)


def places(ids, part, count):
    wanted = lax.broadcasted_iota(jnp.int32, (count, 8 * N_XY), 0).astype(F32)
    match = ids[part : part + 1] == wanted + float(part * BLOCK + 1)
    return jnp.where(match, 1.0, 0.0).astype(BF16)


def row_ids(rows_ref):
    return rows_ref[:, TILES_OUT - 1].astype(F32).reshape(8 * N_XY, 128).T


def row_tiles(rows_ref, part, lane, size):
    first = lane // 128
    return jnp.concatenate(
        [
            rows_ref[:, tile_of(part, first + tile)].reshape(8 * N_XY, 128)
            for tile in range(size // 128)
        ],
        axis=1,
    )


def first_kernel(rows_ref, out_ref, place):
    place[...] = places(row_ids(rows_ref), 0, BLOCK)
    for at in range(0, FLAT, 1024):
        out_ref[:, at : at + 1024] = mm(place[...], row_tiles(rows_ref, 0, at, 1024)).astype(BF16)


def first_section(rows):
    return pl.pallas_call(
        first_kernel,
        out_shape=jax.ShapeDtypeStruct((BLOCK, FLAT), BF16),
        in_specs=[VMEM_SPEC],
        out_specs=VMEM_SPEC,
        scratch_shapes=[pltpu.VMEM((BLOCK, 8 * N_XY), BF16)],
        compiler_params=pltpu.CompilerParams(vmem_limit_bytes=8 * MIB),
        cost_estimate=pl.CostEstimate(flops=1 << 28, bytes_accessed=3 << 20, transcendentals=0),
    )(rows)


GROUP = 4
GROUPS = TILES // GROUP


def sublane_sum(value):
    total = value[0:8]
    for row in range(8, value.shape[0], 8):
        total = total + value[row : row + 8]
    return total


ROOT = math.sqrt(2.0)


def cross_rows(own, other, first_step):
    lanes = own.shape[1]
    a, b = (value.reshape(2, 8, 2, 8, lanes) for value in (own, other))
    shape = (8, 8, lanes)
    line = lax.broadcasted_iota(jnp.int32, shape, 1)
    head = (lax.broadcasted_iota(jnp.int32, shape, 0) == 0) & ((line == 0) | (line == 4))
    pair = line < 4
    if first_step < lanes:
        pair = pair & (lax.broadcasted_iota(jnp.int32, shape, 2) < first_step)

    def along_y(p, r):
        b_cosine, b_sine = b[r, :, 0], b[r, :, 1]
        if first_step:
            mixed, b_sine = b_sine, jnp.where(pair, 0.0, b_sine)
            turned = jnp.where(pair, -mixed, b_cosine)
        else:
            turned = b_cosine
        return (
            a[p, :, 0] * b_cosine + a[p, :, 1] * b_sine,
            a[p, :, 0] * b_sine - a[p, :, 1] * turned,
        )

    cc, cs, sc, ss = along_y(0, 0), along_y(0, 1), along_y(1, 0), along_y(1, 1)
    parts = {}
    for y in range(2):
        parts[0, y] = jnp.where(head, ROOT * cc[y], cc[y] + ss[y])
        parts[1, y] = jnp.where(head, ROOT * ss[y], cs[y] - sc[y])
        if first_step:
            for x in range(2):
                parts[x, y] = jnp.where(pair, ROOT * parts[x, y], parts[x, y])
    rows = jnp.stack([jnp.stack([parts[x, y] for y in range(2)], axis=1) for x in range(2)])
    return rows.reshape(256, lanes)


def down(value):
    return jnp.sum(value, axis=0, keepdims=True)


def weighed(table_ref, high):
    both = mm(table_ref[...], high)
    return both[:256] + both[256:]


def flow_sums(operands, third_ref, fourth_ref, high_ref, twice_ref, sums_ref):
    lanes = 128
    total = jnp.zeros((8, 2 * lanes), F32)
    along_x = jnp.zeros((8, 2 * lanes), F32)
    along_y = jnp.zeros((8, 2 * lanes), F32)
    for q in range(0, TILES, 2):
        rows = jnp.concatenate(
            [cross_rows(*operands(q + i), 0 if q + i else lanes) for i in range(2)], axis=1
        )
        high = rows.astype(BF16)
        twice = 2.0 * rows - high.astype(F32)
        total = total + sublane_sum(rows * rows)
        along_x = along_x + sublane_sum(twice * weighed(third_ref, high))
        for i in range(2):
            high_ref[q + i] = high[:, i * lanes : (i + 1) * lanes]
            twice_ref[q + i] = twice[:, i * lanes : (i + 1) * lanes]
    for g in range(0, TILES, 2):
        high, twice = (
            jnp.concatenate(
                [ref[:, 16 * (g + i) : 16 * (g + i) + 16, :].reshape(256, lanes) for i in range(2)],
                axis=1,
            )
            for ref in (high_ref, twice_ref)
        )
        along_y = along_y + sublane_sum(twice * weighed(fourth_ref, high))
    for i, value in enumerate((total, along_x, along_y)):
        sums_ref[i : i + 1, :] = down(value[:, :lanes] + value[:, lanes:])


def turn(value):
    return pltpu.roll(value, BLOCK, 1)


def flow_sums_packed(operands, third_ref, fourth_ref, turned_ref, sums_ref):
    total = jnp.zeros((8, 256), F32)
    along_x = jnp.zeros((8, 256), F32)
    along_y = jnp.zeros((8, 256), F32)
    left = lax.broadcasted_iota(jnp.int32, (8, 16, 128), 2) < BLOCK
    for p in range(0, TILES // 2, 2):
        pieces = [cross_rows(*operands(p + i), 0 if p + i else BLOCK) for i in range(2)]
        for i, piece in enumerate(pieces):
            straight = piece.reshape(8, 2, 16, 128)
            turned = turn(piece).reshape(8, 2, 16, 128)
            turned_ref[:, 2 * (p + i)] = jnp.where(left, straight[:, 0], turned[:, 1])
            turned_ref[:, 2 * (p + i) + 1] = jnp.where(left, turned[:, 0], straight[:, 1])
        rows = jnp.concatenate(pieces, axis=1)
        high = rows.astype(BF16)
        total = total + sublane_sum(rows * rows)
        twice = 2.0 * rows - high.astype(F32)
        along_x = along_x + sublane_sum(twice * weighed(third_ref, high))
    for g in range(0, TILES // 2, 2):
        rows = jnp.concatenate([turned_ref[g + i].reshape(256, 128) for i in range(2)], axis=1)
        high = rows.astype(BF16)
        twice = 2.0 * rows - high.astype(F32)
        along_y = along_y + sublane_sum(twice * weighed(fourth_ref, high))
    for i, value in enumerate((total, along_x, along_y)):
        value = down(value[:, :128] + value[:, 128:])
        sums_ref[i : i + 1, :] = value + turn(value)


def spectrum_kernel(
    rows_ref, first_ref, second_ref, third_ref, fourth_ref, last_ref, square_ref, sums_ref, third_sums_ref,
    place, high, low, own_first, own_second, high_part, twice_part, turned,
):
    ids = row_ids(rows_ref)
    for j in range(PARTS):
        place[j] = places(ids, j, 2 * BLOCK)
    wide = 8 * TILE
    for at in range(0, FLAT, wide):
        pieces, before = [], None
        for j in range(PARTS):
            value = mm(place[j], row_tiles(rows_ref, j, at, wide))
            pieces.append(value[:BLOCK] if before is None else before + value[:BLOCK])
            before = value[BLOCK:]
        patches = jnp.concatenate(pieces + [before], axis=0).astype(BF16)
        for i in range(wide // TILE):
            both = mm(first_ref[...], patches[:, i * TILE : (i + 1) * TILE], NT)
            t = at // TILE + i
            high[t], low[t] = split(both[:256] + both[256:])

    square = jnp.zeros((8, PATCHES), F32)
    for q in range(TILES):
        at = slice(16 * q, 16 * q + 16)
        own = mm3(
            second_ref[...],
            high[:, at, :].reshape(256, PATCHES),
            low[:, at, :].reshape(256, PATCHES),
        )
        if q == 0:
            own = jnp.where(lax.broadcasted_iota(jnp.int32, (256, 1), 0) == 0, 0.0, own)
        square = square + sublane_sum(own * own)
        own_first[q] = own[:, :128]
        own_second[q] = own[:, 128:]
    square_ref[...] = square
    left = lax.broadcasted_iota(jnp.int32, (256, 128), 1) < BLOCK

    def operands(q):
        own = own_first[q]
        return own, jnp.where(left, turn(own), turn(own_second[q]))

    def packed_operands(p):
        even, odd = own_second[2 * p], own_second[2 * p + 1]
        last = jnp.where(left, turn(even), odd)
        last_ref[p] = last
        return jnp.where(left, even, turn(odd)), last

    flow_sums(operands, third_ref, fourth_ref, high_part, twice_part, sums_ref)
    flow_sums_packed(packed_operands, third_ref, fourth_ref, turned, third_sums_ref)


def spectrum(rows, tabs):
    return pl.pallas_call(
        spectrum_kernel,
        out_shape=[
            jax.ShapeDtypeStruct((TILES // 2, 256, 128), F32),
            jax.ShapeDtypeStruct((8, PATCHES), F32),
            jax.ShapeDtypeStruct((8, 128), F32),
            jax.ShapeDtypeStruct((8, 128), F32),
        ],
        in_specs=[VMEM_SPEC] * 5,
        out_specs=[VMEM_SPEC] * 4,
        scratch_shapes=[
            pltpu.VMEM((PARTS, 2 * BLOCK, 8 * N_XY), BF16),
            pltpu.VMEM((TILES, 256, PATCHES), BF16),
            pltpu.VMEM((TILES, 256, PATCHES), BF16),
            pltpu.VMEM((TILES, 256, 128), F32),
            pltpu.VMEM((TILES, 256, 128), F32),
            pltpu.VMEM((TILES, 256, 128), BF16),
            pltpu.VMEM((TILES, 256, 128), F32),
            pltpu.VMEM((TILES // 2, TILES, 16, 128), F32),
        ],
        compiler_params=pltpu.CompilerParams(vmem_limit_bytes=24 * MIB),
        cost_estimate=pl.CostEstimate(
            flops=2 * TILES * 256 * 256 * 11 * 256, bytes_accessed=12 << 20, transcendentals=0
        ),
    )(rows, *tabs)


def next_spectrum(next_ref, first_ref, second_ref, high, low, follow):
    left = lax.broadcasted_iota(jnp.int32, (16, 128), 1) < BLOCK
    for tg in range(GROUPS):
        rows = jnp.concatenate(
            [
                next_ref[:, (GROUP * tg + i) * TILE : (GROUP * tg + i + 1) * TILE]
                for i in range(GROUP)
            ],
            axis=0,
        )
        both = mm(first_ref[...], rows, NT)
        value = both[:256] + both[256:]
        for half in range(2):
            lanes = value[:, half * 128 : half * 128 + 128]
            rolled = pltpu.roll(lanes, BLOCK, 1)
            for pair in range(TILES // 2):
                g, to = pair // 2, (pair % 2) * 128
                even = slice(32 * pair, 32 * pair + 16)
                odd = slice(32 * pair + 16, 32 * pair + 32)
                for i in range(2):
                    t = GROUP * tg + 2 * half + i
                    if i == 0:
                        packed = jnp.where(left, lanes[even], rolled[odd])
                    else:
                        packed = jnp.where(left, rolled[even], lanes[odd])
                    at = slice(16 * t, 16 * t + 16)
                    up, down = split(packed)
                    high[g, at, to : to + 128] = up
                    low[g, at, to : to + 128] = down
    for g in range(GROUPS):
        follow[g] = mm3(second_ref[...], high[g], low[g])
    follow[0, 0:1, 0:BLOCK] = jnp.zeros((1, BLOCK), F32)


def flow_kernel(
    last_ref, square_ref, early_ref, third_sums_ref, next_ref,
    first_ref, second_ref, third_ref, fourth_ref, out_ref,
    next_high, next_low, follow, turned, late,
):
    next_spectrum(next_ref, first_ref, second_ref, next_high, next_low, follow)

    def operands(p):
        return last_ref[p], follow[p // 2, :, (p % 2) * 128 : (p % 2) * 128 + 128]

    flow_sums_packed(operands, third_ref, fourth_ref, turned, late)
    after = jnp.zeros((8, 256), F32)
    for g in range(GROUPS):
        after = after + sublane_sum(follow[g] * follow[g])
    after = after[:, :128] + after[:, 128:]
    after = after + pltpu.roll(after, BLOCK, 1)
    own = square_ref[...]
    low_roll, high_roll = (pltpu.roll(own[:, i : i + 128], BLOCK, 1) for i in (0, 128))
    left = lax.broadcasted_iota(jnp.int32, (8, 128), 1) < BLOCK
    other = jnp.concatenate(
        [jnp.where(left, low_roll, high_roll), jnp.where(left, high_roll, after)], axis=1
    )
    later = jnp.where(left, third_sums_ref[...], late[...])
    total, along_x, along_y = (
        jnp.concatenate([early_ref[i : i + 1, :], later[i : i + 1, :]], axis=1) for i in range(3)
    )
    norm = (down(own) * (1.0 / FLAT) + 1e-05) * (down(other) * (1.0 / FLAT) + 1e-05)
    factor = (1024.0 / (float(FLAT) * float(FLAT))) / norm
    total = jnp.maximum(total * factor, 0.5)
    tile_rows = []
    for value in (along_x * factor / total, along_y * factor / total):
        for half in range(2):
            lane_tile = value[:, half * 128 : half * 128 + 128]
            tile_rows += [lane_tile, pltpu.roll(lane_tile, 64, 1)]
    grid = jnp.concatenate(tile_rows, axis=0)
    lane = lax.broadcasted_iota(jnp.int32, (8, 128), 1)
    for j in range(N_SEC):
        upper = pltpu.roll(grid, (8 - 8 * j) % 128, 1)
        lower = pltpu.roll(grid, (128 - 8 * j) % 128, 1)
        gy = jnp.where(lane < GYW, lane, lane - GYW) + (8 * j - 8)
        window = jnp.where(lane < GYW, upper, lower)
        window = jnp.where((lane < 2 * GYW) & (gy >= 0) & (gy < 32), window, 0.0)
        packed = window[0:4] + pltpu.roll(window, 64, 1)[4:8]
        for b in range(N_XY):
            out_ref[j * N_XY + b] = packed


def flow_windows(own, following, tabs):
    return pl.pallas_call(
        flow_kernel,
        out_shape=jax.ShapeDtypeStruct((N_SEC * N_XY, 4, 128), F32),
        in_specs=[VMEM_SPEC] * 9,
        out_specs=VMEM_SPEC,
        scratch_shapes=[
            pltpu.VMEM((GROUPS, 256, 256), BF16),
            pltpu.VMEM((GROUPS, 256, 256), BF16),
            pltpu.VMEM((GROUPS, 256, 256), F32),
            pltpu.VMEM((TILES // 2, TILES, 16, 128), F32),
            pltpu.VMEM((8, 128), F32),
        ],
        compiler_params=pltpu.CompilerParams(vmem_limit_bytes=24 * MIB),
        cost_estimate=pl.CostEstimate(
            flops=2 * TILES * 256 * 256 * 8 * 256, bytes_accessed=8 << 20, transcendentals=0
        ),
    )(*own, following, *tabs)


def relax_kernel(arrived_ref, out_ref):
    column, block = lax.axis_index("sec"), lax.axis_index("xy")
    lane = lax.broadcasted_iota(jnp.int32, (8, 128), 1)
    lane = jnp.where(lane < 64, lane, lane - 64)
    top = lane < GYW
    gy = jnp.where(top, lane, lane - GYW) + (8 * column - 8)
    inside = (lane < 2 * GYW) & (gy >= 0) & (gy < 32)
    mask = {}
    for o in range(-4, 5):
        valid = (block + o >= 0) & (block + o < N_XY)
        mask[o] = jnp.where(inside & valid, 0.2, 0.0)
    zero = jnp.zeros((8, 128), F32)
    result = []
    for s in range(0, N_SEC, 2):
        flow, mesh = {}, {}
        for o in range(-4, 5):
            at = jnp.clip(block + o, 0, N_XY - 1)
            value = jnp.concatenate(
                [arrived_ref[s * N_XY + at], arrived_ref[(s + 1) * N_XY + at]], axis=0
            )
            flow[o] = value * mask[o]
            mesh[o] = jnp.where(mask[o] > 0.0, value, 0.0)
        for step in range(ITERS):
            reach = (ITERS - step) // 2
            up = {o: pltpu.roll(mesh[o], 128 - GYW, 1) for o in mesh}
            down = {o: pltpu.roll(mesh[o], GYW, 1) for o in mesh}
            new = {}
            for o in range(-reach, reach + 1):
                near = jnp.where(
                    top, up[o] + up.get(o - 1, zero), down[o] + down.get(o + 1, zero)
                )
                near = near + pltpu.roll(mesh[o], 1, 1) + pltpu.roll(mesh[o], 127, 1)
                new[o] = flow[o] + mask[o] * near
            mesh = new
        result.append(mesh[0])
    turned = jnp.concatenate(result + [jnp.zeros((112, 128), F32)], axis=0).T
    for c in range(2):
        for i in range(2):
            at = 64 * c + GYW * i + 8
            out_ref[c, i] = turned[at : at + 8, :15]


def relax(arrived):
    return pl.pallas_call(
        relax_kernel,
        out_shape=jax.ShapeDtypeStruct((2, 2, 8, 15), F32),
        in_specs=[VMEM_SPEC],
        out_specs=pl.BlockSpec(memory_space=pltpu.VMEM),
        compiler_params=pltpu.CompilerParams(vmem_limit_bytes=8 * MIB),
    )(arrived)


def local(raw_pieces, piece_owner, piece_slot, blend):
    tabs = [jnp.asarray(t) for t in tables()]
    outgoing = send_rows(piece_owner[:, :, 0], piece_slot, blend, raw_pieces)
    arrived = lax.all_to_all(outgoing, "xy", split_axis=0, concat_axis=0, tiled=True)
    first = first_section(arrived)
    back = [(i + 1, i) for i in range(N_SEC - 1)]
    following = lax.ppermute(first, "sec", back)
    own = spectrum(arrived, tabs)
    windows = flow_windows(own, following, tabs)
    got = lax.all_to_all(windows, ("sec", "xy"), split_axis=0, concat_axis=0, tiled=True)
    return relax(got).transpose(3, 0, 1, 2)


def solution(mesh):
    in_specs = (P("sec", "xy", None), P("sec", "xy", None), P("sec", "xy"), P("sec", "xy"))
    out_specs = P(None, None, "xy", "sec")
    return jax.shard_map(local, mesh=mesh, in_specs=in_specs, out_specs=out_specs, check_vma=False)
```

```python
import math

import jax
import jax.numpy as jnp
import numpy as np
from jax import lax
from jax.experimental import pallas as pl
from jax.experimental.pallas import tpu as pltpu
from jax.sharding import PartitionSpec as P

PS = 64
FLAT = PS * PS
CAP = 6
N_SEC = 4
N_XY = 32
SEC_DEV = 4
PIECES = 96
BLOCK = 64
ITERS = 8
KEYS = SEC_DEV * 128
CHUNK = SEC_DEV * CAP
LANE_TILES = FLAT // 128
PARTS = CHUNK // 8
TILES_OUT = PARTS * LANE_TILES + 1
PATCHES = SEC_DEV * BLOCK
TILE = 256
TILES = FLAT // TILE
GYW = 24
F32 = jnp.float32
BF16 = jnp.bfloat16
MIB = 1024 * 1024

VMEM_SPEC = pl.BlockSpec(memory_space=pltpu.VMEM)
NT = (((1,), (1,)), ((), ()))
NN = (((1,), (0,)), ((), ()))


def real_basis():
    pos = np.arange(PS)
    rows = np.zeros((2, 32, PS))
    for k in range(32):
        angle = 2.0 * math.pi * ((k * pos) % PS) / PS
        rows[0, k] = np.cos(angle)
        rows[1, k] = np.sin(angle) if k else np.cos(math.pi * pos)
        rows[:, k] *= (math.sqrt(2.0) if k else 1.0) / 8.0
    return rows


def split_table(table):
    high = table.astype(jnp.bfloat16)
    low = (table - high.astype(np.float64)).astype(jnp.bfloat16)
    return np.concatenate([high, low], axis=0)


def tables():
    basis = real_basis()
    by_x = basis.reshape(2, 8, 4, PS)
    by_y = basis.reshape(2, 16, 2, PS)
    two, four = np.eye(2), np.eye(4)
    first = np.einsum("ab,pqky->qpkaby", four, by_y).reshape(256, 256)
    second = np.einsum("pu,kv,cgitb->cgpkituvb", two, two, by_x.reshape(2, 8, 4, 16, 4))
    second = second.reshape(256, 256)
    shift = (np.arange(PS) + 32) % PS - 32
    weigh = np.einsum("pkd,d,rld->pkrl", basis, shift, basis)
    third = np.einsum("pu,kv,cgidhj->cgpkidhuvj", two, two, weigh.reshape(2, 8, 4, 2, 8, 4))
    third = third.reshape(256, 256)
    fourth = np.einsum("ij,pqkurv->qpkiruvj", four, weigh.reshape(2, 16, 2, 2, 16, 2))
    fourth = fourth.reshape(256, 256)
    return [split_table(t) for t in (first, second, third, fourth)]


def mm(a, b, dims=NN):
    return lax.dot_general(a, b, dims, preferred_element_type=F32)


def split(value):
    high = value.astype(BF16)
    return high, (value - high.astype(F32)).astype(BF16)


def mm3(table, high, low):
    both = mm(table, high)
    return both[:256] + both[256:] + mm(table[:256], low)


def lane_rows(scratch, ref):
    scratch[...] = jnp.zeros_like(scratch)
    scratch[0:SEC_DEV, 0:PIECES] = ref[...].astype(F32)
    return scratch[0:SEC_DEV, :]


def column(row):
    return jnp.broadcast_to(row, (128, 128)).T


SEND_LANES = 1024
SENDS = FLAT // SEND_LANES
SEND_TILES = SEND_LANES // 128


def tile_of(part, lane_tile):
    return (lane_tile // SEND_TILES * PARTS + part) * SEND_TILES + lane_tile % SEND_TILES


def send_kernel(
    owner_hbm, slot_hbm, blend_hbm, raw_hbm, out_hbm,
    owner_ref, slot_ref, blend_ref, raw_ref, lanes, select, blend, slots, warped, out_ref,
    sems, raw_sems, out_sems,
):
    small = [
        pltpu.make_async_copy(source, target, sems.at[i])
        for i, (source, target) in enumerate(
            [(owner_hbm, owner_ref), (slot_hbm, slot_ref), (blend_hbm, blend_ref)]
        )
    ]
    for copy in small:
        copy.start()
    large = [
        pltpu.make_async_copy(
            raw_hbm.at[:, :, pl.ds(i * SEND_LANES, SEND_LANES)], raw_ref.at[i], raw_sems.at[i]
        )
        for i in range(SENDS)
    ]
    large[0].start()
    for s in range(SEC_DEV):
        for i in range(SENDS):
            warped[i, 128 * s + PIECES : 128 * s + 128, :] = jnp.zeros((32, SEND_LANES), BF16)
    line = lax.broadcasted_iota(jnp.int32, (128, 128), 0)
    lane = lax.broadcasted_iota(jnp.int32, (128, 128), 1)
    lane_id = lax.broadcasted_iota(jnp.int32, (8 * N_XY, 128), 1)
    rows = lax.broadcasted_iota(jnp.int32, (8 * N_XY, 128), 0)
    rows = (rows // 8) * CHUNK + rows % 8
    for copy in small:
        copy.wait()
    large[1].start()
    owners = lane_rows(lanes, owner_ref)
    slot_rows = lane_rows(lanes, slot_ref)
    blend_rows = lane_rows(lanes, blend_ref)
    for s in range(SEC_DEV):
        owner = owners[s : s + 1]
        same = jnp.where((column(owner) == owner) & (line < lane), 1.0, 0.0)
        rank = jnp.sum(same, axis=0, keepdims=True)
        target = (owner * CHUNK + rank + float(s * CAP)).astype(jnp.int32)
        target = jnp.where(lane[0:1] < PIECES, target, -1)
        for j in range(PARTS):
            if s - j in (0, 1):
                at = slice(128 * (s - j), 128 * (s - j) + 128)
                select[j, :, at] = jnp.where(rows + 8 * j == target, 1.0, 0.0).astype(BF16)
        at = slice(128 * s, 128 * s + 128)
        blend[at, :] = column(blend_rows[s : s + 1])
        slots[at, :] = (column(slot_rows[s : s + 1]) + float(s * BLOCK + 1)).astype(BF16)

    ids = [mm(select[j], slots[128 * j : 128 * j + 256, :]) for j in range(PARTS)]
    ids = jnp.where(lane_id == 0, ids[0], jnp.where(lane_id == 1, ids[1], ids[2]))
    out_ref[:, TILES_OUT - 1] = ids.reshape(N_XY, 8, 128).astype(BF16)
    copies = []

    def leave(first, count):
        at = pl.ds(first, count)
        copies.append(
            pltpu.make_async_copy(out_ref.at[:, at], out_hbm.at[:, at], out_sems.at[len(copies)])
        )
        copies[-1].start()

    for i in range(SENDS):
        large[i].wait()
        if i == 0:
            large[2].start()
            large[3].start()
        for s in range(SEC_DEV):
            at = slice(128 * s, 128 * s + PIECES)
            scale = blend[at, :]
            for lane_at in range(0, SEND_LANES, 128):
                to = slice(lane_at, lane_at + 128)
                warped[i, at, to] = (raw_ref[i, s, :, to].astype(F32) * scale).astype(BF16)
        for j in range(PARTS):
            value = mm(select[j], warped[i, 128 * j : 128 * j + 256, :])
            for tile in range(SEND_TILES):
                piece = value[:, tile * 128 : tile * 128 + 128].reshape(N_XY, 8, 128)
                out_ref[:, tile_of(j, i * SEND_TILES + tile)] = piece.astype(BF16)
            if i == SENDS - 1:
                leave((i * PARTS + j) * SEND_TILES, SEND_TILES + (j == PARTS - 1))
        if i < SENDS - 1:
            leave(i * PARTS * SEND_TILES, PARTS * SEND_TILES)
    for copy in copies:
        copy.wait()


def send_rows(owner, slot, blend, raw):
    hbm = pl.BlockSpec(memory_space=pltpu.HBM)
    return pl.pallas_call(
        send_kernel,
        out_shape=jax.ShapeDtypeStruct((N_XY, TILES_OUT, 8, 128), BF16),
        in_specs=[hbm, hbm, hbm, hbm],
        out_specs=hbm,
        scratch_shapes=[
            pltpu.VMEM((SEC_DEV, PIECES), jnp.int32),
            pltpu.VMEM((SEC_DEV, PIECES), jnp.int32),
            pltpu.VMEM((SEC_DEV, PIECES), F32),
            pltpu.VMEM((SENDS, SEC_DEV, PIECES, SEND_LANES), BF16),
            pltpu.VMEM((8, 128), F32),
            pltpu.VMEM((PARTS, 8 * N_XY, 256), BF16),
            pltpu.VMEM((KEYS, 128), F32),
            pltpu.VMEM((KEYS, 128), BF16),
            pltpu.VMEM((SENDS, KEYS, SEND_LANES), BF16),
            pltpu.VMEM((N_XY, TILES_OUT, 8, 128), BF16),
            pltpu.SemaphoreType.DMA((3,)),
            pltpu.SemaphoreType.DMA((SENDS,)),
            pltpu.SemaphoreType.DMA((SENDS + PARTS - 1,)),
        ],
        compiler_params=pltpu.CompilerParams(vmem_limit_bytes=60 * MIB),
    )(owner, slot, blend, raw)


def places(ids, part, count):
    wanted = lax.broadcasted_iota(jnp.int32, (count, 8 * N_XY), 0).astype(F32)
    match = ids[part : part + 1] == wanted + float(part * BLOCK + 1)
    return jnp.where(match, 1.0, 0.0).astype(BF16)


def row_ids(rows_ref):
    return rows_ref[:, TILES_OUT - 1].astype(F32).reshape(8 * N_XY, 128).T


def row_tiles(rows_ref, part, lane, size):
    first = lane // 128
    return jnp.concatenate(
        [
            rows_ref[:, tile_of(part, first + tile)].reshape(8 * N_XY, 128)
            for tile in range(size // 128)
        ],
        axis=1,
    )


def first_kernel(rows_ref, out_ref, place):
    place[...] = places(row_ids(rows_ref), 0, BLOCK)
    for at in range(0, FLAT, 1024):
        out_ref[:, at : at + 1024] = mm(place[...], row_tiles(rows_ref, 0, at, 1024)).astype(BF16)


def first_section(rows):
    return pl.pallas_call(
        first_kernel,
        out_shape=jax.ShapeDtypeStruct((BLOCK, FLAT), BF16),
        in_specs=[VMEM_SPEC],
        out_specs=VMEM_SPEC,
        scratch_shapes=[pltpu.VMEM((BLOCK, 8 * N_XY), BF16)],
        compiler_params=pltpu.CompilerParams(vmem_limit_bytes=8 * MIB),
        cost_estimate=pl.CostEstimate(flops=1 << 28, bytes_accessed=3 << 20, transcendentals=0),
    )(rows)


GROUP = 4
GROUPS = TILES // GROUP


def sublane_sum(value):
    total = value[0:8]
    for row in range(8, value.shape[0], 8):
        total = total + value[row : row + 8]
    return total


ROOT = math.sqrt(2.0)


def cross_rows(own, other, first_step):
    lanes = own.shape[1]
    a, b = (value.reshape(2, 8, 2, 8, lanes) for value in (own, other))
    shape = (8, 8, lanes)
    line = lax.broadcasted_iota(jnp.int32, shape, 1)
    head = (lax.broadcasted_iota(jnp.int32, shape, 0) == 0) & ((line == 0) | (line == 4))
    pair = line < 4
    if first_step < lanes:
        pair = pair & (lax.broadcasted_iota(jnp.int32, shape, 2) < first_step)

    def along_y(p, r):
        b_cosine, b_sine = b[r, :, 0], b[r, :, 1]
        if first_step:
            mixed, b_sine = b_sine, jnp.where(pair, 0.0, b_sine)
            turned = jnp.where(pair, -mixed, b_cosine)
        else:
            turned = b_cosine
        return (
            a[p, :, 0] * b_cosine + a[p, :, 1] * b_sine,
            a[p, :, 0] * b_sine - a[p, :, 1] * turned,
        )

    cc, cs, sc, ss = along_y(0, 0), along_y(0, 1), along_y(1, 0), along_y(1, 1)
    parts = {}
    for y in range(2):
        parts[0, y] = jnp.where(head, ROOT * cc[y], cc[y] + ss[y])
        parts[1, y] = jnp.where(head, ROOT * ss[y], cs[y] - sc[y])
        if first_step:
            for x in range(2):
                parts[x, y] = jnp.where(pair, ROOT * parts[x, y], parts[x, y])
    rows = jnp.stack([jnp.stack([parts[x, y] for y in range(2)], axis=1) for x in range(2)])
    return rows.reshape(256, lanes)


def down(value):
    return jnp.sum(value, axis=0, keepdims=True)


def weighed(table_ref, high):
    both = mm(table_ref[...], high)
    return both[:256] + both[256:]


def flow_sums(operands, third_ref, fourth_ref, high_ref, twice_ref, sums_ref):
    lanes = 128
    total = jnp.zeros((8, 2 * lanes), F32)
    along_x = jnp.zeros((8, 2 * lanes), F32)
    along_y = jnp.zeros((8, 2 * lanes), F32)
    for q in range(0, TILES, 2):
        rows = jnp.concatenate(
            [cross_rows(*operands(q + i), 0 if q + i else lanes) for i in range(2)], axis=1
        )
        high = rows.astype(BF16)
        twice = 2.0 * rows - high.astype(F32)
        total = total + sublane_sum(rows * rows)
        along_x = along_x + sublane_sum(twice * weighed(third_ref, high))
        for i in range(2):
            high_ref[q + i] = high[:, i * lanes : (i + 1) * lanes]
            twice_ref[q + i] = twice[:, i * lanes : (i + 1) * lanes]
    for g in range(0, TILES, 2):
        high, twice = (
            jnp.concatenate(
                [ref[:, 16 * (g + i) : 16 * (g + i) + 16, :].reshape(256, lanes) for i in range(2)],
                axis=1,
            )
            for ref in (high_ref, twice_ref)
        )
        along_y = along_y + sublane_sum(twice * weighed(fourth_ref, high))
    for i, value in enumerate((total, along_x, along_y)):
        sums_ref[i : i + 1, :] = down(value[:, :lanes] + value[:, lanes:])


def turn(value):
    return pltpu.roll(value, BLOCK, 1)


def flow_sums_packed(operands, third_ref, fourth_ref, turned_ref, sums_ref):
    total = jnp.zeros((8, 256), F32)
    along_x = jnp.zeros((8, 256), F32)
    along_y = jnp.zeros((8, 256), F32)
    left = lax.broadcasted_iota(jnp.int32, (8, 16, 128), 2) < BLOCK
    for p in range(0, TILES // 2, 2):
        pieces = [cross_rows(*operands(p + i), 0 if p + i else BLOCK) for i in range(2)]
        for i, piece in enumerate(pieces):
            straight = piece.reshape(8, 2, 16, 128)
            turned = turn(piece).reshape(8, 2, 16, 128)
            turned_ref[:, 2 * (p + i)] = jnp.where(left, straight[:, 0], turned[:, 1])
            turned_ref[:, 2 * (p + i) + 1] = jnp.where(left, turned[:, 0], straight[:, 1])
        rows = jnp.concatenate(pieces, axis=1)
        high = rows.astype(BF16)
        total = total + sublane_sum(rows * rows)
        twice = 2.0 * rows - high.astype(F32)
        along_x = along_x + sublane_sum(twice * weighed(third_ref, high))
    for g in range(0, TILES // 2, 2):
        rows = jnp.concatenate([turned_ref[g + i].reshape(256, 128) for i in range(2)], axis=1)
        high = rows.astype(BF16)
        twice = 2.0 * rows - high.astype(F32)
        along_y = along_y + sublane_sum(twice * weighed(fourth_ref, high))
    for i, value in enumerate((total, along_x, along_y)):
        value = down(value[:, :128] + value[:, 128:])
        sums_ref[i : i + 1, :] = value + turn(value)


def spectrum_kernel(
    rows_ref, first_ref, second_ref, third_ref, fourth_ref, last_ref, square_ref, sums_ref, third_sums_ref,
    place, high, low, own_first, own_second, high_part, twice_part, turned,
):
    ids = row_ids(rows_ref)
    for j in range(PARTS):
        place[j] = places(ids, j, 2 * BLOCK)
    wide = 8 * TILE
    for at in range(0, FLAT, wide):
        pieces, before = [], None
        for j in range(PARTS):
            value = mm(place[j], row_tiles(rows_ref, j, at, wide))
            pieces.append(value[:BLOCK] if before is None else before + value[:BLOCK])
            before = value[BLOCK:]
        patches = jnp.concatenate(pieces + [before], axis=0).astype(BF16)
        for i in range(wide // TILE):
            both = mm(first_ref[...], patches[:, i * TILE : (i + 1) * TILE], NT)
            t = at // TILE + i
            high[t], low[t] = split(both[:256] + both[256:])

    square = jnp.zeros((8, PATCHES), F32)
    for q in range(TILES):
        at = slice(16 * q, 16 * q + 16)
        own = mm3(
            second_ref[...],
            high[:, at, :].reshape(256, PATCHES),
            low[:, at, :].reshape(256, PATCHES),
        )
        if q == 0:
            own = jnp.where(lax.broadcasted_iota(jnp.int32, (256, 1), 0) == 0, 0.0, own)
        square = square + sublane_sum(own * own)
        own_first[q] = own[:, :128]
        own_second[q] = own[:, 128:]
    square_ref[...] = square
    left = lax.broadcasted_iota(jnp.int32, (256, 128), 1) < BLOCK

    def operands(q):
        own = own_first[q]
        return own, jnp.where(left, turn(own), turn(own_second[q]))

    def packed_operands(p):
        even, odd = own_second[2 * p], own_second[2 * p + 1]
        last = jnp.where(left, turn(even), odd)
        last_ref[p] = last
        return jnp.where(left, even, turn(odd)), last

    flow_sums(operands, third_ref, fourth_ref, high_part, twice_part, sums_ref)
    flow_sums_packed(packed_operands, third_ref, fourth_ref, turned, third_sums_ref)


def spectrum(rows, tabs):
    return pl.pallas_call(
        spectrum_kernel,
        out_shape=[
            jax.ShapeDtypeStruct((TILES // 2, 256, 128), F32),
            jax.ShapeDtypeStruct((8, PATCHES), F32),
            jax.ShapeDtypeStruct((8, 128), F32),
            jax.ShapeDtypeStruct((8, 128), F32),
        ],
        in_specs=[VMEM_SPEC] * 5,
        out_specs=[VMEM_SPEC] * 4,
        scratch_shapes=[
            pltpu.VMEM((PARTS, 2 * BLOCK, 8 * N_XY), BF16),
            pltpu.VMEM((TILES, 256, PATCHES), BF16),
            pltpu.VMEM((TILES, 256, PATCHES), BF16),
            pltpu.VMEM((TILES, 256, 128), F32),
            pltpu.VMEM((TILES, 256, 128), F32),
            pltpu.VMEM((TILES, 256, 128), BF16),
            pltpu.VMEM((TILES, 256, 128), F32),
            pltpu.VMEM((TILES // 2, TILES, 16, 128), F32),
        ],
        compiler_params=pltpu.CompilerParams(vmem_limit_bytes=24 * MIB),
        cost_estimate=pl.CostEstimate(
            flops=2 * TILES * 256 * 256 * 11 * 256, bytes_accessed=12 << 20, transcendentals=0
        ),
    )(rows, *tabs)


def next_spectrum(next_ref, first_ref, second_ref, high, low, follow):
    left = lax.broadcasted_iota(jnp.int32, (16, 128), 1) < BLOCK
    for tg in range(GROUPS):
        rows = jnp.concatenate(
            [
                next_ref[:, (GROUP * tg + i) * TILE : (GROUP * tg + i + 1) * TILE]
                for i in range(GROUP)
            ],
            axis=0,
        )
        both = mm(first_ref[...], rows, NT)
        value = both[:256] + both[256:]
        for half in range(2):
            lanes = value[:, half * 128 : half * 128 + 128]
            rolled = pltpu.roll(lanes, BLOCK, 1)
            for pair in range(TILES // 2):
                g, to = pair // 2, (pair % 2) * 128
                even = slice(32 * pair, 32 * pair + 16)
                odd = slice(32 * pair + 16, 32 * pair + 32)
                for i in range(2):
                    t = GROUP * tg + 2 * half + i
                    if i == 0:
                        packed = jnp.where(left, lanes[even], rolled[odd])
                    else:
                        packed = jnp.where(left, rolled[even], lanes[odd])
                    at = slice(16 * t, 16 * t + 16)
                    up, down = split(packed)
                    high[g, at, to : to + 128] = up
                    low[g, at, to : to + 128] = down
    for g in range(GROUPS):
        follow[g] = mm3(second_ref[...], high[g], low[g])
    follow[0, 0:1, 0:BLOCK] = jnp.zeros((1, BLOCK), F32)


def flow_kernel(
    last_ref, square_ref, early_ref, third_sums_ref, next_ref,
    first_ref, second_ref, third_ref, fourth_ref, out_ref,
    next_high, next_low, follow, turned, late,
):
    next_spectrum(next_ref, first_ref, second_ref, next_high, next_low, follow)

    def operands(p):
        return last_ref[p], follow[p // 2, :, (p % 2) * 128 : (p % 2) * 128 + 128]

    flow_sums_packed(operands, third_ref, fourth_ref, turned, late)
    after = jnp.zeros((8, 256), F32)
    for g in range(GROUPS):
        after = after + sublane_sum(follow[g] * follow[g])
    after = after[:, :128] + after[:, 128:]
    after = after + pltpu.roll(after, BLOCK, 1)
    own = square_ref[...]
    low_roll, high_roll = (pltpu.roll(own[:, i : i + 128], BLOCK, 1) for i in (0, 128))
    left = lax.broadcasted_iota(jnp.int32, (8, 128), 1) < BLOCK
    other = jnp.concatenate(
        [jnp.where(left, low_roll, high_roll), jnp.where(left, high_roll, after)], axis=1
    )
    later = jnp.where(left, third_sums_ref[...], late[...])
    total, along_x, along_y = (
        jnp.concatenate([early_ref[i : i + 1, :], later[i : i + 1, :]], axis=1) for i in range(3)
    )
    norm = (down(own) * (1.0 / FLAT) + 1e-05) * (down(other) * (1.0 / FLAT) + 1e-05)
    factor = (1024.0 / (float(FLAT) * float(FLAT))) / norm
    total = jnp.maximum(total * factor, 0.5)
    tile_rows = []
    for value in (along_x * factor / total, along_y * factor / total):
        for half in range(2):
            lane_tile = value[:, half * 128 : half * 128 + 128]
            tile_rows += [lane_tile, pltpu.roll(lane_tile, 64, 1)]
    grid = jnp.concatenate(tile_rows, axis=0)
    lane = lax.broadcasted_iota(jnp.int32, (8, 128), 1)
    for j in range(N_SEC):
        upper = pltpu.roll(grid, (8 - 8 * j) % 128, 1)
        lower = pltpu.roll(grid, (128 - 8 * j) % 128, 1)
        gy = jnp.where(lane < GYW, lane, lane - GYW) + (8 * j - 8)
        window = jnp.where(lane < GYW, upper, lower)
        window = jnp.where((lane < 2 * GYW) & (gy >= 0) & (gy < 32), window, 0.0)
        packed = window[0:4] + pltpu.roll(window, 64, 1)[4:8]
        for b in range(N_XY):
            out_ref[j * N_XY + b] = packed


def flow_windows(own, following, tabs):
    return pl.pallas_call(
        flow_kernel,
        out_shape=jax.ShapeDtypeStruct((N_SEC * N_XY, 4, 128), F32),
        in_specs=[VMEM_SPEC] * 9,
        out_specs=VMEM_SPEC,
        scratch_shapes=[
            pltpu.VMEM((GROUPS, 256, 256), BF16),
            pltpu.VMEM((GROUPS, 256, 256), BF16),
            pltpu.VMEM((GROUPS, 256, 256), F32),
            pltpu.VMEM((TILES // 2, TILES, 16, 128), F32),
            pltpu.VMEM((8, 128), F32),
        ],
        compiler_params=pltpu.CompilerParams(vmem_limit_bytes=24 * MIB),
        cost_estimate=pl.CostEstimate(
            flops=2 * TILES * 256 * 256 * 8 * 256, bytes_accessed=8 << 20, transcendentals=0
        ),
    )(*own, following, *tabs)


def relax_kernel(arrived_ref, out_ref):
    column, block = lax.axis_index("sec"), lax.axis_index("xy")
    lane = lax.broadcasted_iota(jnp.int32, (8, 128), 1)
    lane = jnp.where(lane < 64, lane, lane - 64)
    top = lane < GYW
    gy = jnp.where(top, lane, lane - GYW) + (8 * column - 8)
    inside = (lane < 2 * GYW) & (gy >= 0) & (gy < 32)
    mask = {}
    for o in range(-4, 5):
        valid = (block + o >= 0) & (block + o < N_XY)
        mask[o] = jnp.where(inside & valid, 0.2, 0.0)
    zero = jnp.zeros((8, 128), F32)
    result = []
    for s in range(0, N_SEC, 2):
        flow, mesh = {}, {}
        for o in range(-4, 5):
            at = jnp.clip(block + o, 0, N_XY - 1)
            value = jnp.concatenate(
                [arrived_ref[s * N_XY + at], arrived_ref[(s + 1) * N_XY + at]], axis=0
            )
            flow[o] = value * mask[o]
            mesh[o] = jnp.where(mask[o] > 0.0, value, 0.0)
        for step in range(ITERS):
            reach = (ITERS - step) // 2
            up = {o: pltpu.roll(mesh[o], 128 - GYW, 1) for o in mesh}
            down = {o: pltpu.roll(mesh[o], GYW, 1) for o in mesh}
            new = {}
            for o in range(-reach, reach + 1):
                near = jnp.where(
                    top, up[o] + up.get(o - 1, zero), down[o] + down.get(o + 1, zero)
                )
                near = near + pltpu.roll(mesh[o], 1, 1) + pltpu.roll(mesh[o], 127, 1)
                new[o] = flow[o] + mask[o] * near
            mesh = new
        result.append(mesh[0])
    turned = jnp.concatenate(result + [jnp.zeros((112, 128), F32)], axis=0).T
    for c in range(2):
        for i in range(2):
            at = 64 * c + GYW * i + 8
            out_ref[c, i] = turned[at : at + 8, :15]


def relax(arrived):
    return pl.pallas_call(
        relax_kernel,
        out_shape=jax.ShapeDtypeStruct((2, 2, 8, 15), F32),
        in_specs=[VMEM_SPEC],
        out_specs=pl.BlockSpec(memory_space=pltpu.VMEM),
        compiler_params=pltpu.CompilerParams(vmem_limit_bytes=8 * MIB),
    )(arrived)


def local(raw_pieces, piece_owner, piece_slot, blend):
    tabs = [jnp.asarray(t) for t in tables()]
    outgoing = send_rows(piece_owner[:, :, 0], piece_slot, blend, raw_pieces)
    arrived = lax.all_to_all(outgoing, "xy", split_axis=0, concat_axis=0, tiled=True)
    first = first_section(arrived)
    back = [(i + 1, i) for i in range(N_SEC - 1)]
    following = lax.ppermute(first, "sec", back)
    own = spectrum(arrived, tabs)
    windows = flow_windows(own, following, tabs)
    got = lax.all_to_all(windows, ("sec", "xy"), split_axis=0, concat_axis=0, tiled=True)
    return relax(got).transpose(3, 0, 1, 2)


def solution(mesh):
    in_specs = (P("sec", "xy", None), P("sec", "xy", None), P("sec", "xy"), P("sec", "xy"))
    out_specs = P(None, None, "xy", "sec")
    return jax.shard_map(local, mesh=mesh, in_specs=in_specs, out_specs=out_specs, check_vma=False)
```

```python
import math

import jax
import jax.numpy as jnp
import numpy as np
from jax import lax
from jax.experimental import pallas as pl
from jax.experimental.pallas import tpu as pltpu
from jax.sharding import PartitionSpec as P

PS = 64
FLAT = PS * PS
CAP = 6
N_SEC = 4
N_XY = 32
SEC_DEV = 4
PIECES = 96
BLOCK = 64
ITERS = 8
KEYS = SEC_DEV * 128
CHUNK = SEC_DEV * CAP
LANE_TILES = FLAT // 128
PARTS = CHUNK // 8
TILES_OUT = PARTS * LANE_TILES + 1
PATCHES = SEC_DEV * BLOCK
TILE = 256
TILES = FLAT // TILE
GYW = 24
F32 = jnp.float32
BF16 = jnp.bfloat16
MIB = 1024 * 1024

VMEM_SPEC = pl.BlockSpec(memory_space=pltpu.VMEM)
NT = (((1,), (1,)), ((), ()))
NN = (((1,), (0,)), ((), ()))


def real_basis():
    pos = np.arange(PS)
    rows = np.zeros((2, 32, PS))
    for k in range(32):
        angle = 2.0 * math.pi * ((k * pos) % PS) / PS
        rows[0, k] = np.cos(angle)
        rows[1, k] = np.sin(angle) if k else np.cos(math.pi * pos)
        rows[:, k] *= (math.sqrt(2.0) if k else 1.0) / 8.0
    return rows


def split_table(table):
    high = table.astype(jnp.bfloat16)
    low = (table - high.astype(np.float64)).astype(jnp.bfloat16)
    return np.concatenate([high, low], axis=0)


def tables():
    basis = real_basis()
    by_x = basis.reshape(2, 8, 4, PS)
    by_y = basis.reshape(2, 16, 2, PS)
    two, four = np.eye(2), np.eye(4)
    first = np.einsum("ab,pqky->qpkaby", four, by_y).reshape(256, 256)
    second = np.einsum("pu,kv,cgitb->cgpkituvb", two, two, by_x.reshape(2, 8, 4, 16, 4))
    second = second.reshape(256, 256)
    shift = (np.arange(PS) + 32) % PS - 32
    weigh = np.einsum("pkd,d,rld->pkrl", basis, shift, basis)
    third = np.einsum("pu,kv,cgidhj->cgpkidhuvj", two, two, weigh.reshape(2, 8, 4, 2, 8, 4))
    third = third.reshape(256, 256)
    fourth = np.einsum("ij,pqkurv->qpkiruvj", four, weigh.reshape(2, 16, 2, 2, 16, 2))
    fourth = fourth.reshape(256, 256)
    return [split_table(t) for t in (first, second, third, fourth)]


def mm(a, b, dims=NN):
    return lax.dot_general(a, b, dims, preferred_element_type=F32)


def split(value):
    high = value.astype(BF16)
    return high, (value - high.astype(F32)).astype(BF16)


def mm3(table, high, low):
    both = mm(table, high)
    return both[:256] + both[256:] + mm(table[:256], low)


def lane_rows(scratch, ref):
    scratch[...] = jnp.zeros_like(scratch)
    scratch[0:SEC_DEV, 0:PIECES] = ref[...].astype(F32)
    return scratch[0:SEC_DEV, :]


def column(row):
    return jnp.broadcast_to(row, (128, 128)).T


SEND_LANES = 1024
SENDS = FLAT // SEND_LANES
SEND_TILES = SEND_LANES // 128


def tile_of(part, lane_tile):
    return (lane_tile // SEND_TILES * PARTS + part) * SEND_TILES + lane_tile % SEND_TILES


def send_kernel(
    owner_hbm, slot_hbm, blend_hbm, raw_hbm, out_hbm,
    owner_ref, slot_ref, blend_ref, raw_ref, lanes, select, blend, slots, warped, out_ref,
    sems, raw_sems, out_sems,
):
    small = [
        pltpu.make_async_copy(source, target, sems.at[i])
        for i, (source, target) in enumerate(
            [(owner_hbm, owner_ref), (slot_hbm, slot_ref), (blend_hbm, blend_ref)]
        )
    ]
    for copy in small:
        copy.start()
    large = [
        pltpu.make_async_copy(
            raw_hbm.at[:, :, pl.ds(i * SEND_LANES, SEND_LANES)], raw_ref.at[i], raw_sems.at[i]
        )
        for i in range(SENDS)
    ]
    large[0].start()
    for s in range(SEC_DEV):
        for i in range(SENDS):
            warped[i, 128 * s + PIECES : 128 * s + 128, :] = jnp.zeros((32, SEND_LANES), BF16)
    line = lax.broadcasted_iota(jnp.int32, (128, 128), 0)
    lane = lax.broadcasted_iota(jnp.int32, (128, 128), 1)
    lane_id = lax.broadcasted_iota(jnp.int32, (8 * N_XY, 128), 1)
    rows = lax.broadcasted_iota(jnp.int32, (8 * N_XY, 128), 0)
    rows = (rows // 8) * CHUNK + rows % 8
    for copy in small:
        copy.wait()
    large[1].start()
    owners = lane_rows(lanes, owner_ref)
    slot_rows = lane_rows(lanes, slot_ref)
    blend_rows = lane_rows(lanes, blend_ref)
    for s in range(SEC_DEV):
        owner = owners[s : s + 1]
        same = jnp.where((column(owner) == owner) & (line < lane), 1.0, 0.0)
        rank = jnp.sum(same, axis=0, keepdims=True)
        target = (owner * CHUNK + rank + float(s * CAP)).astype(jnp.int32)
        target = jnp.where(lane[0:1] < PIECES, target, -1)
        for j in range(PARTS):
            if s - j in (0, 1):
                at = slice(128 * (s - j), 128 * (s - j) + 128)
                select[j, :, at] = jnp.where(rows + 8 * j == target, 1.0, 0.0).astype(BF16)
        at = slice(128 * s, 128 * s + 128)
        blend[at, :] = column(blend_rows[s : s + 1])
        slots[at, :] = (column(slot_rows[s : s + 1]) + float(s * BLOCK + 1)).astype(BF16)

    ids = [mm(select[j], slots[128 * j : 128 * j + 256, :]) for j in range(PARTS)]
    ids = jnp.where(lane_id == 0, ids[0], jnp.where(lane_id == 1, ids[1], ids[2]))
    out_ref[:, TILES_OUT - 1] = ids.reshape(N_XY, 8, 128).astype(BF16)
    copies = []

    def leave(first, count):
        at = pl.ds(first, count)
        copies.append(
            pltpu.make_async_copy(out_ref.at[:, at], out_hbm.at[:, at], out_sems.at[len(copies)])
        )
        copies[-1].start()

    for i in range(SENDS):
        large[i].wait()
        if i == 0:
            large[2].start()
            large[3].start()
        for s in range(SEC_DEV):
            at = slice(128 * s, 128 * s + PIECES)
            scale = blend[at, :]
            for lane_at in range(0, SEND_LANES, 128):
                to = slice(lane_at, lane_at + 128)
                warped[i, at, to] = (raw_ref[i, s, :, to].astype(F32) * scale).astype(BF16)
        for j in range(PARTS):
            value = mm(select[j], warped[i, 128 * j : 128 * j + 256, :])
            for tile in range(SEND_TILES):
                piece = value[:, tile * 128 : tile * 128 + 128].reshape(N_XY, 8, 128)
                out_ref[:, tile_of(j, i * SEND_TILES + tile)] = piece.astype(BF16)
            if i == SENDS - 1:
                leave((i * PARTS + j) * SEND_TILES, SEND_TILES + (j == PARTS - 1))
        if i < SENDS - 1:
            leave(i * PARTS * SEND_TILES, PARTS * SEND_TILES)
    for copy in copies:
        copy.wait()


def send_rows(owner, slot, blend, raw):
    hbm = pl.BlockSpec(memory_space=pltpu.HBM)
    return pl.pallas_call(
        send_kernel,
        out_shape=jax.ShapeDtypeStruct((N_XY, TILES_OUT, 8, 128), BF16),
        in_specs=[hbm, hbm, hbm, hbm],
        out_specs=hbm,
        scratch_shapes=[
            pltpu.VMEM((SEC_DEV, PIECES), jnp.int32),
            pltpu.VMEM((SEC_DEV, PIECES), jnp.int32),
            pltpu.VMEM((SEC_DEV, PIECES), F32),
            pltpu.VMEM((SENDS, SEC_DEV, PIECES, SEND_LANES), BF16),
            pltpu.VMEM((8, 128), F32),
            pltpu.VMEM((PARTS, 8 * N_XY, 256), BF16),
            pltpu.VMEM((KEYS, 128), F32),
            pltpu.VMEM((KEYS, 128), BF16),
            pltpu.VMEM((SENDS, KEYS, SEND_LANES), BF16),
            pltpu.VMEM((N_XY, TILES_OUT, 8, 128), BF16),
            pltpu.SemaphoreType.DMA((3,)),
            pltpu.SemaphoreType.DMA((SENDS,)),
            pltpu.SemaphoreType.DMA((SENDS + PARTS - 1,)),
        ],
        compiler_params=pltpu.CompilerParams(vmem_limit_bytes=60 * MIB),
    )(owner, slot, blend, raw)


def places(ids, part, count):
    wanted = lax.broadcasted_iota(jnp.int32, (count, 8 * N_XY), 0).astype(F32)
    match = ids[part : part + 1] == wanted + float(part * BLOCK + 1)
    return jnp.where(match, 1.0, 0.0).astype(BF16)


def row_ids(rows_ref):
    return rows_ref[:, TILES_OUT - 1].astype(F32).reshape(8 * N_XY, 128).T


def row_tiles(rows_ref, part, lane, size):
    first = lane // 128
    return jnp.concatenate(
        [
            rows_ref[:, tile_of(part, first + tile)].reshape(8 * N_XY, 128)
            for tile in range(size // 128)
        ],
        axis=1,
    )


def first_kernel(rows_ref, out_ref, place):
    place[...] = places(row_ids(rows_ref), 0, BLOCK)
    for at in range(0, FLAT, 1024):
        out_ref[:, at : at + 1024] = mm(place[...], row_tiles(rows_ref, 0, at, 1024)).astype(BF16)


def first_section(rows):
    return pl.pallas_call(
        first_kernel,
        out_shape=jax.ShapeDtypeStruct((BLOCK, FLAT), BF16),
        in_specs=[VMEM_SPEC],
        out_specs=VMEM_SPEC,
        scratch_shapes=[pltpu.VMEM((BLOCK, 8 * N_XY), BF16)],
        compiler_params=pltpu.CompilerParams(vmem_limit_bytes=8 * MIB),
        cost_estimate=pl.CostEstimate(flops=1 << 28, bytes_accessed=3 << 20, transcendentals=0),
    )(rows)


GROUP = 4
GROUPS = TILES // GROUP


def sublane_sum(value):
    total = value[0:8]
    for row in range(8, value.shape[0], 8):
        total = total + value[row : row + 8]
    return total


ROOT = math.sqrt(2.0)


def cross_rows(own, other, first_step):
    lanes = own.shape[1]
    a, b = (value.reshape(2, 8, 2, 8, lanes) for value in (own, other))
    shape = (8, 8, lanes)
    line = lax.broadcasted_iota(jnp.int32, shape, 1)
    head = (lax.broadcasted_iota(jnp.int32, shape, 0) == 0) & ((line == 0) | (line == 4))
    pair = line < 4
    if first_step < lanes:
        pair = pair & (lax.broadcasted_iota(jnp.int32, shape, 2) < first_step)

    def along_y(p, r):
        b_cosine, b_sine = b[r, :, 0], b[r, :, 1]
        if first_step:
            mixed, b_sine = b_sine, jnp.where(pair, 0.0, b_sine)
            turned = jnp.where(pair, -mixed, b_cosine)
        else:
            turned = b_cosine
        return (
            a[p, :, 0] * b_cosine + a[p, :, 1] * b_sine,
            a[p, :, 0] * b_sine - a[p, :, 1] * turned,
        )

    cc, cs, sc, ss = along_y(0, 0), along_y(0, 1), along_y(1, 0), along_y(1, 1)
    parts = {}
    for y in range(2):
        parts[0, y] = jnp.where(head, ROOT * cc[y], cc[y] + ss[y])
        parts[1, y] = jnp.where(head, ROOT * ss[y], cs[y] - sc[y])
        if first_step:
            for x in range(2):
                parts[x, y] = jnp.where(pair, ROOT * parts[x, y], parts[x, y])
    rows = jnp.stack([jnp.stack([parts[x, y] for y in range(2)], axis=1) for x in range(2)])
    return rows.reshape(256, lanes)


def down(value):
    return jnp.sum(value, axis=0, keepdims=True)


def weighed(table_ref, high):
    both = mm(table_ref[...], high)
    return both[:256] + both[256:]


def flow_sums(operands, third_ref, fourth_ref, high_ref, twice_ref, sums_ref):
    lanes = 128
    total = jnp.zeros((8, 2 * lanes), F32)
    along_x = jnp.zeros((8, 2 * lanes), F32)
    along_y = jnp.zeros((8, 2 * lanes), F32)
    for q in range(0, TILES, 2):
        rows = jnp.concatenate(
            [cross_rows(*operands(q + i), 0 if q + i else lanes) for i in range(2)], axis=1
        )
        high = rows.astype(BF16)
        twice = 2.0 * rows - high.astype(F32)
        total = total + sublane_sum(rows * rows)
        along_x = along_x + sublane_sum(twice * weighed(third_ref, high))
        for i in range(2):
            high_ref[q + i] = high[:, i * lanes : (i + 1) * lanes]
            twice_ref[q + i] = twice[:, i * lanes : (i + 1) * lanes]
    for g in range(0, TILES, 2):
        high, twice = (
            jnp.concatenate(
                [ref[:, 16 * (g + i) : 16 * (g + i) + 16, :].reshape(256, lanes) for i in range(2)],
                axis=1,
            )
            for ref in (high_ref, twice_ref)
        )
        along_y = along_y + sublane_sum(twice * weighed(fourth_ref, high))
    for i, value in enumerate((total, along_x, along_y)):
        sums_ref[i : i + 1, :] = down(value[:, :lanes] + value[:, lanes:])


def turn(value):
    return pltpu.roll(value, BLOCK, 1)


def flow_sums_packed(operands, third_ref, fourth_ref, turned_ref, sums_ref):
    total = jnp.zeros((8, 256), F32)
    along_x = jnp.zeros((8, 256), F32)
    along_y = jnp.zeros((8, 256), F32)
    left = lax.broadcasted_iota(jnp.int32, (8, 16, 128), 2) < BLOCK
    for p in range(0, TILES // 2, 2):
        pieces = [cross_rows(*operands(p + i), 0 if p + i else BLOCK) for i in range(2)]
        for i, piece in enumerate(pieces):
            straight = piece.reshape(8, 2, 16, 128)
            turned = turn(piece).reshape(8, 2, 16, 128)
            turned_ref[:, 2 * (p + i)] = jnp.where(left, straight[:, 0], turned[:, 1])
            turned_ref[:, 2 * (p + i) + 1] = jnp.where(left, turned[:, 0], straight[:, 1])
        rows = jnp.concatenate(pieces, axis=1)
        high = rows.astype(BF16)
        total = total + sublane_sum(rows * rows)
        twice = 2.0 * rows - high.astype(F32)
        along_x = along_x + sublane_sum(twice * weighed(third_ref, high))
    for g in range(0, TILES // 2, 2):
        rows = jnp.concatenate([turned_ref[g + i].reshape(256, 128) for i in range(2)], axis=1)
        high = rows.astype(BF16)
        twice = 2.0 * rows - high.astype(F32)
        along_y = along_y + sublane_sum(twice * weighed(fourth_ref, high))
    for i, value in enumerate((total, along_x, along_y)):
        value = down(value[:, :128] + value[:, 128:])
        sums_ref[i : i + 1, :] = value + turn(value)


def spectrum_kernel(
    rows_ref, first_ref, second_ref, third_ref, fourth_ref, last_ref, square_ref, sums_ref, third_sums_ref,
    place, high, low, own_first, own_second, high_part, twice_part, turned,
):
    ids = row_ids(rows_ref)
    for j in range(PARTS):
        place[j] = places(ids, j, 2 * BLOCK)
    wide = 8 * TILE
    for at in range(0, FLAT, wide):
        pieces, before = [], None
        for j in range(PARTS):
            value = mm(place[j], row_tiles(rows_ref, j, at, wide))
            pieces.append(value[:BLOCK] if before is None else before + value[:BLOCK])
            before = value[BLOCK:]
        patches = jnp.concatenate(pieces + [before], axis=0).astype(BF16)
        for i in range(wide // TILE):
            both = mm(first_ref[...], patches[:, i * TILE : (i + 1) * TILE], NT)
            t = at // TILE + i
            high[t], low[t] = split(both[:256] + both[256:])

    square = jnp.zeros((8, PATCHES), F32)
    for q in range(TILES):
        at = slice(16 * q, 16 * q + 16)
        own = mm3(
            second_ref[...],
            high[:, at, :].reshape(256, PATCHES),
            low[:, at, :].reshape(256, PATCHES),
        )
        if q == 0:
            own = jnp.where(lax.broadcasted_iota(jnp.int32, (256, 1), 0) == 0, 0.0, own)
        square = square + sublane_sum(own * own)
        own_first[q] = own[:, :128]
        own_second[q] = own[:, 128:]
    square_ref[...] = square
    left = lax.broadcasted_iota(jnp.int32, (256, 128), 1) < BLOCK

    def operands(q):
        own = own_first[q]
        return own, jnp.where(left, turn(own), turn(own_second[q]))

    def packed_operands(p):
        even, odd = own_second[2 * p], own_second[2 * p + 1]
        last = jnp.where(left, turn(even), odd)
        last_ref[p] = last
        return jnp.where(left, even, turn(odd)), last

    flow_sums(operands, third_ref, fourth_ref, high_part, twice_part, sums_ref)
    flow_sums_packed(packed_operands, third_ref, fourth_ref, turned, third_sums_ref)


def spectrum(rows, tabs):
    return pl.pallas_call(
        spectrum_kernel,
        out_shape=[
            jax.ShapeDtypeStruct((TILES // 2, 256, 128), F32),
            jax.ShapeDtypeStruct((8, PATCHES), F32),
            jax.ShapeDtypeStruct((8, 128), F32),
            jax.ShapeDtypeStruct((8, 128), F32),
        ],
        in_specs=[VMEM_SPEC] * 5,
        out_specs=[VMEM_SPEC] * 4,
        scratch_shapes=[
            pltpu.VMEM((PARTS, 2 * BLOCK, 8 * N_XY), BF16),
            pltpu.VMEM((TILES, 256, PATCHES), BF16),
            pltpu.VMEM((TILES, 256, PATCHES), BF16),
            pltpu.VMEM((TILES, 256, 128), F32),
            pltpu.VMEM((TILES, 256, 128), F32),
            pltpu.VMEM((TILES, 256, 128), BF16),
            pltpu.VMEM((TILES, 256, 128), F32),
            pltpu.VMEM((TILES // 2, TILES, 16, 128), F32),
        ],
        compiler_params=pltpu.CompilerParams(vmem_limit_bytes=24 * MIB),
        cost_estimate=pl.CostEstimate(
            flops=2 * TILES * 256 * 256 * 11 * 256, bytes_accessed=12 << 20, transcendentals=0
        ),
    )(rows, *tabs)


def next_spectrum(next_ref, first_ref, second_ref, high, low, follow):
    left = lax.broadcasted_iota(jnp.int32, (16, 128), 1) < BLOCK
    for tg in range(GROUPS):
        rows = jnp.concatenate(
            [
                next_ref[:, (GROUP * tg + i) * TILE : (GROUP * tg + i + 1) * TILE]
                for i in range(GROUP)
            ],
            axis=0,
        )
        both = mm(first_ref[...], rows, NT)
        value = both[:256] + both[256:]
        for half in range(2):
            lanes = value[:, half * 128 : half * 128 + 128]
            rolled = pltpu.roll(lanes, BLOCK, 1)
            for pair in range(TILES // 2):
                g, to = pair // 2, (pair % 2) * 128
                even = slice(32 * pair, 32 * pair + 16)
                odd = slice(32 * pair + 16, 32 * pair + 32)
                for i in range(2):
                    t = GROUP * tg + 2 * half + i
                    if i == 0:
                        packed = jnp.where(left, lanes[even], rolled[odd])
                    else:
                        packed = jnp.where(left, rolled[even], lanes[odd])
                    at = slice(16 * t, 16 * t + 16)
                    up, down = split(packed)
                    high[g, at, to : to + 128] = up
                    low[g, at, to : to + 128] = down
    for g in range(GROUPS):
        follow[g] = mm3(second_ref[...], high[g], low[g])
    follow[0, 0:1, 0:BLOCK] = jnp.zeros((1, BLOCK), F32)


def flow_kernel(
    last_ref, square_ref, early_ref, third_sums_ref, next_ref,
    first_ref, second_ref, third_ref, fourth_ref, out_ref,
    next_high, next_low, follow, turned, late,
):
    next_spectrum(next_ref, first_ref, second_ref, next_high, next_low, follow)

    def operands(p):
        return last_ref[p], follow[p // 2, :, (p % 2) * 128 : (p % 2) * 128 + 128]

    flow_sums_packed(operands, third_ref, fourth_ref, turned, late)
    after = jnp.zeros((8, 256), F32)
    for g in range(GROUPS):
        after = after + sublane_sum(follow[g] * follow[g])
    after = after[:, :128] + after[:, 128:]
    after = after + pltpu.roll(after, BLOCK, 1)
    own = square_ref[...]
    low_roll, high_roll = (pltpu.roll(own[:, i : i + 128], BLOCK, 1) for i in (0, 128))
    left = lax.broadcasted_iota(jnp.int32, (8, 128), 1) < BLOCK
    other = jnp.concatenate(
        [jnp.where(left, low_roll, high_roll), jnp.where(left, high_roll, after)], axis=1
    )
    later = jnp.where(left, third_sums_ref[...], late[...])
    total, along_x, along_y = (
        jnp.concatenate([early_ref[i : i + 1, :], later[i : i + 1, :]], axis=1) for i in range(3)
    )
    norm = (down(own) * (1.0 / FLAT) + 1e-05) * (down(other) * (1.0 / FLAT) + 1e-05)
    factor = (1024.0 / (float(FLAT) * float(FLAT))) / norm
    total = jnp.maximum(total * factor, 0.5)
    tile_rows = []
    for value in (along_x * factor / total, along_y * factor / total):
        for half in range(2):
            lane_tile = value[:, half * 128 : half * 128 + 128]
            tile_rows += [lane_tile, pltpu.roll(lane_tile, 64, 1)]
    grid = jnp.concatenate(tile_rows, axis=0)
    lane = lax.broadcasted_iota(jnp.int32, (8, 128), 1)
    for j in range(N_SEC):
        upper = pltpu.roll(grid, (8 - 8 * j) % 128, 1)
        lower = pltpu.roll(grid, (128 - 8 * j) % 128, 1)
        gy = jnp.where(lane < GYW, lane, lane - GYW) + (8 * j - 8)
        window = jnp.where(lane < GYW, upper, lower)
        window = jnp.where((lane < 2 * GYW) & (gy >= 0) & (gy < 32), window, 0.0)
        packed = window[0:4] + pltpu.roll(window, 64, 1)[4:8]
        for b in range(N_XY):
            out_ref[j * N_XY + b] = packed


def flow_windows(own, following, tabs):
    return pl.pallas_call(
        flow_kernel,
        out_shape=jax.ShapeDtypeStruct((N_SEC * N_XY, 4, 128), F32),
        in_specs=[VMEM_SPEC] * 9,
        out_specs=VMEM_SPEC,
        scratch_shapes=[
            pltpu.VMEM((GROUPS, 256, 256), BF16),
            pltpu.VMEM((GROUPS, 256, 256), BF16),
            pltpu.VMEM((GROUPS, 256, 256), F32),
            pltpu.VMEM((TILES // 2, TILES, 16, 128), F32),
            pltpu.VMEM((8, 128), F32),
        ],
        compiler_params=pltpu.CompilerParams(vmem_limit_bytes=24 * MIB),
        cost_estimate=pl.CostEstimate(
            flops=2 * TILES * 256 * 256 * 8 * 256, bytes_accessed=8 << 20, transcendentals=0
        ),
    )(*own, following, *tabs)


def relax_kernel(arrived_ref, out_ref):
    column, block = lax.axis_index("sec"), lax.axis_index("xy")
    lane = lax.broadcasted_iota(jnp.int32, (8, 128), 1)
    lane = jnp.where(lane < 64, lane, lane - 64)
    top = lane < GYW
    gy = jnp.where(top, lane, lane - GYW) + (8 * column - 8)
    inside = (lane < 2 * GYW) & (gy >= 0) & (gy < 32)
    mask = {}
    for o in range(-4, 5):
        valid = (block + o >= 0) & (block + o < N_XY)
        mask[o] = jnp.where(inside & valid, 0.2, 0.0)
    zero = jnp.zeros((8, 128), F32)
    result = []
    for s in range(0, N_SEC, 2):
        flow, mesh = {}, {}
        for o in range(-4, 5):
            at = jnp.clip(block + o, 0, N_XY - 1)
            value = jnp.concatenate(
                [arrived_ref[s * N_XY + at], arrived_ref[(s + 1) * N_XY + at]], axis=0
            )
            flow[o] = value * mask[o]
            mesh[o] = jnp.where(mask[o] > 0.0, value, 0.0)
        def swap(value):
            return jnp.where(top, pltpu.roll(value, 128 - GYW, 1), pltpu.roll(value, GYW, 1))

        other, other_flow = ({o: swap(v) for o, v in part.items()} for part in (mesh, flow))
        for step in range(ITERS):
            reach = (ITERS - step) // 2
            new, new_other = {}, {}
            for o in range(-reach, reach + 1):
                near = other[o] + jnp.where(top, other.get(o - 1, zero), other.get(o + 1, zero))
                sides = pltpu.roll(mesh[o], 1, 1) + pltpu.roll(mesh[o], 127, 1)
                new[o] = flow[o] + mask[o] * (near + sides)
                if step < ITERS - 1:
                    near = mesh[o] + jnp.where(top, mesh.get(o + 1, zero), mesh.get(o - 1, zero))
                    sides = pltpu.roll(other[o], 1, 1) + pltpu.roll(other[o], 127, 1)
                    new_other[o] = other_flow[o] + mask[o] * (near + sides)
            mesh, other = new, new_other
        result.append(mesh[0])
    turned = jnp.concatenate(result + [jnp.zeros((112, 128), F32)], axis=0).T
    for c in range(2):
        for i in range(2):
            at = 64 * c + GYW * i + 8
            out_ref[c, i] = turned[at : at + 8, :15]


def relax(arrived):
    return pl.pallas_call(
        relax_kernel,
        out_shape=jax.ShapeDtypeStruct((2, 2, 8, 15), F32),
        in_specs=[VMEM_SPEC],
        out_specs=pl.BlockSpec(memory_space=pltpu.VMEM),
        compiler_params=pltpu.CompilerParams(vmem_limit_bytes=8 * MIB),
    )(arrived)


def local(raw_pieces, piece_owner, piece_slot, blend):
    tabs = [jnp.asarray(t) for t in tables()]
    outgoing = send_rows(piece_owner[:, :, 0], piece_slot, blend, raw_pieces)
    arrived = lax.all_to_all(outgoing, "xy", split_axis=0, concat_axis=0, tiled=True)
    first = first_section(arrived)
    back = [(i + 1, i) for i in range(N_SEC - 1)]
    following = lax.ppermute(first, "sec", back)
    own = spectrum(arrived, tabs)
    windows = flow_windows(own, following, tabs)
    got = lax.all_to_all(windows, ("sec", "xy"), split_axis=0, concat_axis=0, tiled=True)
    return relax(got).transpose(3, 0, 1, 2)


def solution(mesh):
    in_specs = (P("sec", "xy", None), P("sec", "xy", None), P("sec", "xy"), P("sec", "xy"))
    out_specs = P(None, None, "xy", "sec")
    return jax.shard_map(local, mesh=mesh, in_specs=in_specs, out_specs=out_specs, check_vma=False)
```

```python
import math

import jax
import jax.numpy as jnp
import numpy as np
from jax import lax
from jax.experimental import pallas as pl
from jax.experimental.pallas import tpu as pltpu
from jax.sharding import PartitionSpec as P

PS = 64
FLAT = PS * PS
CAP = 6
N_SEC = 4
N_XY = 32
SEC_DEV = 4
PIECES = 96
BLOCK = 64
ITERS = 8
KEYS = SEC_DEV * 128
CHUNK = SEC_DEV * CAP
LANE_TILES = FLAT // 128
PARTS = CHUNK // 8
TILES_OUT = PARTS * LANE_TILES + 1
PATCHES = SEC_DEV * BLOCK
TILE = 256
TILES = FLAT // TILE
GYW = 24
F32 = jnp.float32
BF16 = jnp.bfloat16
MIB = 1024 * 1024

VMEM_SPEC = pl.BlockSpec(memory_space=pltpu.VMEM)
NT = (((1,), (1,)), ((), ()))
NN = (((1,), (0,)), ((), ()))


def real_basis():
    pos = np.arange(PS)
    rows = np.zeros((2, 32, PS))
    for k in range(32):
        angle = 2.0 * math.pi * ((k * pos) % PS) / PS
        rows[0, k] = np.cos(angle)
        rows[1, k] = np.sin(angle) if k else np.cos(math.pi * pos)
        rows[:, k] *= (math.sqrt(2.0) if k else 1.0) / 8.0
    return rows


def split_table(table):
    high = table.astype(jnp.bfloat16)
    low = (table - high.astype(np.float64)).astype(jnp.bfloat16)
    return np.concatenate([high, low], axis=0)


def tables():
    basis = real_basis()
    by_x = basis.reshape(2, 8, 4, PS)
    by_y = basis.reshape(2, 16, 2, PS)
    two, four = np.eye(2), np.eye(4)
    first = np.einsum("ab,pqky->qpkaby", four, by_y).reshape(256, 256)
    second = np.einsum("pu,kv,cgitb->cgpkituvb", two, two, by_x.reshape(2, 8, 4, 16, 4))
    second = second.reshape(256, 256)
    shift = (np.arange(PS) + 32) % PS - 32
    weigh = np.einsum("pkd,d,rld->pkrl", basis, shift, basis)
    third = np.einsum("pu,kv,cgidhj->cgpkidhuvj", two, two, weigh.reshape(2, 8, 4, 2, 8, 4))
    third = third.reshape(256, 256)
    fourth = np.einsum("ij,pqkurv->qpkiruvj", four, weigh.reshape(2, 16, 2, 2, 16, 2))
    fourth = fourth.reshape(256, 256)
    return [split_table(t) for t in (first, second, third, fourth)]


def mm(a, b, dims=NN):
    return lax.dot_general(a, b, dims, preferred_element_type=F32)


def split(value):
    high = value.astype(BF16)
    return high, (value - high.astype(F32)).astype(BF16)


def mm3(table, high, low):
    both = mm(table, high)
    return both[:256] + both[256:] + mm(table[:256], low)


def lane_rows(scratch, ref):
    scratch[...] = jnp.zeros_like(scratch)
    scratch[0:SEC_DEV, 0:PIECES] = ref[...].astype(F32)
    return scratch[0:SEC_DEV, :]


def column(row):
    return jnp.broadcast_to(row, (128, 128)).T


SEND_LANES = 1024
SENDS = FLAT // SEND_LANES
SEND_TILES = SEND_LANES // 128


def tile_of(part, lane_tile):
    return (lane_tile // SEND_TILES * PARTS + part) * SEND_TILES + lane_tile % SEND_TILES


def send_kernel(
    owner_hbm, slot_hbm, blend_hbm, raw_hbm, out_hbm,
    owner_ref, slot_ref, blend_ref, raw_ref, lanes, select, blend, slots, warped, out_ref,
    sems, raw_sems, out_sems,
):
    small = [
        pltpu.make_async_copy(source, target, sems.at[i])
        for i, (source, target) in enumerate(
            [(owner_hbm, owner_ref), (slot_hbm, slot_ref), (blend_hbm, blend_ref)]
        )
    ]
    for copy in small:
        copy.start()
    large = [
        pltpu.make_async_copy(
            raw_hbm.at[:, :, pl.ds(i * SEND_LANES, SEND_LANES)], raw_ref.at[i], raw_sems.at[i]
        )
        for i in range(SENDS)
    ]
    large[0].start()
    for s in range(SEC_DEV):
        for i in range(SENDS):
            warped[i, 128 * s + PIECES : 128 * s + 128, :] = jnp.zeros((32, SEND_LANES), BF16)
    line = lax.broadcasted_iota(jnp.int32, (128, 128), 0)
    lane = lax.broadcasted_iota(jnp.int32, (128, 128), 1)
    lane_id = lax.broadcasted_iota(jnp.int32, (8 * N_XY, 128), 1)
    rows = lax.broadcasted_iota(jnp.int32, (8 * N_XY, 128), 0)
    rows = (rows // 8) * CHUNK + rows % 8
    for copy in small:
        copy.wait()
    large[1].start()
    owners = lane_rows(lanes, owner_ref)
    slot_rows = lane_rows(lanes, slot_ref)
    blend_rows = lane_rows(lanes, blend_ref)
    for s in range(SEC_DEV):
        owner = owners[s : s + 1]
        same = jnp.where((column(owner) == owner) & (line < lane), 1.0, 0.0)
        rank = jnp.sum(same, axis=0, keepdims=True)
        target = (owner * CHUNK + rank + float(s * CAP)).astype(jnp.int32)
        target = jnp.where(lane[0:1] < PIECES, target, -1)
        for j in range(PARTS):
            if s - j in (0, 1):
                at = slice(128 * (s - j), 128 * (s - j) + 128)
                select[j, :, at] = jnp.where(rows + 8 * j == target, 1.0, 0.0).astype(BF16)
        at = slice(128 * s, 128 * s + 128)
        blend[at, :] = column(blend_rows[s : s + 1])
        slots[at, :] = (column(slot_rows[s : s + 1]) + float(s * BLOCK + 1)).astype(BF16)

    ids = [mm(select[j], slots[128 * j : 128 * j + 256, :]) for j in range(PARTS)]
    ids = jnp.where(lane_id == 0, ids[0], jnp.where(lane_id == 1, ids[1], ids[2]))
    out_ref[:, TILES_OUT - 1] = ids.reshape(N_XY, 8, 128).astype(BF16)
    copies = []

    def leave(first, count):
        at = pl.ds(first, count)
        copies.append(
            pltpu.make_async_copy(out_ref.at[:, at], out_hbm.at[:, at], out_sems.at[len(copies)])
        )
        copies[-1].start()

    for i in range(SENDS):
        large[i].wait()
        if i == 0:
            large[2].start()
            large[3].start()
        for s in range(SEC_DEV):
            at = slice(128 * s, 128 * s + PIECES)
            scale = blend[at, :]
            for lane_at in range(0, SEND_LANES, 128):
                to = slice(lane_at, lane_at + 128)
                warped[i, at, to] = (raw_ref[i, s, :, to].astype(F32) * scale).astype(BF16)
        for j in range(PARTS):
            value = mm(select[j], warped[i, 128 * j : 128 * j + 256, :])
            for tile in range(SEND_TILES):
                piece = value[:, tile * 128 : tile * 128 + 128].reshape(N_XY, 8, 128)
                out_ref[:, tile_of(j, i * SEND_TILES + tile)] = piece.astype(BF16)
            if i == SENDS - 1:
                leave((i * PARTS + j) * SEND_TILES, SEND_TILES + (j == PARTS - 1))
        if i < SENDS - 1:
            leave(i * PARTS * SEND_TILES, PARTS * SEND_TILES)
    for copy in copies:
        copy.wait()


def send_rows(owner, slot, blend, raw):
    hbm = pl.BlockSpec(memory_space=pltpu.HBM)
    return pl.pallas_call(
        send_kernel,
        out_shape=jax.ShapeDtypeStruct((N_XY, TILES_OUT, 8, 128), BF16),
        in_specs=[hbm, hbm, hbm, hbm],
        out_specs=hbm,
        scratch_shapes=[
            pltpu.VMEM((SEC_DEV, PIECES), jnp.int32),
            pltpu.VMEM((SEC_DEV, PIECES), jnp.int32),
            pltpu.VMEM((SEC_DEV, PIECES), F32),
            pltpu.VMEM((SENDS, SEC_DEV, PIECES, SEND_LANES), BF16),
            pltpu.VMEM((8, 128), F32),
            pltpu.VMEM((PARTS, 8 * N_XY, 256), BF16),
            pltpu.VMEM((KEYS, 128), F32),
            pltpu.VMEM((KEYS, 128), BF16),
            pltpu.VMEM((SENDS, KEYS, SEND_LANES), BF16),
            pltpu.VMEM((N_XY, TILES_OUT, 8, 128), BF16),
            pltpu.SemaphoreType.DMA((3,)),
            pltpu.SemaphoreType.DMA((SENDS,)),
            pltpu.SemaphoreType.DMA((SENDS + PARTS - 1,)),
        ],
        compiler_params=pltpu.CompilerParams(vmem_limit_bytes=60 * MIB),
    )(owner, slot, blend, raw)


def places(ids, part, count):
    wanted = lax.broadcasted_iota(jnp.int32, (count, 8 * N_XY), 0).astype(F32)
    match = ids[part : part + 1] == wanted + float(part * BLOCK + 1)
    return jnp.where(match, 1.0, 0.0).astype(BF16)


def row_ids(rows_ref):
    return rows_ref[:, TILES_OUT - 1].astype(F32).reshape(8 * N_XY, 128).T


def row_tiles(rows_ref, part, lane, size):
    first = lane // 128
    return jnp.concatenate(
        [
            rows_ref[:, tile_of(part, first + tile)].reshape(8 * N_XY, 128)
            for tile in range(size // 128)
        ],
        axis=1,
    )


def first_kernel(rows_ref, out_ref, place):
    place[...] = places(row_ids(rows_ref), 0, BLOCK)
    for at in range(0, FLAT, 1024):
        out_ref[:, at : at + 1024] = mm(place[...], row_tiles(rows_ref, 0, at, 1024)).astype(BF16)


def first_section(rows):
    return pl.pallas_call(
        first_kernel,
        out_shape=jax.ShapeDtypeStruct((BLOCK, FLAT), BF16),
        in_specs=[VMEM_SPEC],
        out_specs=VMEM_SPEC,
        scratch_shapes=[pltpu.VMEM((BLOCK, 8 * N_XY), BF16)],
        compiler_params=pltpu.CompilerParams(vmem_limit_bytes=8 * MIB),
        cost_estimate=pl.CostEstimate(flops=1 << 28, bytes_accessed=3 << 20, transcendentals=0),
    )(rows)


GROUP = 4
GROUPS = TILES // GROUP


def sublane_sum(value):
    total = value[0:8]
    for row in range(8, value.shape[0], 8):
        total = total + value[row : row + 8]
    return total


ROOT = math.sqrt(2.0)


def cross_rows(own, other, first_step):
    lanes = own.shape[1]
    a, b = (value.reshape(2, 8, 2, 8, lanes) for value in (own, other))
    shape = (8, 8, lanes)
    line = lax.broadcasted_iota(jnp.int32, shape, 1)
    head = (lax.broadcasted_iota(jnp.int32, shape, 0) == 0) & ((line == 0) | (line == 4))
    pair = line < 4
    if first_step < lanes:
        pair = pair & (lax.broadcasted_iota(jnp.int32, shape, 2) < first_step)

    def along_y(p, r):
        b_cosine, b_sine = b[r, :, 0], b[r, :, 1]
        if first_step:
            mixed, b_sine = b_sine, jnp.where(pair, 0.0, b_sine)
            turned = jnp.where(pair, -mixed, b_cosine)
        else:
            turned = b_cosine
        return (
            a[p, :, 0] * b_cosine + a[p, :, 1] * b_sine,
            a[p, :, 0] * b_sine - a[p, :, 1] * turned,
        )

    cc, cs, sc, ss = along_y(0, 0), along_y(0, 1), along_y(1, 0), along_y(1, 1)
    parts = {}
    for y in range(2):
        parts[0, y] = jnp.where(head, ROOT * cc[y], cc[y] + ss[y])
        parts[1, y] = jnp.where(head, ROOT * ss[y], cs[y] - sc[y])
        if first_step:
            for x in range(2):
                parts[x, y] = jnp.where(pair, ROOT * parts[x, y], parts[x, y])
    rows = jnp.stack([jnp.stack([parts[x, y] for y in range(2)], axis=1) for x in range(2)])
    return rows.reshape(256, lanes)


def down(value):
    return jnp.sum(value, axis=0, keepdims=True)


def weighed(table_ref, high):
    both = mm(table_ref[...], high)
    return both[:256] + both[256:]


def flow_sums(operands, third_ref, fourth_ref, high_ref, twice_ref, sums_ref):
    lanes = 128
    total = jnp.zeros((8, 4 * lanes), F32)
    along_x = jnp.zeros((8, 4 * lanes), F32)
    along_y = jnp.zeros((8, 4 * lanes), F32)
    for q in range(0, TILES, 4):
        rows = jnp.concatenate(
            [cross_rows(*operands(q + i), 0 if q + i else lanes) for i in range(4)], axis=1
        )
        high = rows.astype(BF16)
        twice = 2.0 * rows - high.astype(F32)
        total = total + sublane_sum(rows * rows)
        along_x = along_x + sublane_sum(twice * weighed(third_ref, high))
        for i in range(4):
            high_ref[q + i] = high[:, i * lanes : (i + 1) * lanes]
            twice_ref[q + i] = twice[:, i * lanes : (i + 1) * lanes]
    for g in range(0, TILES, 4):
        high, twice = (
            jnp.concatenate(
                [ref[:, 16 * (g + i) : 16 * (g + i) + 16, :].reshape(256, lanes) for i in range(4)],
                axis=1,
            )
            for ref in (high_ref, twice_ref)
        )
        along_y = along_y + sublane_sum(twice * weighed(fourth_ref, high))
    for i, value in enumerate((total, along_x, along_y)):
        value = value[:, : 2 * lanes] + value[:, 2 * lanes :]
        sums_ref[i : i + 1, :] = down(value[:, :lanes] + value[:, lanes:])


def turn(value):
    return pltpu.roll(value, BLOCK, 1)


def flow_sums_packed(operands, third_ref, fourth_ref, turned_ref, sums_ref):
    total = jnp.zeros((8, 256), F32)
    along_x = jnp.zeros((8, 256), F32)
    along_y = jnp.zeros((8, 256), F32)
    left = lax.broadcasted_iota(jnp.int32, (8, 16, 128), 2) < BLOCK
    for p in range(0, TILES // 2, 2):
        pieces = [cross_rows(*operands(p + i), 0 if p + i else BLOCK) for i in range(2)]
        for i, piece in enumerate(pieces):
            straight = piece.reshape(8, 2, 16, 128)
            turned = turn(piece).reshape(8, 2, 16, 128)
            turned_ref[:, 2 * (p + i)] = jnp.where(left, straight[:, 0], turned[:, 1])
            turned_ref[:, 2 * (p + i) + 1] = jnp.where(left, turned[:, 0], straight[:, 1])
        rows = jnp.concatenate(pieces, axis=1)
        high = rows.astype(BF16)
        total = total + sublane_sum(rows * rows)
        twice = 2.0 * rows - high.astype(F32)
        along_x = along_x + sublane_sum(twice * weighed(third_ref, high))
    for g in range(0, TILES // 2, 2):
        rows = jnp.concatenate([turned_ref[g + i].reshape(256, 128) for i in range(2)], axis=1)
        high = rows.astype(BF16)
        twice = 2.0 * rows - high.astype(F32)
        along_y = along_y + sublane_sum(twice * weighed(fourth_ref, high))
    for i, value in enumerate((total, along_x, along_y)):
        value = down(value[:, :128] + value[:, 128:])
        sums_ref[i : i + 1, :] = value + turn(value)


def spectrum_kernel(
    rows_ref, first_ref, second_ref, third_ref, fourth_ref, last_ref, square_ref, sums_ref, third_sums_ref,
    place, high, low, own_first, own_second, high_part, twice_part, turned,
):
    ids = row_ids(rows_ref)
    for j in range(PARTS):
        place[j] = places(ids, j, 2 * BLOCK)
    wide = 8 * TILE
    for at in range(0, FLAT, wide):
        pieces, before = [], None
        for j in range(PARTS):
            value = mm(place[j], row_tiles(rows_ref, j, at, wide))
            pieces.append(value[:BLOCK] if before is None else before + value[:BLOCK])
            before = value[BLOCK:]
        patches = jnp.concatenate(pieces + [before], axis=0).astype(BF16)
        for i in range(wide // TILE):
            both = mm(first_ref[...], patches[:, i * TILE : (i + 1) * TILE], NT)
            t = at // TILE + i
            high[t], low[t] = split(both[:256] + both[256:])

    square = jnp.zeros((8, PATCHES), F32)
    for q in range(TILES):
        if q % 2 == 0:
            pairs = [
                jnp.concatenate(
                    [ref[:, 16 * i : 16 * i + 16, :].reshape(256, PATCHES) for i in (q, q + 1)],
                    axis=1,
                )
                for ref in (high, low)
            ]
            both_q = mm3(second_ref[...], *pairs)
        own = both_q[:, (q % 2) * PATCHES : (q % 2 + 1) * PATCHES]
        if q == 0:
            own = jnp.where(lax.broadcasted_iota(jnp.int32, (256, 1), 0) == 0, 0.0, own)
        square = square + sublane_sum(own * own)
        own_first[q] = own[:, :128]
        own_second[q] = own[:, 128:]
    square_ref[...] = square
    left = lax.broadcasted_iota(jnp.int32, (256, 128), 1) < BLOCK

    def operands(q):
        own = own_first[q]
        return own, jnp.where(left, turn(own), turn(own_second[q]))

    def packed_operands(p):
        even, odd = own_second[2 * p], own_second[2 * p + 1]
        last = jnp.where(left, turn(even), odd)
        last_ref[p] = last
        return jnp.where(left, even, turn(odd)), last

    flow_sums(operands, third_ref, fourth_ref, high_part, twice_part, sums_ref)
    flow_sums_packed(packed_operands, third_ref, fourth_ref, turned, third_sums_ref)


def spectrum(rows, tabs):
    return pl.pallas_call(
        spectrum_kernel,
        out_shape=[
            jax.ShapeDtypeStruct((TILES // 2, 256, 128), F32),
            jax.ShapeDtypeStruct((8, PATCHES), F32),
            jax.ShapeDtypeStruct((8, 128), F32),
            jax.ShapeDtypeStruct((8, 128), F32),
        ],
        in_specs=[VMEM_SPEC] * 5,
        out_specs=[VMEM_SPEC] * 4,
        scratch_shapes=[
            pltpu.VMEM((PARTS, 2 * BLOCK, 8 * N_XY), BF16),
            pltpu.VMEM((TILES, 256, PATCHES), BF16),
            pltpu.VMEM((TILES, 256, PATCHES), BF16),
            pltpu.VMEM((TILES, 256, 128), F32),
            pltpu.VMEM((TILES, 256, 128), F32),
            pltpu.VMEM((TILES, 256, 128), BF16),
            pltpu.VMEM((TILES, 256, 128), F32),
            pltpu.VMEM((TILES // 2, TILES, 16, 128), F32),
        ],
        compiler_params=pltpu.CompilerParams(vmem_limit_bytes=24 * MIB),
        cost_estimate=pl.CostEstimate(
            flops=2 * TILES * 256 * 256 * 11 * 256, bytes_accessed=12 << 20, transcendentals=0
        ),
    )(rows, *tabs)


def next_spectrum(next_ref, first_ref, second_ref, high, low, follow):
    left = lax.broadcasted_iota(jnp.int32, (16, 128), 1) < BLOCK
    for tg in range(GROUPS):
        rows = jnp.concatenate(
            [
                next_ref[:, (GROUP * tg + i) * TILE : (GROUP * tg + i + 1) * TILE]
                for i in range(GROUP)
            ],
            axis=0,
        )
        both = mm(first_ref[...], rows, NT)
        value = both[:256] + both[256:]
        for half in range(2):
            lanes = value[:, half * 128 : half * 128 + 128]
            rolled = pltpu.roll(lanes, BLOCK, 1)
            for pair in range(TILES // 2):
                g, to = pair // 2, (pair % 2) * 128
                even = slice(32 * pair, 32 * pair + 16)
                odd = slice(32 * pair + 16, 32 * pair + 32)
                for i in range(2):
                    t = GROUP * tg + 2 * half + i
                    if i == 0:
                        packed = jnp.where(left, lanes[even], rolled[odd])
                    else:
                        packed = jnp.where(left, rolled[even], lanes[odd])
                    at = slice(16 * t, 16 * t + 16)
                    up, down = split(packed)
                    high[g, at, to : to + 128] = up
                    low[g, at, to : to + 128] = down
    for g in range(GROUPS):
        follow[g] = mm3(second_ref[...], high[g], low[g])
    follow[0, 0:1, 0:BLOCK] = jnp.zeros((1, BLOCK), F32)


def flow_kernel(
    last_ref, square_ref, early_ref, third_sums_ref, next_ref,
    first_ref, second_ref, third_ref, fourth_ref, out_ref,
    next_high, next_low, follow, turned, late,
):
    next_spectrum(next_ref, first_ref, second_ref, next_high, next_low, follow)

    def operands(p):
        return last_ref[p], follow[p // 2, :, (p % 2) * 128 : (p % 2) * 128 + 128]

    flow_sums_packed(operands, third_ref, fourth_ref, turned, late)
    after = jnp.zeros((8, 256), F32)
    for g in range(GROUPS):
        after = after + sublane_sum(follow[g] * follow[g])
    after = after[:, :128] + after[:, 128:]
    after = after + pltpu.roll(after, BLOCK, 1)
    own = square_ref[...]
    low_roll, high_roll = (pltpu.roll(own[:, i : i + 128], BLOCK, 1) for i in (0, 128))
    left = lax.broadcasted_iota(jnp.int32, (8, 128), 1) < BLOCK
    other = jnp.concatenate(
        [jnp.where(left, low_roll, high_roll), jnp.where(left, high_roll, after)], axis=1
    )
    later = jnp.where(left, third_sums_ref[...], late[...])
    total, along_x, along_y = (
        jnp.concatenate([early_ref[i : i + 1, :], later[i : i + 1, :]], axis=1) for i in range(3)
    )
    norm = (down(own) * (1.0 / FLAT) + 1e-05) * (down(other) * (1.0 / FLAT) + 1e-05)
    factor = (1024.0 / (float(FLAT) * float(FLAT))) / norm
    total = jnp.maximum(total * factor, 0.5)
    tile_rows = []
    for value in (along_x * factor / total, along_y * factor / total):
        for half in range(2):
            lane_tile = value[:, half * 128 : half * 128 + 128]
            tile_rows += [lane_tile, pltpu.roll(lane_tile, 64, 1)]
    grid = jnp.concatenate(tile_rows, axis=0)
    lane = lax.broadcasted_iota(jnp.int32, (8, 128), 1)
    for j in range(N_SEC):
        upper = pltpu.roll(grid, (8 - 8 * j) % 128, 1)
        lower = pltpu.roll(grid, (128 - 8 * j) % 128, 1)
        gy = jnp.where(lane < GYW, lane, lane - GYW) + (8 * j - 8)
        window = jnp.where(lane < GYW, upper, lower)
        window = jnp.where((lane < 2 * GYW) & (gy >= 0) & (gy < 32), window, 0.0)
        packed = window[0:4] + pltpu.roll(window, 64, 1)[4:8]
        for b in range(N_XY):
            out_ref[j * N_XY + b] = packed


def flow_windows(own, following, tabs):
    return pl.pallas_call(
        flow_kernel,
        out_shape=jax.ShapeDtypeStruct((N_SEC * N_XY, 4, 128), F32),
        in_specs=[VMEM_SPEC] * 9,
        out_specs=VMEM_SPEC,
        scratch_shapes=[
            pltpu.VMEM((GROUPS, 256, 256), BF16),
            pltpu.VMEM((GROUPS, 256, 256), BF16),
            pltpu.VMEM((GROUPS, 256, 256), F32),
            pltpu.VMEM((TILES // 2, TILES, 16, 128), F32),
            pltpu.VMEM((8, 128), F32),
        ],
        compiler_params=pltpu.CompilerParams(vmem_limit_bytes=24 * MIB),
        cost_estimate=pl.CostEstimate(
            flops=2 * TILES * 256 * 256 * 8 * 256, bytes_accessed=8 << 20, transcendentals=0
        ),
    )(*own, following, *tabs)


def relax_kernel(arrived_ref, out_ref):
    column, block = lax.axis_index("sec"), lax.axis_index("xy")
    lane = lax.broadcasted_iota(jnp.int32, (8, 128), 1)
    lane = jnp.where(lane < 64, lane, lane - 64)
    top = lane < GYW
    gy = jnp.where(top, lane, lane - GYW) + (8 * column - 8)
    inside = (lane < 2 * GYW) & (gy >= 0) & (gy < 32)
    mask = {}
    for o in range(-4, 5):
        valid = (block + o >= 0) & (block + o < N_XY)
        mask[o] = jnp.where(inside & valid, 0.2, 0.0)
    zero = jnp.zeros((8, 128), F32)
    result = []
    for s in range(0, N_SEC, 2):
        flow, mesh = {}, {}
        for o in range(-4, 5):
            at = jnp.clip(block + o, 0, N_XY - 1)
            value = jnp.concatenate(
                [arrived_ref[s * N_XY + at], arrived_ref[(s + 1) * N_XY + at]], axis=0
            )
            flow[o] = value * mask[o]
            mesh[o] = jnp.where(mask[o] > 0.0, value, 0.0)
        def swap(value):
            return jnp.where(top, pltpu.roll(value, 128 - GYW, 1), pltpu.roll(value, GYW, 1))

        other, other_flow = ({o: swap(v) for o, v in part.items()} for part in (mesh, flow))
        for step in range(ITERS):
            reach = (ITERS - step) // 2
            new, new_other = {}, {}
            for o in range(-reach, reach + 1):
                near = other[o] + jnp.where(top, other.get(o - 1, zero), other.get(o + 1, zero))
                sides = pltpu.roll(mesh[o], 1, 1) + pltpu.roll(mesh[o], 127, 1)
                new[o] = flow[o] + mask[o] * (near + sides)
                if step < ITERS - 1:
                    near = mesh[o] + jnp.where(top, mesh.get(o + 1, zero), mesh.get(o - 1, zero))
                    sides = pltpu.roll(other[o], 1, 1) + pltpu.roll(other[o], 127, 1)
                    new_other[o] = other_flow[o] + mask[o] * (near + sides)
            mesh, other = new, new_other
        result.append(mesh[0])
    turned = jnp.concatenate(result + [jnp.zeros((112, 128), F32)], axis=0).T
    for c in range(2):
        for i in range(2):
            at = 64 * c + GYW * i + 8
            out_ref[c, i] = turned[at : at + 8, :15]


def relax(arrived):
    return pl.pallas_call(
        relax_kernel,
        out_shape=jax.ShapeDtypeStruct((2, 2, 8, 15), F32),
        in_specs=[VMEM_SPEC],
        out_specs=pl.BlockSpec(memory_space=pltpu.VMEM),
        compiler_params=pltpu.CompilerParams(vmem_limit_bytes=8 * MIB),
    )(arrived)


def local(raw_pieces, piece_owner, piece_slot, blend):
    tabs = [jnp.asarray(t) for t in tables()]
    outgoing = send_rows(piece_owner[:, :, 0], piece_slot, blend, raw_pieces)
    arrived = lax.all_to_all(outgoing, "xy", split_axis=0, concat_axis=0, tiled=True)
    first = first_section(arrived)
    back = [(i + 1, i) for i in range(N_SEC - 1)]
    following = lax.ppermute(first, "sec", back)
    own = spectrum(arrived, tabs)
    windows = flow_windows(own, following, tabs)
    got = lax.all_to_all(windows, ("sec", "xy"), split_axis=0, concat_axis=0, tiled=True)
    return relax(got).transpose(3, 0, 1, 2)


def solution(mesh):
    in_specs = (P("sec", "xy", None), P("sec", "xy", None), P("sec", "xy"), P("sec", "xy"))
    out_specs = P(None, None, "xy", "sec")
    return jax.shard_map(local, mesh=mesh, in_specs=in_specs, out_specs=out_specs, check_vma=False)
```
